128 devices in a mesh: section: 2 (over core), dp: 64 (over x, y, z).
Axes of the slice: x: 4, y: 4, z: 4, core: 2. Of those that a mesh axis runs over, the one named last changes fastest.
Arguments:
- latents_in: bfloat16 [3, 64, 64, 1024], P(None, 'dp'), may hold values from -6 to 6
- media: bfloat16 [3, 64, 512, 1024], P(None, 'dp'), may hold values from -6 to 6
- frame_count: int32 [3, 64], P(None, 'dp'), may hold values from 1 to 8, as said below
- gains: float32 [2, 3, 1024], P('section'), may hold values from 0.25 to 1.75
- biases: float32 [2, 3, 1024], P('section'), may hold values from -2 to 2
- w_query: bfloat16 [2, 1024, 512], P('section'), may hold values from -0.1875 to 0.1875
- w_keyval: bfloat16 [2, 1024, 1024], P('section'), may hold values from -0.1875 to 0.1875
- w_out: bfloat16 [2, 512, 1024], P('section'), may hold values from -4 to 4
- w_up: bfloat16 [2, 1024, 4096], P('section'), may hold values from -0.1875 to 0.1875
- w_down: bfloat16 [2, 4096, 1024], P('section'), may hold values from -0.09375 to 0.09375
- cotangent: bfloat16 [3, 64, 64, 1024], P(None, 'dp'), may hold values from -6 to 6
Outputs:
- resampled: float32 [3, 64, 64, 1024], P(None, 'dp', None, 'section')
- latents_grad: float32 [3, 64, 64, 1024], P(None, 'dp', None, 'section')
- media_grad: float32 [3, 64, 512, 1024], P(None, 'dp', None, 'section')
- gains_grad: float32 [2, 3, 1024], P('section', None, 'dp')
- biases_grad: float32 [2, 3, 1024], P('section', None, 'dp')
- w_query_grad: float32 [2, 1024, 512], P('section', 'dp')
- w_keyval_grad: float32 [2, 1024, 1024], P('section', 'dp')
- w_out_grad: float32 [2, 512, 1024], P('section', 'dp')
- w_up_grad: float32 [2, 1024, 4096], P('section', 'dp')
- w_down_grad: float32 [2, 4096, 1024], P('section', 'dp')
The draws below stay inside these ranges and needn't reach their ends.
Inputs may be any that keep to these rules, and one draw needn't show every extreme that they name: The first frame_count frame slots of a video, 64 patches each, are real and the rest are padding.
All inputs are finite; a program needn't handle non-finite values.
Results may differ from the reference program's by a relative error of at most 0.015.
Values sent between devices are 32-bit elements; how exact they have to be, the bound alone decides.
A program may use at most 320 MiB of HBM per device.

```python
import jax
import jax.numpy as jnp
from jax import lax

D = 1024
HEADS = 8
HEAD_DIM = 64
LATENTS = 64
FF = 4096
FRAMES = 8
PATCHES = 64
MICRO = 3
INNER = 512
SLOTS = 512
VIDEOS = 64


def draw_frame_count(key, part):
    key = jax.random.fold_in(key, 7)
    key_counts, key_place = jax.random.split(key, 2)
    counts = jax.random.randint(key_counts, (MICRO * VIDEOS,), 1, FRAMES + 1)
    position = jax.random.randint(key_place, (), 0, MICRO * VIDEOS)
    counts = counts.at[position].set(FRAMES)
    counts = counts.at[(position + 1) % (MICRO * VIDEOS)].set(1)
    return counts.reshape(MICRO, VIDEOS).astype(jnp.int32)


def level_of(stream_key, shape, shards, smallest, largest):
    gain, own = 1.0, jax.random.fold_in(stream_key, 6)
    for dim, parts in shards:
        heights = jnp.exp(jax.random.uniform(jax.random.fold_in(own, dim), (parts,), jnp.float32, smallest / len(shards), largest / len(shards)))
        gain = gain * jnp.repeat(heights, shape[dim] // parts).reshape([-1 if axis == dim else 1 for axis in range(len(shape))])
    return gain


def scatter_about(own_key, extent, scale, reach, cuts=(), held_as=jnp.bfloat16):
    entries = scale * jax.random.normal(own_key, extent, jnp.float32)
    if cuts:
        entries = entries * level_of(own_key, extent, cuts, -0.22, 0.18)
    return jnp.clip(entries, -reach, reach).astype(held_as)


def setup_inputs(seed: int = 0) -> dict:
    seeds = jax.random.split(jax.random.key(seed), 12)
    latents_in = scatter_about(seeds[0], (MICRO, VIDEOS, LATENTS, D), 1.0, 6.0, ((1, 64),))
    media = scatter_about(seeds[1], (MICRO, VIDEOS, SLOTS, D), 1.0, 6.0, ((1, 64),))
    frame_count = draw_frame_count(jax.random.fold_in(seeds[11], 71), 0)
    gains = jnp.clip(1.0 + 0.15 * jax.random.normal(seeds[3], (2, 3, D), jnp.float32), 0.25, 1.75)
    biases = scatter_about(seeds[4], (2, 3, D), 0.3, 2.0, ((0, 2),), jnp.float32)
    w_query = scatter_about(seeds[5], (2, D, INNER), D ** -0.5, 0.1875, ((0, 2),))
    w_keyval = scatter_about(seeds[6], (2, D, 2 * INNER), D ** -0.5, 0.1875, ((0, 2),))
    w_out = scatter_about(seeds[7], (2, INNER, D), (max(1, 2 * INNER // SLOTS)) ** -0.5, 4.0, ((0, 2),))
    w_up = scatter_about(seeds[8], (2, D, FF), D ** -0.5, 0.1875, ((0, 2),))
    w_down = scatter_about(seeds[9], (2, FF, D), FF ** -0.5, 0.09375, ((0, 2),))
    cotangent = scatter_about(seeds[10], (MICRO, VIDEOS, LATENTS, D), 1.0, 6.0, ((1, 64),))
    return {"latents_in": latents_in, "media": media, "frame_count": frame_count, "gains": gains, "biases": biases, "w_query": w_query, "w_keyval": w_keyval, "w_out": w_out, "w_up": w_up, "w_down": w_down, "cotangent": cotangent}


NORM_EPS = 1e-05
MASK_FILL = -1e+30

@jax.custom_vjp
def low(v):
    return lax.optimization_barrier(v.astype(jnp.bfloat16)).astype(jnp.float32)

@jax.custom_vjp
def low_back(v):
    return v

def low_keep(v):
    return (low(v), None)

def low_pass(kept, grad):
    return (grad,)

def back_keep(v):
    return (v, None)

def back_low(kept, grad):
    return (low(grad),)
low.defvjp(low_keep, low_pass)
low_back.defvjp(back_keep, back_low)

def matmul_high(left, right):
    return jnp.dot(left, right, precision=lax.Precision.HIGHEST, preferred_element_type=jnp.float32)

def layer_norm(values_in, gain_row, bias_row):
    average = lax.optimization_barrier(jnp.mean(values_in, -1, keepdims=True))
    centred = values_in - average
    variance = lax.optimization_barrier(jnp.mean(centred * centred, -1, keepdims=True))
    return centred * lax.rsqrt(variance + NORM_EPS) * gain_row + bias_row

def resample_layer(latents, media_rows, key_valid, layer_params):
    gain_rows, bias_rows, w_query, w_keyval, w_out, w_up, w_down = layer_params
    score_scale = HEAD_DIM ** (-0.5)
    media_in = low(layer_norm(media_rows, gain_rows[0], bias_rows[0]))
    latent_in = low(layer_norm(latents, gain_rows[1], bias_rows[1]))
    queries = low(low_back(matmul_high(latent_in, w_query) * score_scale))
    keyvals = low(low_back(jnp.concatenate([matmul_high(media_in, w_keyval), matmul_high(latent_in, w_keyval)], 0)))
    key_total = keyvals.shape[0]
    query_heads = queries.reshape(LATENTS, HEADS, HEAD_DIM)
    key_heads = keyvals[:, :INNER].reshape(key_total, HEADS, HEAD_DIM)
    value_heads = keyvals[:, INNER:].reshape(key_total, HEADS, HEAD_DIM)
    scores = low_back(jnp.einsum('lhe,khe->hlk', query_heads, key_heads, precision=lax.Precision.HIGHEST))
    scores = jnp.where(key_valid, scores, MASK_FILL)
    attention = jax.nn.softmax(scores, axis=-1)
    attended = jnp.einsum('hlk,khe->lhe', low(attention), value_heads, precision=lax.Precision.HIGHEST)
    attended = low(low_back(attended.reshape(LATENTS, INNER)))
    mixed = latents + low_back(matmul_high(attended, w_out))
    ff_in = low(layer_norm(mixed, gain_rows[2], bias_rows[2]))
    activated = low(jax.nn.gelu(low_back(matmul_high(ff_in, w_up)), approximate=False))
    return mixed + low_back(matmul_high(activated, w_down))

def resample_video(params, latents, media_rows, frames_real):
    key_valid = jnp.concatenate([jnp.arange(SLOTS) // PATCHES < frames_real, jnp.ones((LATENTS,), dtype=bool)])
    for layer_number in range(2):
        latents = resample_layer(latents, media_rows, key_valid, tuple((stacked[layer_number] for stacked in params)))
    return latents

def reference(latents_in, media, frame_count, gains, biases, w_query, w_keyval, w_out, w_up, w_down, cotangent):
    params = (gains.astype(jnp.float32), biases.astype(jnp.float32), w_query.astype(jnp.float32), w_keyval.astype(jnp.float32), w_out.astype(jnp.float32), w_up.astype(jnp.float32), w_down.astype(jnp.float32))
    video_total = MICRO * VIDEOS
    latents = latents_in.astype(jnp.float32).reshape(video_total, LATENTS, D)
    media_rows = media.astype(jnp.float32).reshape(video_total, SLOTS, D)
    frames_real = frame_count.reshape(video_total).astype(jnp.int32)
    checked = jax.checkpoint(resample_video)

    def all_videos(params_in, latents_all, media_all):

        def one_video(carry, item):
            return (carry, checked(params_in, item[0], item[1], item[2]))
        unused, outputs = lax.scan(one_video, jnp.zeros((), jnp.float32), (latents_all, media_all, frames_real))
        return outputs
    resampled, pullback = jax.vjp(all_videos, params, latents, media_rows)
    param_grads, latent_grads, media_grads = pullback(cotangent.astype(jnp.float32).reshape(video_total, LATENTS, D))
    return (resampled.reshape(MICRO, VIDEOS, LATENTS, D), latent_grads.reshape(MICRO, VIDEOS, LATENTS, D), media_grads.reshape(MICRO, VIDEOS, SLOTS, D), param_grads[0], param_grads[1], param_grads[2], param_grads[3], param_grads[4], param_grads[5], param_grads[6])
```

```python
import jax
import jax.numpy as jnp
from jax import lax
from jax.experimental import pallas as pl
from jax.experimental.pallas import tpu as pltpu
from jax.sharding import PartitionSpec as P

HEADS = 8
PATCHES = 64


NORM_EPS = 1e-05
MASK_FILL = -1e30
ROOT_HALF = 0.7071067811865476
INV_ROOT_TAU = 0.3989422804014327


def passed_along(block, axis, distance):
    devices = range(lax.axis_size(axis))
    route = [((i - distance) % len(devices), i) for i in devices]
    return lax.ppermute(block, axis, route)


def matmul(left, right):
    return jnp.dot(left, right, preferred_element_type=jnp.float32)


def cross_rows(left, right):
    return lax.dot_general(
        left, right, (((0,), (0,)), ((), ())), preferred_element_type=jnp.float32
    )


def against_rows(left, right):
    return lax.dot_general(
        left, right, (((1,), (1,)), ((), ())), preferred_element_type=jnp.float32
    )


def norm_parts(values_in, gain_row, bias_row):
    average = jnp.mean(values_in, -1, keepdims=True)
    centred = values_in - average
    inverse = lax.rsqrt(jnp.mean(centred * centred, -1, keepdims=True) + NORM_EPS)
    normed = centred * inverse
    return (normed * gain_row + bias_row, normed, inverse)


def norm_back(grad_rows, normed, inverse, gain_row):
    scaled = grad_rows * gain_row
    inner_mean = jnp.mean(scaled, -1, keepdims=True)
    along_mean = jnp.mean(scaled * normed, -1, keepdims=True)
    grad_in = inverse * (scaled - inner_mean - normed * along_mean)
    return (grad_in, jnp.sum(grad_rows * normed, 0), jnp.sum(grad_rows, 0))


def gelu_slope(pre_act):
    return (
        0.5 * (1.0 + lax.erf(pre_act * ROOT_HALF))
        + pre_act * jnp.exp(-0.5 * pre_act * pre_act) * INV_ROOT_TAU
    )


def layer_forward(layer_input, media_rows, key_valid, norm_gains, norm_biases, weights, head_count):
    w_query, w_keyval, w_out, w_up, w_down = weights
    inner_width = w_query.shape[1]
    head_width = inner_width // head_count
    score_scale = head_width ** (-0.5)
    latent_rows = layer_input.shape[0]
    media_full, media_normed, media_inverse = norm_parts(
        media_rows.astype(jnp.float32), norm_gains[0], norm_biases[0]
    )
    media_in = media_full.astype(jnp.bfloat16)
    latent_full, latent_normed, latent_inverse = norm_parts(
        layer_input, norm_gains[1], norm_biases[1]
    )
    latent_in = latent_full.astype(jnp.bfloat16)
    queries = (matmul(latent_in, w_query) * score_scale).astype(jnp.bfloat16)
    keyvals = jnp.concatenate([matmul(media_in, w_keyval), matmul(latent_in, w_keyval)], 0).astype(
        jnp.bfloat16
    )
    key_count = keyvals.shape[0]
    query_heads = queries.reshape(latent_rows, head_count, head_width)
    key_heads = keyvals[:, :inner_width].reshape(key_count, head_count, head_width)
    value_heads = keyvals[:, inner_width:].reshape(key_count, head_count, head_width)
    scores = jnp.einsum("lhe,khe->hlk", query_heads, key_heads, preferred_element_type=jnp.float32)
    scores = jnp.where(key_valid, scores, MASK_FILL)
    attention = jnp.exp(scores - jnp.max(scores, -1, keepdims=True))
    attention = attention / jnp.sum(attention, -1, keepdims=True)
    attention_low = attention.astype(jnp.bfloat16)
    attended = jnp.einsum(
        "hlk,khe->lhe", attention_low, value_heads, preferred_element_type=jnp.float32
    )
    attended = attended.reshape(latent_rows, inner_width).astype(jnp.bfloat16)
    mixed = layer_input + matmul(attended, w_out)
    ff_full, ff_normed, ff_inverse = norm_parts(mixed, norm_gains[2], norm_biases[2])
    ff_in = ff_full.astype(jnp.bfloat16)
    pre_act = matmul(ff_in, w_up)
    activated = jax.nn.gelu(pre_act, approximate=False).astype(jnp.bfloat16)
    layer_out = mixed + matmul(activated, w_down)
    kept_state = (
        media_in,
        media_normed,
        media_inverse,
        latent_in,
        latent_normed,
        latent_inverse,
        query_heads,
        key_heads,
        value_heads,
        attention,
        attention_low,
        attended,
        ff_in,
        ff_normed,
        ff_inverse,
        pre_act,
        activated,
    )
    return (layer_out, kept_state)


def layer_backward(grad_y, kept_state, norm_gains, weights, head_count):
    (
        media_in,
        media_normed,
        media_inverse,
        latent_in,
        latent_normed,
        latent_inverse,
        query_heads,
        key_heads,
        value_heads,
        attention,
        attention_low,
        attended,
        ff_in,
        ff_normed,
        ff_inverse,
        pre_act,
        activated,
    ) = kept_state
    w_query, w_keyval, w_out, w_up, w_down = weights
    inner_width = w_query.shape[1]
    head_width = inner_width // head_count
    score_scale = head_width ** (-0.5)
    latent_rows = grad_y.shape[0]
    key_count = key_heads.shape[0]
    slot_count = media_in.shape[0]
    grad_out = grad_y.astype(jnp.bfloat16)
    grad_pre = (against_rows(grad_out, w_down) * gelu_slope(pre_act)).astype(jnp.bfloat16)
    grad_ffn, ff_gain_term, ff_bias_term = norm_back(
        against_rows(grad_pre, w_up), ff_normed, ff_inverse, norm_gains[2]
    )
    grad_mixed = grad_y + grad_ffn
    grad_attn = grad_mixed.astype(jnp.bfloat16)
    grad_att = (
        against_rows(grad_attn, w_out)
        .astype(jnp.bfloat16)
        .reshape(latent_rows, head_count, head_width)
    )
    grad_probs = jnp.einsum(
        "lhe,khe->hlk", grad_att, value_heads, preferred_element_type=jnp.float32
    )
    grad_scores = attention * (grad_probs - jnp.sum(attention * grad_probs, -1, keepdims=True))
    grad_scores = grad_scores.astype(jnp.bfloat16)
    grad_queries = jnp.einsum(
        "hlk,khe->lhe", grad_scores, key_heads, preferred_element_type=jnp.float32
    )
    grad_queries = grad_queries.astype(jnp.bfloat16).reshape(latent_rows, inner_width)
    grad_keys = jnp.einsum(
        "hlk,lhe->khe", grad_scores, query_heads, preferred_element_type=jnp.float32
    )
    grad_values = jnp.einsum(
        "hlk,lhe->khe", attention_low, grad_att, preferred_element_type=jnp.float32
    )
    grad_keyvals = jnp.concatenate(
        [grad_keys.reshape(key_count, inner_width), grad_values.reshape(key_count, inner_width)], 1
    ).astype(jnp.bfloat16)
    grad_media_kv = grad_keyvals[:slot_count]
    grad_latent_kv = grad_keyvals[slot_count:]
    grad_media_in = against_rows(grad_media_kv, w_keyval)
    grad_latent_in = against_rows(grad_queries, w_query) * score_scale + against_rows(
        grad_latent_kv, w_keyval
    )
    grad_media, media_gain_term, media_bias_term = norm_back(
        grad_media_in, media_normed, media_inverse, norm_gains[0]
    )
    grad_latent, latent_gain_term, latent_bias_term = norm_back(
        grad_latent_in, latent_normed, latent_inverse, norm_gains[1]
    )
    grad_input = grad_mixed + grad_latent
    gain_terms = jnp.stack([media_gain_term, latent_gain_term, ff_gain_term])
    bias_terms = jnp.stack([media_bias_term, latent_bias_term, ff_bias_term])
    return (
        grad_input,
        grad_media,
        (ff_in, activated, attended, media_in, latent_in, grad_out, grad_pre, grad_attn, grad_queries, grad_keyvals, gain_terms, bias_terms),
    )


MESH = pl.DeviceIdType.MESH
CHUNKS = 41
GROUPS = 14
TICKS = GROUPS + 6
ROWS = (256, 64, 16)
COLS = 256


def chunk_plan(c):
    left = jnp.where(c < 16, c // 4, jnp.where(c < 32, 4, jnp.where(c < 34, 5, jnp.where(c < 35, 7, jnp.where(c < 37, 14, 8)))))
    right = jnp.where(c < 16, c % 4, jnp.where(c < 32, c - 12, jnp.where(c < 34, 20 + 2 * (c - 32), jnp.where(c < 35, 24, jnp.where(c < 37, c - 10, 27 + 7 * (c - 37))))))
    steps = jnp.where(c < 32, 1, jnp.where(c < 34, 2, jnp.where(c < 37, 1, 7)))
    return left, right, steps


def shard_kernel(left_ref, right_ref, out_ref, own1, own2, own3, a1, a2, a3, b1, b2, b3, send_sem, recv_sem):
    me = lax.axis_index("dp")
    coords = (me // 16, (me // 4) % 4, me % 4)
    strides = (16, 4, 1)

    def at(axis, shift):
        return (coords[axis] + shift) % 4

    def neighbour(axis, shift):
        return me + (at(axis, shift) - coords[axis]) * strides[axis]

    barrier = pltpu.get_barrier_semaphore()
    for axis in range(3):
        for shift in (1, 3):
            pl.semaphore_signal(barrier, inc=1, device_id={"dp": neighbour(axis, shift)}, device_id_type=MESH)
    pl.semaphore_wait(barrier, 6)

    own = (own1, own2, own3)
    got_a = (a1, a2, a3)
    got_b = (b1, b2, b3)

    def copy(order, stage, step, way, group, tick):
        axis = (order + stage) % 3
        half = ROWS[stage] // 2
        place = own[stage].at[order, group % 3]
        turn = tick % 2
        sem = (((order * 3 + stage) * 2 + step) * 2 + way) * 2 + turn
        shift = 1 if way == 0 else 3
        if step == 0:
            source = place.at[at(axis, 2), pl.ds(way * half, half)]
            target = got_a[stage].at[order, way, turn]
        else:
            source = place.at[at(axis, shift)]
            target = got_b[stage].at[order, way, turn]
        return pltpu.make_async_remote_copy(
            src_ref=source,
            dst_ref=target,
            send_sem=send_sem.at[sem],
            recv_sem=recv_sem.at[sem],
            device_id={"dp": neighbour(axis, shift)},
            device_id_type=MESH,
        )

    def terms(order, group):
        chunk = 3 * group + order
        left, right, steps = chunk_plan(chunk)
        slot = group % 3

        def place(step, first):
            for i in range(4):
                block = jnp.dot(
                    left_ref[left + step, pl.ds(256 * i, 256), :], right_ref[right + step], preferred_element_type=jnp.float32
                )
                for j in range(4):
                    for k in range(4):
                        spot = ((i, j, k), (j, k, i), (k, i, j))[order]
                        rows = pl.ds((spot[1] * 4 + spot[2]) * 16, 16)
                        part = block[(j * 4 + k) * 16 : (j * 4 + k) * 16 + 16]
                        if first:
                            own1[order, slot, spot[0], rows, :] = part
                        else:
                            own1[order, slot, spot[0], rows, :] += part

        place(0, True)

        def more(step, carry):
            place(step, False)
            return carry

        lax.fori_loop(1, steps, more, 0)

    def valid(order, group):
        return (group >= 0) & (group * 3 + order < CHUNKS)

    def tick(t, carry):
        for order in range(3):

            @pl.when(valid(order, t))
            def _():
                terms(order, t)

        for stage in range(3):
            for order in range(3):
                axis = (order + stage) % 3
                half = ROWS[stage] // 2
                turn = (t - 1) % 2
                group_a = t - 1 - 2 * stage

                @pl.when(valid(order, group_a))
                def _():
                    for way in range(2):
                        done = copy(order, stage, 0, way, group_a, t - 1)
                        done.wait()
                        spot = at(axis, 1 if way == 0 else 3)
                        own[stage][order, group_a % 3, spot, pl.ds(way * half, half), :] += got_a[stage][order, way, turn]

                group_b = t - 2 - 2 * stage

                @pl.when(valid(order, group_b))
                def _():
                    for way in range(2):
                        done = copy(order, stage, 1, way, group_b, t - 1)
                        done.wait()
                    total = (
                        own[stage][order, group_b % 3, at(axis, 0)]
                        + got_b[stage][order, 0, turn]
                        + got_b[stage][order, 1, turn]
                    )
                    if stage < 2:
                        own[stage + 1][order, group_b % 3] = total.reshape(4, ROWS[stage + 1], COLS)
                    else:
                        out_ref[group_b * 3 + order] = total

        for stage in range(3):
            for order in range(3):
                group_a = t - 2 * stage
                group_b = t - 1 - 2 * stage

                @pl.when(valid(order, group_a))
                def _():
                    for way in range(2):
                        copy(order, stage, 0, way, group_a, t).start()

                @pl.when(valid(order, group_b))
                def _():
                    for way in range(2):
                        copy(order, stage, 1, way, group_b, t).start()

        return carry

    lax.fori_loop(0, TICKS, tick, 0)


def scattered_terms(left, right):
    vmem = pl.BlockSpec(memory_space=pltpu.VMEM)
    f32 = jnp.float32
    return pl.pallas_call(
        shard_kernel,
        out_shape=jax.ShapeDtypeStruct((CHUNKS, 16, COLS), f32),
        in_specs=[vmem, vmem],
        out_specs=vmem,
        scratch_shapes=[pltpu.VMEM((3, 3, 4, r, COLS), f32) for r in ROWS]
        + [pltpu.VMEM((3, 2, 2, r // 2, COLS), f32) for r in ROWS]
        + [pltpu.VMEM((3, 2, 2, r, COLS), f32) for r in ROWS]
        + [pltpu.SemaphoreType.DMA((72,)), pltpu.SemaphoreType.DMA((72,))],
        compiler_params=pltpu.CompilerParams(collective_id=1, has_side_effects=True, vmem_limit_bytes=50 * 2**20),
        name="scatter_terms",
    )(left, right)


def rows_deep(block):
    rows = block.shape[0]
    full = -(-rows // 256) * 256
    return jnp.pad(block, ((0, full - rows), (0, 0))).reshape(full // 256, 256, block.shape[1])


def column_blocks(block):
    deep = rows_deep(block)[0]
    return deep.reshape(256, -1, 256).transpose(1, 0, 2)


def flat_rows(block):
    return block.reshape(-1, block.shape[-1])


def body(
    latents_in, media, frame_count, gains, biases, w_query, w_keyval, w_out, w_up, w_down, cotangent
):
    section_index = lax.axis_index("section")
    micro_count = media.shape[0]
    slot_count = media.shape[2]
    half_width = media.shape[3] // 2
    latent_rows = latents_in.shape[2]
    norm_gains = gains[0]
    norm_biases = biases[0]
    weights = (w_query[0], w_keyval[0], w_out[0], w_up[0], w_down[0])
    frame_of_slot = jnp.arange(slot_count) // PATCHES
    key_valid = jnp.concatenate(
        [frame_of_slot[None] < frame_count, jnp.ones((micro_count, latent_rows), dtype=bool)], 1
    )

    def forward(x):
        return jax.vmap(
            lambda a, b, c: layer_forward(a, b, c, norm_gains, norm_biases, weights, HEADS)
        )(x, media[:, 0], key_valid)

    given = latents_in[:, 0].astype(jnp.float32)
    first, unused_state = forward(given)
    x = jnp.where(section_index == 0, given, passed_along(first, "section", 1))
    y, state = forward(x)
    complete = jnp.where(section_index == 1, y, passed_along(y, "section", 1))
    resampled = lax.dynamic_slice_in_dim(complete, section_index * half_width, half_width, 2)

    def backward(g):
        return jax.vmap(lambda a, b: layer_backward(a, b, norm_gains, weights, HEADS))(g, state)

    given_grad = cotangent[:, 0].astype(jnp.float32)
    first_grad = backward(given_grad)[0]
    grad_y = jnp.where(section_index == 1, given_grad, passed_along(first_grad, "section", 1))
    grad_x, grad_media, terms = backward(grad_y)
    complete = jnp.where(section_index == 0, grad_x, passed_along(grad_x, "section", 1))
    latents_grad = lax.dynamic_slice_in_dim(complete, section_index * half_width, half_width, 2)
    ff_in, activated, attended, media_in, latent_in, grad_out, grad_pre, grad_attn, grad_queries, grad_keyvals = [
        flat_rows(t) for t in terms[:10]
    ]
    grad_media_kv = flat_rows(terms[9][:, :slot_count])
    grad_latent_kv = flat_rows(terms[9][:, slot_count:])
    gain_terms, bias_terms = jnp.sum(terms[10], 0), jnp.sum(terms[11], 0)

    def deep_left(block):
        return rows_deep(block).transpose(0, 2, 1)

    low_columns = jnp.concatenate([gain_terms, bias_terms], 0)
    high = low_columns.astype(jnp.bfloat16)
    low = (low_columns - high.astype(jnp.float32)).astype(jnp.bfloat16)
    act_left = deep_left(activated)[0].reshape(64, 4, 16, 256).transpose(1, 0, 2, 3).reshape(4, 1024, 256)
    att_left = deep_left(attended)[0].reshape(64, 8, 256)
    none = jnp.zeros_like(att_left)
    left = jnp.concatenate(
        [
            act_left,
            deep_left(ff_in),
            jnp.concatenate([att_left, none], 1).reshape(1, 1024, 256),
            jnp.concatenate([none, att_left], 1).reshape(1, 1024, 256),
            deep_left(jnp.concatenate([high, low], 0)),
            deep_left(media_in),
            deep_left(latent_in),
        ],
        0,
    )
    eye = (jnp.arange(256)[:, None] % 6 == jnp.arange(256)[None, :]) & (jnp.arange(256)[:, None] < 12)
    right = jnp.concatenate(
        [
            column_blocks(grad_out),
            column_blocks(grad_pre),
            column_blocks(grad_attn),
            eye.astype(jnp.bfloat16)[None],
            column_blocks(grad_queries),
            jnp.concatenate([rows_deep(grad_media_kv), rows_deep(grad_latent_kv)], 0)
            .reshape(7, 256, 4, 256)
            .transpose(2, 0, 1, 3)
            .reshape(28, 256, 256),
        ],
        0,
    )
    got = scattered_terms(left, right)
    media_grad = lax.psum_scatter(grad_media, "section", scatter_dimension=2, tiled=True)
    small = got[34, :, :6].T
    return (
        resampled[:, None],
        latents_grad[:, None],
        media_grad[:, None],
        small[None, :3],
        small[None, 3:],
        got[35:37].transpose(1, 0, 2).reshape(1, 16, 512) * 0.125,
        got[37:41].transpose(1, 0, 2).reshape(1, 16, 1024),
        got[32:34].reshape(2, 2, 8, 256).transpose(2, 0, 1, 3).reshape(1, 8, 1024),
        got[16:32].transpose(1, 0, 2).reshape(1, 16, 4096),
        got[0:16].reshape(4, 4, 16, 256).transpose(0, 2, 1, 3).reshape(1, 64, 1024),
    )


def solution(mesh):
    placed = (
        P(None, "dp", None, None),
        P(None, "dp", None, None),
        P(None, "dp"),
        P("section", None, None),
        P("section", None, None),
        P("section", None, None),
        P("section", None, None),
        P("section", None, None),
        P("section", None, None),
        P("section", None, None),
        P(None, "dp", None, None),
    )
    return jax.shard_map(
        body,
        mesh=mesh,
        in_specs=placed,
        out_specs=(
            P(None, "dp", None, "section"),
            P(None, "dp", None, "section"),
            P(None, "dp", None, "section"),
            P("section", None, "dp"),
            P("section", None, "dp"),
            P("section", "dp", None),
            P("section", "dp", None),
            P("section", "dp", None),
            P("section", "dp", None),
            P("section", "dp", None),
        ),
        check_vma=False,
    )
```

```python
import jax
import jax.numpy as jnp
from jax import lax
from jax.experimental import pallas as pl
from jax.experimental.pallas import tpu as pltpu
from jax.sharding import PartitionSpec as P

MESH = pl.DeviceIdType.MESH
F32 = jnp.float32
BF16 = jnp.bfloat16
NORM_EPS = 1e-05
MASK_FILL = -1e30
ROOT_HALF = 0.7071067811865476
INV_ROOT_TAU = 0.3989422804014327
ROWS_ALL = 192
KEYS = 640
FF_STEPS = 8


def mm(left, right):
    return jnp.dot(left, right, preferred_element_type=F32)


def mm_nt(left, right):
    return lax.dot_general(left, right, (((1,), (1,)), ((), ())), preferred_element_type=F32)


def mm_tn(left, right):
    return lax.dot_general(left, right, (((0,), (0,)), ((), ())), preferred_element_type=F32)


def normed_rows(values):
    average = jnp.mean(values, -1, keepdims=True)
    centred = values - average
    inverse = lax.rsqrt(jnp.mean(centred * centred, -1, keepdims=True) + NORM_EPS)
    return centred * inverse, inverse


def norm_back(grad, normed, inverse, gain):
    scaled = grad * gain
    inner = jnp.mean(scaled, -1, keepdims=True)
    along = jnp.mean(scaled * normed, -1, keepdims=True)
    back = inverse * (scaled - inner - normed * along)
    return back, jnp.sum(grad * normed, 0, keepdims=True), jnp.sum(grad, 0, keepdims=True)


def turned(block):
    rows = block.shape[0]
    if rows < 256:
        block = jnp.concatenate([block, jnp.zeros((256 - rows, block.shape[1]), block.dtype)], 0)
    return block.T.astype(BF16)


def head_stack(block):
    lane = lax.broadcasted_iota(jnp.int32, (64, 256), 1) // 64
    return jnp.concatenate([jnp.where(lane == h, block, jnp.zeros_like(block)) for h in range(4)], 0)


def head_merge(block):
    lane = lax.broadcasted_iota(jnp.int32, (64, 256), 1) // 64
    return sum(jnp.where(lane == h, block[64 * h : 64 * h + 64], 0.0) for h in range(4))


def layers_kernel(
    latents, media, mask, gains, biases, w_query, w_keyval, w_out, w_up, w_down, cotangent,
    resampled, latents_grad, media_grad, left, right,
    xs, x1s, gys, n1s, n2s, inv, accs, lin, ffin, qs, kv, probs, att, gatt, pres, sums, stage, got, sent,
    wu, wd, w_sem, x_sem, g_sem, r_sem, l_sem, m_send, m_recv,
):
    section = lax.axis_index("section")
    other = 1 - section
    barrier = pltpu.get_barrier_semaphore()
    pl.semaphore_signal(barrier, inc=1, device_id={"section": other}, device_id_type=MESH)
    pl.semaphore_wait(barrier, 1)

    def to_other(source, target, sem):
        return pltpu.make_async_remote_copy(
            src_ref=source, dst_ref=target, send_sem=sem.at[0], recv_sem=sem.at[1],
            device_id={"section": other}, device_id_type=MESH,
        )

    def weights(step):
        slot = step % 2
        at = pl.ds(pl.multiple_of(step * 512, 512), 512)
        return (
            pltpu.make_async_copy(w_up.at[:, at], wu.at[slot], w_sem.at[0, slot]),
            pltpu.make_async_copy(w_down.at[at, :], wd.at[slot], w_sem.at[1, slot]),
        )

    def fetch(step):
        for c in weights(step):
            c.start()

    def fetched(step):
        for c in weights(step):
            c.wait()

    fetch(0)
    def media_block(i, carry):
        rows = pl.ds(pl.multiple_of(i * 256, 256), 256)
        normed, _ = normed_rows(media[rows, :].astype(F32))
        media_in = (normed * gains[0:1, :] + biases[0:1, :]).astype(BF16)
        left[8 + i] = turned(media_in.astype(F32))
        at = pl.ds(pl.multiple_of((i % 2) * 256, 256), 256)
        kv[i // 2, at, :] = mm(media_in, w_keyval[...]).astype(BF16)
        return carry

    lax.fori_loop(0, 6, media_block, 0)
    for v in range(3):
        kv[v, pl.ds(576, 64), :] = jnp.zeros((64, 1024), BF16)
    for k in range(55):
        if k != 24 and not (k >= 27 and (k - 27) % 7 != 6):
            right[k, pl.ds(192, 64), :] = jnp.zeros((64, 256), BF16)
    row = lax.broadcasted_iota(jnp.int32, (256, 256), 0)
    col = lax.broadcasted_iota(jnp.int32, (256, 256), 1)
    right[24] = jnp.where(((row == col) & (row < 6)) | ((row == col + 6) & (row >= 6) & (row < 12)), 1.0, 0.0).astype(BF16)

    @pl.when(section == 0)
    def _():
        xs[...] = latents[...].astype(F32)

    @pl.when(section == 1)
    def _():
        to_other(accs, xs, x_sem).wait_recv()

    normed, inverse = normed_rows(xs[...])
    n1s[...] = normed
    inv[0] = jnp.broadcast_to(inverse, (ROWS_ALL, 128))
    latent_in = (normed * gains[1:2, :] + biases[1:2, :]).astype(BF16)
    lin[...] = latent_in
    left[14] = turned(latent_in.astype(F32))
    qs[...] = (mm(lin[...], w_query[...]) * 0.125).astype(BF16)
    latent_kv = mm(lin[...], w_keyval[...]).astype(BF16)
    for v in range(3):
        kv[v, pl.ds(512, 64), :] = latent_kv[64 * v : 64 * v + 64]

    def attend(v, carry):
        rows = pl.ds(pl.multiple_of(v * 64, 64), 64)
        for g in range(2):
            cols = pl.ds(256 * g, 256)
            stacked = head_stack(qs[rows, cols])
            scores = mm_nt(stacked, kv[v, :, cols])
            scores = jnp.where(mask[v] > 0.0, scores, MASK_FILL)
            raised = jnp.exp(scores - jnp.max(scores, -1, keepdims=True))
            p = raised * (1.0 / jnp.sum(raised, -1, keepdims=True))
            probs[v, g] = p
            mixed = mm(p.astype(BF16), kv[v, :, pl.ds(512 + 256 * g, 256)])
            att[rows, cols] = head_merge(mixed).astype(BF16)
        return carry

    lax.fori_loop(0, 3, attend, 0)

    x1 = xs[...] + mm(att[...], w_out[...])
    x1s[...] = x1
    normed, inverse = normed_rows(x1)
    n2s[...] = normed
    inv[1] = jnp.broadcast_to(inverse, (ROWS_ALL, 128))
    ffin[...] = (normed * gains[2:3, :] + biases[2:3, :]).astype(BF16)
    left[4] = turned(ffin[...].astype(F32))
    att_rows = att[...].astype(F32)
    att_t = jnp.concatenate([att_rows, jnp.zeros((64, 512), F32)], 0).T.reshape(64, 8, 256)
    none = jnp.zeros_like(att_t)
    left[5] = jnp.concatenate([att_t, none], 1).reshape(1024, 256).astype(BF16)
    left[6] = jnp.concatenate([none, att_t], 1).reshape(1024, 256).astype(BF16)

    accs[...] = x1s[...]

    def ff_forward(j, carry):
        fetched(j)

        @pl.when(j + 1 < FF_STEPS)
        def _():
            fetch(j + 1)

        pre = mm(ffin[...], wu[j % 2])
        pres[j] = pre
        act = (pre * (0.5 * (1.0 + lax.erf(pre * ROOT_HALF)))).astype(BF16)
        act_t = turned(act.astype(F32)).reshape(8, 4, 16, 256)
        at = pl.ds(pl.multiple_of(j * 128, 128), 128)
        for i in range(4):
            left[i, at, :] = act_t[:, i].reshape(128, 256)
        accs[...] += mm(act, wd[j % 2])
        return carry

    lax.fori_loop(0, FF_STEPS, ff_forward, 0)
    fetch(0)

    @pl.when(section == 0)
    def _():
        to_other(accs, xs, x_sem).start()
        to_other(sent, resampled, r_sem).wait_recv()
        to_other(accs, xs, x_sem).wait_send()
        to_other(accs, gys, g_sem).wait_recv()

    @pl.when(section == 1)
    def _():
        sent[...] = accs[:, pl.ds(0, 512)]
        to_other(sent, resampled, r_sem).start()
        resampled[...] = accs[:, pl.ds(512, 512)]
        gys[...] = cotangent[...].astype(F32)
        to_other(sent, resampled, r_sem).wait_send()

    grad_out = gys[...].astype(BF16)
    for k in range(4):
        right[k, pl.ds(0, 192), :] = grad_out[:, 256 * k : 256 * k + 256]
    ffin[...] = grad_out
    accs[...] = jnp.zeros((ROWS_ALL, 1024), F32)

    def ff_backward(j, carry):
        fetched(j)

        @pl.when(j + 1 < FF_STEPS)
        def _():
            fetch(j + 1)

        grad_act = mm_nt(ffin[...], wd[j % 2])
        pre = pres[j]
        slope = 0.5 * (1.0 + lax.erf(pre * ROOT_HALF)) + pre * jnp.exp(-0.5 * pre * pre) * INV_ROOT_TAU
        grad_pre = (grad_act * slope).astype(BF16)
        right[4 + 2 * j, pl.ds(0, 192), :] = grad_pre[:, :256]
        right[5 + 2 * j, pl.ds(0, 192), :] = grad_pre[:, 256:]
        accs[...] += mm_nt(grad_pre, wu[j % 2])
        return carry

    lax.fori_loop(0, FF_STEPS, ff_backward, 0)

    back, gain_sum, bias_sum = norm_back(accs[...], n2s[...], inv[1][:, :1], gains[2:3, :])
    sums[pl.ds(2, 1), :] = gain_sum
    sums[pl.ds(5, 1), :] = bias_sum
    grad_x1 = gys[...] + back
    gys[...] = grad_x1
    grad_attn = grad_x1.astype(BF16)
    for k in range(4):
        right[20 + k, pl.ds(0, 192), :] = grad_attn[:, 256 * k : 256 * k + 256]
    gatt[...] = mm_nt(grad_attn, w_out[...]).astype(BF16)

    def attend_back(v, carry):
        rows = pl.ds(pl.multiple_of(v * 64, 64), 64)
        for g in range(2):
            cols = pl.ds(256 * g, 256)
            q_stack = head_stack(qs[rows, cols])
            g_stack = head_stack(gatt[rows, cols])
            p = probs[v, g]
            grad_p = mm_nt(g_stack, kv[v, :, pl.ds(512 + 256 * g, 256)])
            weighted = p * grad_p
            grad_s = (weighted - p * jnp.sum(weighted, -1, keepdims=True)).astype(BF16)
            right[25 + g, rows, :] = head_merge(mm(grad_s, kv[v, :, cols])).astype(BF16)
            for base, value in (
                (27 + 7 * g, mm_tn(grad_s, q_stack)),
                (41 + 7 * g, mm_tn(p.astype(BF16), g_stack)),
            ):
                value = value.astype(BF16)
                right[base + 2 * v] = value[:256]
                right[base + 2 * v + 1] = value[256:512]
                right[base + 6, rows, :] = value[512:576]
        return carry

    lax.fori_loop(0, 3, attend_back, 0)

    grad_in = mm_nt(right[25, pl.ds(0, 192), :], w_query[:, pl.ds(0, 256)]) + mm_nt(
        right[26, pl.ds(0, 192), :], w_query[:, pl.ds(256, 256)]
    )
    grad_in = grad_in * 0.125
    for k in range(4):
        grad_in += mm_nt(right[33 + 7 * k, pl.ds(0, 192), :], w_keyval[:, pl.ds(256 * k, 256)])
    back, gain_sum, bias_sum = norm_back(grad_in, n1s[...], inv[0][:, :1], gains[1:2, :])
    sums[pl.ds(1, 1), :] = gain_sum
    sums[pl.ds(4, 1), :] = bias_sum
    accs[...] = gys[...] + back

    @pl.when(section == 1)
    def _():
        to_other(accs, gys, g_sem).start()
        to_other(accs, gys, g_sem).wait_send()

    @pl.when(section == 0)
    def _():
        sent[...] = accs[:, pl.ds(512, 512)]
        to_other(sent, latents_grad, l_sem).start()
        latents_grad[...] = accs[:, pl.ds(0, 512)]
        to_other(sent, latents_grad, l_sem).wait_send()

    def media_copy(i):
        return pltpu.make_async_remote_copy(
            src_ref=stage.at[i, other], dst_ref=got.at[i], send_sem=m_send.at[i], recv_sem=m_recv.at[i],
            device_id={"section": other}, device_id_type=MESH,
        )

    sums[pl.ds(0, 1), :] = jnp.zeros((1, 1024), F32)
    sums[pl.ds(3, 1), :] = jnp.zeros((1, 1024), F32)

    def media_back(i, carry):
        rows = pl.ds(pl.multiple_of(i * 256, 256), 256)
        normed, inverse = normed_rows(media[rows, :].astype(F32))
        grad_media = jnp.zeros((256, 1024), F32)
        for k in range(4):
            grad_media += mm_nt(right[27 + 7 * k + i], w_keyval[:, pl.ds(256 * k, 256)])
        back, gain_sum, bias_sum = norm_back(grad_media, normed, inverse, gains[0:1, :])
        sums[pl.ds(0, 1), :] += gain_sum
        sums[pl.ds(3, 1), :] += bias_sum
        stage[i, 0] = back[:, :512]
        stage[i, 1] = back[:, 512:]
        media_copy(i).start()
        return carry

    lax.fori_loop(0, 6, media_back, 0)

    total = sums[pl.ds(0, 6), :]
    high = total.astype(BF16).astype(F32)
    left[7] = turned(jnp.concatenate([high, total - high, jnp.zeros((244, 1024), F32)], 0))

    def media_sum(i, carry):
        media_copy(i).wait()
        rows = pl.ds(pl.multiple_of(i * 256, 256), 256)
        media_grad[rows, :] = stage[i, section] + got[i]
        return carry

    lax.fori_loop(0, 6, media_sum, 0)

    @pl.when(section == 1)
    def _():
        to_other(sent, latents_grad, l_sem).wait_recv()


def run_layers(latents, media, mask, gains, biases, w_query, w_keyval, w_out, w_up, w_down, cotangent):
    vmem = pl.BlockSpec(memory_space=pltpu.VMEM)
    hbm = pl.BlockSpec(memory_space=pl.ANY)
    sds = jax.ShapeDtypeStruct
    return pl.pallas_call(
        layers_kernel,
        out_shape=[
            sds((192, 512), F32), sds((192, 512), F32), sds((1536, 512), F32), sds((15, 1024, 256), BF16), sds((55, 256, 256), BF16),
        ],
        in_specs=[vmem] * 8 + [hbm, hbm, vmem],
        out_specs=[vmem] * 5,
        scratch_shapes=[
            pltpu.VMEM((192, 1024), F32),
            pltpu.VMEM((192, 1024), F32),
            pltpu.VMEM((192, 1024), F32),
            pltpu.VMEM((192, 1024), F32),
            pltpu.VMEM((192, 1024), F32),
            pltpu.VMEM((2, 192, 128), F32),
            pltpu.VMEM((192, 1024), F32),
            pltpu.VMEM((192, 1024), BF16),
            pltpu.VMEM((192, 1024), BF16),
            pltpu.VMEM((192, 512), BF16),
            pltpu.VMEM((3, KEYS, 1024), BF16),
            pltpu.VMEM((3, 2, 256, KEYS), F32),
            pltpu.VMEM((192, 512), BF16),
            pltpu.VMEM((192, 512), BF16),
            pltpu.VMEM((FF_STEPS, 192, 512), F32),
            pltpu.VMEM((8, 1024), F32),
            pltpu.VMEM((6, 2, 256, 512), F32),
            pltpu.VMEM((6, 256, 512), F32),
            pltpu.VMEM((192, 512), F32),
            pltpu.VMEM((2, 1024, 512), BF16),
            pltpu.VMEM((2, 512, 1024), BF16),
            pltpu.SemaphoreType.DMA((2, 2)),
            pltpu.SemaphoreType.DMA((2,)),
            pltpu.SemaphoreType.DMA((2,)),
            pltpu.SemaphoreType.DMA((2,)),
            pltpu.SemaphoreType.DMA((2,)),
            pltpu.SemaphoreType.DMA((6,)),
            pltpu.SemaphoreType.DMA((6,)),
        ],
        compiler_params=pltpu.CompilerParams(collective_id=2, has_side_effects=True, vmem_limit_bytes=60 * 2**20),
        name="layers",
    )(latents, media, mask, gains, biases, w_query, w_keyval, w_out, w_up, w_down, cotangent)


CHUNKS = 41
GROUPS = 14
TICKS = GROUPS + 6
ROWS = (256, 64, 16)
COLS = 256


def chunk_plan(c):
    left = jnp.where(c < 16, c // 4, jnp.where(c < 32, 4, jnp.where(c < 34, 5, jnp.where(c < 35, 7, jnp.where(c < 37, 14, 8)))))
    right = jnp.where(c < 16, c % 4, jnp.where(c < 32, c - 12, jnp.where(c < 34, 20 + 2 * (c - 32), jnp.where(c < 35, 24, jnp.where(c < 37, c - 10, 27 + 7 * (c - 37))))))
    steps = jnp.where(c < 32, 1, jnp.where(c < 34, 2, jnp.where(c < 37, 1, 7)))
    return left, right, steps


def shard_kernel(left_ref, right_ref, out_ref, own1, own2, own3, a1, a2, a3, b1, b2, b3, send_sem, recv_sem):
    me = lax.axis_index("dp")
    coords = (me // 16, (me // 4) % 4, me % 4)
    strides = (16, 4, 1)

    def at(axis, shift):
        return (coords[axis] + shift) % 4

    def neighbour(axis, shift):
        return me + (at(axis, shift) - coords[axis]) * strides[axis]

    barrier = pltpu.get_barrier_semaphore()
    for axis in range(3):
        for shift in (1, 3):
            pl.semaphore_signal(barrier, inc=1, device_id={"dp": neighbour(axis, shift)}, device_id_type=MESH)
    pl.semaphore_wait(barrier, 6)

    own = (own1, own2, own3)
    got_a = (a1, a2, a3)
    got_b = (b1, b2, b3)

    def copy(order, stage, step, way, group, tick):
        axis = (order + stage) % 3
        half = ROWS[stage] // 2
        place = own[stage].at[order, group % 3]
        turn = tick % 2
        sem = (((order * 3 + stage) * 2 + step) * 2 + way) * 2 + turn
        shift = 1 if way == 0 else 3
        if step == 0:
            source = place.at[at(axis, 2), pl.ds(way * half, half)]
            target = got_a[stage].at[order, way, turn]
        else:
            source = place.at[at(axis, shift)]
            target = got_b[stage].at[order, way, turn]
        return pltpu.make_async_remote_copy(
            src_ref=source,
            dst_ref=target,
            send_sem=send_sem.at[sem],
            recv_sem=recv_sem.at[sem],
            device_id={"dp": neighbour(axis, shift)},
            device_id_type=MESH,
        )

    def terms(order, group):
        chunk = 3 * group + order
        left, right, steps = chunk_plan(chunk)
        slot = group % 3

        def place(step, first):
            for i in range(4):
                block = jnp.dot(
                    left_ref[left + step, pl.ds(256 * i, 256), :], right_ref[right + step], preferred_element_type=jnp.float32
                )
                for j in range(4):
                    for k in range(4):
                        spot = ((i, j, k), (j, k, i), (k, i, j))[order]
                        rows = pl.ds((spot[1] * 4 + spot[2]) * 16, 16)
                        part = block[(j * 4 + k) * 16 : (j * 4 + k) * 16 + 16]
                        if first:
                            own1[order, slot, spot[0], rows, :] = part
                        else:
                            own1[order, slot, spot[0], rows, :] += part

        place(0, True)

        def more(step, carry):
            place(step, False)
            return carry

        lax.fori_loop(1, steps, more, 0)

    def valid(order, group):
        return (group >= 0) & (group * 3 + order < CHUNKS)

    def tick(t, carry):
        for order in range(3):

            @pl.when(valid(order, t))
            def _():
                terms(order, t)

        for stage in range(3):
            for order in range(3):
                axis = (order + stage) % 3
                half = ROWS[stage] // 2
                turn = (t - 1) % 2
                group_a = t - 1 - 2 * stage

                @pl.when(valid(order, group_a))
                def _():
                    for way in range(2):
                        done = copy(order, stage, 0, way, group_a, t - 1)
                        done.wait()
                        spot = at(axis, 1 if way == 0 else 3)
                        own[stage][order, group_a % 3, spot, pl.ds(way * half, half), :] += got_a[stage][order, way, turn]

                group_b = t - 2 - 2 * stage

                @pl.when(valid(order, group_b))
                def _():
                    for way in range(2):
                        done = copy(order, stage, 1, way, group_b, t - 1)
                        done.wait()
                    total = (
                        own[stage][order, group_b % 3, at(axis, 0)]
                        + got_b[stage][order, 0, turn]
                        + got_b[stage][order, 1, turn]
                    )
                    if stage < 2:
                        own[stage + 1][order, group_b % 3] = total.reshape(4, ROWS[stage + 1], COLS)
                    else:
                        out_ref[group_b * 3 + order] = total

        for stage in range(3):
            for order in range(3):
                group_a = t - 2 * stage
                group_b = t - 1 - 2 * stage

                @pl.when(valid(order, group_a))
                def _():
                    for way in range(2):
                        copy(order, stage, 0, way, group_a, t).start()

                @pl.when(valid(order, group_b))
                def _():
                    for way in range(2):
                        copy(order, stage, 1, way, group_b, t).start()

        return carry

    lax.fori_loop(0, TICKS, tick, 0)


def scattered_terms(left, right):
    vmem = pl.BlockSpec(memory_space=pltpu.VMEM)
    f32 = jnp.float32
    return pl.pallas_call(
        shard_kernel,
        out_shape=jax.ShapeDtypeStruct((CHUNKS, 16, COLS), f32),
        in_specs=[vmem, vmem],
        out_specs=vmem,
        scratch_shapes=[pltpu.VMEM((3, 3, 4, r, COLS), f32) for r in ROWS]
        + [pltpu.VMEM((3, 2, 2, r // 2, COLS), f32) for r in ROWS]
        + [pltpu.VMEM((3, 2, 2, r, COLS), f32) for r in ROWS]
        + [pltpu.SemaphoreType.DMA((72,)), pltpu.SemaphoreType.DMA((72,))],
        compiler_params=pltpu.CompilerParams(collective_id=1, has_side_effects=True, vmem_limit_bytes=50 * 2**20),
        name="scatter_terms",
    )(left, right)


def body(
    latents_in, media, frame_count, gains, biases, w_query, w_keyval, w_out, w_up, w_down, cotangent
):
    key = jnp.arange(KEYS)
    valid = (key[None] < 64 * frame_count) | ((key[None] >= 512) & (key[None] < 576))
    mask = valid.astype(F32)[:, None, :]
    resampled, latents_grad, media_grad, left, right = run_layers(
        latents_in.reshape(192, 1024), media.reshape(1536, 1024), mask, gains[0], biases[0],
        w_query[0], w_keyval[0], w_out[0], w_up[0], w_down[0], cotangent.reshape(192, 1024),
    )
    got = scattered_terms(left, right)
    small = got[34, :, :6].T
    return (
        resampled.reshape(3, 1, 64, 512),
        latents_grad.reshape(3, 1, 64, 512),
        media_grad.reshape(3, 1, 512, 512),
        small[None, :3],
        small[None, 3:],
        got[35:37].transpose(1, 0, 2).reshape(1, 16, 512) * 0.125,
        got[37:41].transpose(1, 0, 2).reshape(1, 16, 1024),
        got[32:34].reshape(2, 2, 8, 256).transpose(2, 0, 1, 3).reshape(1, 8, 1024),
        got[16:32].transpose(1, 0, 2).reshape(1, 16, 4096),
        got[0:16].reshape(4, 4, 16, 256).transpose(0, 2, 1, 3).reshape(1, 64, 1024),
    )


def solution(mesh):
    placed = (
        P(None, "dp", None, None),
        P(None, "dp", None, None),
        P(None, "dp"),
        P("section", None, None),
        P("section", None, None),
        P("section", None, None),
        P("section", None, None),
        P("section", None, None),
        P("section", None, None),
        P("section", None, None),
        P(None, "dp", None, None),
    )
    return jax.shard_map(
        body,
        mesh=mesh,
        in_specs=placed,
        out_specs=(
            P(None, "dp", None, "section"),
            P(None, "dp", None, "section"),
            P(None, "dp", None, "section"),
            P("section", None, "dp"),
            P("section", None, "dp"),
            P("section", "dp", None),
            P("section", "dp", None),
            P("section", "dp", None),
            P("section", "dp", None),
            P("section", "dp", None),
        ),
        check_vma=False,
    )
```

```python
import jax
import jax.numpy as jnp
from jax import lax
from jax.experimental import pallas as pl
from jax.experimental.pallas import tpu as pltpu
from jax.sharding import PartitionSpec as P

VMEM_BYTES = 63 * 2**20
MESH = pl.DeviceIdType.MESH
F32 = jnp.float32
BF16 = jnp.bfloat16
NORM_EPS = 1e-05
MASK_FILL = -1e30
ROOT_HALF = 0.7071067811865476
INV_ROOT_TAU = 0.3989422804014327
ROWS_ALL = 192
KEYS = 640
FF_STEPS = 8
RING_ROWS = (256, 64, 16)
COLS = 256
X, Y, Z = 0, 1, 2
FF_IN, ACT, G_OUT, G_PRE = 0, 1, 2, 3
L_LATENT, L_SMALL, L_FF, L_ACT, L_ATT = 6, 7, 8, 12, 16
R_PRE, R_OUT, R_ATT, R_QUERY, R_SMALL, R_KV = 0, 16, 32, 36, 38, 39
ABC, BCA, CBA, BAC = (0, 1, 2), (1, 2, 0), (2, 1, 0), (1, 0, 2)
PLAN = (
    (
        ("down", 0, (X, Z), ABC),
        ("down", 1, (X, Z), ABC),
        ("query", 0, (X, Y, Z), ABC),
        ("query", 1, (X, Y, Z), ABC),
        ("keyval", 0, (X, Y, Z), ABC),
        ("keyval", 2, (X, Y, Z), ABC),
    ),
    (
        ("out", 0, (Y, Z, X), BCA),
        ("out", 1, (Y, Z, X), BCA),
        ("up", 0, (Y, Z), BCA),
        ("up", 1, (Y, Z), BCA),
        ("keyval", 1, (Y, Z, X), BCA),
        ("keyval", 3, (Y, Z, X), BCA),
    ),
    (
        ("down", 2, (Z, X), BAC),
        ("down", 3, (Z, X), BAC),
        ("up", 2, (Z, Y), CBA),
        ("up", 3, (Z, Y), CBA),
        ("small", 0, (Z, Y, X), CBA),
        None,
    ),
)
GROUPS = 6
TICKS = GROUPS + 6


def mm(left, right):
    return jnp.dot(left, right, preferred_element_type=F32)


def mm_nt(left, right):
    return lax.dot_general(left, right, (((1,), (1,)), ((), ())), preferred_element_type=F32)


def mm_tn(left, right):
    return lax.dot_general(left, right, (((0,), (0,)), ((), ())), preferred_element_type=F32)


def normed_rows(values):
    average = jnp.mean(values, -1, keepdims=True)
    centred = values - average
    inverse = lax.rsqrt(jnp.mean(centred * centred, -1, keepdims=True) + NORM_EPS)
    return centred * inverse, inverse


def norm_back(grad, normed, inverse, gain):
    scaled = grad * gain
    inner = jnp.mean(scaled, -1, keepdims=True)
    along = jnp.mean(scaled * normed, -1, keepdims=True)
    back = inverse * (scaled - inner - normed * along)
    return back, jnp.sum(grad * normed, 0, keepdims=True), jnp.sum(grad, 0, keepdims=True)


def turned(block):
    rows = block.shape[0]
    if rows < 256:
        block = jnp.concatenate([block, jnp.zeros((256 - rows, block.shape[1]), block.dtype)], 0)
    return block.T.astype(BF16)


def head_stack(block):
    lane = lax.broadcasted_iota(jnp.int32, (64, 256), 1) // 64
    return jnp.concatenate([jnp.where(lane == h, block, jnp.zeros_like(block)) for h in range(4)], 0)


def head_merge(block):
    lane = lax.broadcasted_iota(jnp.int32, (64, 256), 1) // 64
    return sum(jnp.where(lane == h, block[64 * h : 64 * h + 64], 0.0) for h in range(4))


def column(block, k):
    return block[:, COLS * k : COLS * k + COLS]


def resampler_kernel(
    latents, media, mask, gains, biases, w_query, w_keyval, w_out, w_up, w_down, cotangent,
    resampled, latents_grad, out_small, out_query, out_keyval, out_out, out_up, out_down, m_own, m_got, land,
    xs, x1s, gys, accs, lin, ffin, qs, att, gatt, pres, sums, sent, m_stage, m_buf, wu, wd, gave,
    lefts, rights, own1, own2, own3, far1, far2, far3, near1, near2, near3, up_sum, up_got,
    w_sem, b_sem, x_sem, g_sem, r_sem, l_sem, m_send, m_recv, m_local, e_send, e_recv, c_sem, t_send, t_recv, u_send, u_recv,
):
    section = lax.axis_index("section")
    other = 1 - section
    me = lax.axis_index("dp")
    coords = (me // 16, (me // 4) % 4, me % 4)
    strides = (16, 4, 1)

    def at(axis, shift):
        return (coords[axis] + shift) % 4

    def peer(axis, shift):
        return me + (at(axis, shift) - coords[axis]) * strides[axis]

    barrier = pltpu.get_barrier_semaphore()
    pl.semaphore_signal(barrier, inc=1, device_id={"section": other}, device_id_type=MESH)
    greeted = [(X, 1), (X, 2), (X, 3), (Y, 1), (Y, 2), (Y, 3), (Z, 1), (Z, 3)]
    for axis, shift in greeted:
        pl.semaphore_signal(barrier, inc=1, device_id={"dp": peer(axis, shift)}, device_id_type=MESH)
    pl.semaphore_wait(barrier, 1 + len(greeted))

    def to_other(source, target, sem):
        return pltpu.make_async_remote_copy(
            src_ref=source, dst_ref=target, send_sem=sem.at[0], recv_sem=sem.at[1],
            device_id={"section": other}, device_id_type=MESH,
        )

    def weights(step):
        slot = step % 2
        cols = pl.ds(pl.multiple_of(step * 512, 512), 512)
        return (
            pltpu.make_async_copy(w_up.at[:, cols], wu.at[slot], w_sem.at[0, slot]),
            pltpu.make_async_copy(w_down.at[cols, :], wd.at[slot], w_sem.at[1, slot]),
        )

    def fetch(step):
        for c in weights(step):
            c.start()

    def fetched(step):
        for c in weights(step):
            c.wait()

    def media_rows(i):
        return pltpu.make_async_copy(
            media.at[pl.ds(pl.multiple_of(i * 256, 256), 256), :], m_buf.at[i % 2], b_sem.at[i % 2]
        )

    def exchange(kind, shift):
        axis = X if kind in (FF_IN, G_PRE) else Y
        if kind == FF_IN:
            source = gave.at[0]
        elif kind == G_OUT:
            source = gave.at[1]
        elif kind == ACT:
            source = own1.at[pl.ds(18 + 4 * at(axis, shift), 4), pl.ds(0, ROWS_ALL), :]
        else:
            source = pres.at[pl.ds(4 * at(axis, shift), 4)]
        return pltpu.make_async_remote_copy(
            src_ref=source, dst_ref=land.at[kind, shift - 1], send_sem=e_send.at[kind, shift - 1], recv_sem=e_recv.at[kind, shift - 1],
            device_id={"dp": peer(axis, shift)}, device_id_type=MESH,
        )

    def give(kind):
        for shift in (1, 3, 2):
            exchange(kind, shift).start()

    def taken(kind, use):
        def held(s):
            if kind == G_PRE:
                return own1.at[pl.ds(8 + 12 * (s % 2), 4), pl.ds(0, ROWS_ALL), :]
            return m_stage.at[s % 2, :, pl.ds(0, ROWS_ALL), :]

        def load(s):
            return pltpu.make_async_copy(land.at[kind, s], held(s), c_sem.at[s % 2])

        exchange(kind, 1).wait()
        load(0).start()
        for s in range(3):
            if s < 2:
                exchange(kind, s + 2).wait()
                load(s + 1).start()
            load(s).wait()
            use(s + 1, held(s))

    fetch(0)
    media_rows(0).start()

    def to_rows(ref, value):
        for k in range(4):
            ref[k] = column(value, k)

    @pl.when(section == 0)
    def _():
        given = pltpu.make_async_copy(latents, lin, c_sem.at[0])
        given.start()
        given.wait()
        xs[...] = lin[...].astype(F32)

    @pl.when(section == 1)
    def _():
        given = pltpu.make_async_copy(cotangent, lin, c_sem.at[0])
        given.start()
        given.wait()
        gys[...] = lin[...].astype(F32)
        to_rows(gave.at[1], lin[...].astype(F32))
        give(G_OUT)

    def media_block(i, carry):
        @pl.when(i < 5)
        def _():
            media_rows(i + 1).start()

        media_rows(i).wait()
        normed, _ = normed_rows(m_buf[i % 2].astype(F32))
        media_in = (normed * gains[0:1, :] + biases[0:1, :]).astype(BF16)
        keyval = mm(media_in, w_keyval[...]).astype(BF16)
        for j in range(4):
            lefts[i, j] = column(keyval, j)
        return carry

    lax.fori_loop(0, 6, media_block, 0)
    for k in list(range(38)) + [R_KV + 7 * j + 6 for j in range(4)]:
        rights[k, pl.ds(192, 64), :] = jnp.zeros((64, COLS), BF16)
    row = lax.broadcasted_iota(jnp.int32, (256, COLS), 0)
    col = lax.broadcasted_iota(jnp.int32, (256, COLS), 1)
    rights[R_SMALL] = jnp.where(((row == col) & (row < 6)) | ((row == col + 6) & (row >= 6) & (row < 12)), 1.0, 0.0).astype(BF16)

    @pl.when(section == 1)
    def _():
        to_other(accs, xs, x_sem).wait_recv()

    normed, _ = normed_rows(xs[...])
    lin[...] = (normed * gains[1:2, :] + biases[1:2, :]).astype(BF16)
    qs[...] = (mm(lin[...], w_query[...]) * 0.125).astype(BF16)
    latent_kv = mm(lin[...], w_keyval[...]).astype(BF16)
    for v in range(3):
        for j in range(4):
            rows = pl.ds((v % 2) * 128, 64)
            lefts[6 + v // 2, j, rows, :] = latent_kv[64 * v : 64 * v + 64, COLS * j : COLS * j + COLS]
            lefts[6 + v // 2, j, pl.ds((v % 2) * 128 + 64, 64), :] = jnp.zeros((64, COLS), BF16)

    def keyvals_of(v, j):
        tail = pl.ds(pl.multiple_of((v % 2) * 128, 128), 128)
        return lefts[2 * v, j], lefts[2 * v + 1, j], lefts[6 + v // 2, j, tail, :]

    def attend(v, carry):
        rows = pl.ds(pl.multiple_of(v * 64, 64), 64)
        valid = mask[v] > 0.0
        for g in range(2):
            cols = pl.ds(COLS * g, COLS)
            stacked = head_stack(qs[rows, cols])
            scores = [mm_nt(stacked, k) for k in keyvals_of(v, g)]
            scores = [
                jnp.where(valid[:, 256 * n : 256 * n + s.shape[1]], s, MASK_FILL) for n, s in enumerate(scores)
            ]
            top = jnp.max(jnp.maximum(scores[0], scores[1]), -1, keepdims=True)
            top = jnp.maximum(top, jnp.max(scores[2], -1, keepdims=True))
            raised = [jnp.exp(s - top) for s in scores]
            whole = jnp.sum(raised[0] + raised[1], -1, keepdims=True) + jnp.sum(raised[2], -1, keepdims=True)
            scale = 1.0 / whole
            mixed = jnp.zeros((256, COLS), F32)
            for n, (e, values) in enumerate(zip(raised, keyvals_of(v, 2 + g))):
                p = e * scale
                own1[(v * 2 + g) * 3 + n, :, pl.ds(0, p.shape[1])] = p
                mixed += mm(p.astype(BF16), values)
            att[rows, cols] = head_merge(mixed).astype(BF16)
        return carry

    lax.fori_loop(0, 3, attend, 0)

    x1 = xs[...] + mm(att[...], w_out[...])
    x1s[...] = x1
    accs[...] = x1
    normed, _ = normed_rows(x1)
    ffin[...] = (normed * gains[2:3, :] + biases[2:3, :]).astype(BF16)
    to_rows(gave.at[0], ffin[...].astype(F32))
    give(FF_IN)

    def ff_forward(j, carry):
        fetched(j)

        @pl.when(j + 1 < FF_STEPS)
        def _():
            fetch(j + 1)

        pre = mm(ffin[...], wu[j % 2])
        act = (pre * (0.5 * (1.0 + lax.erf(pre * ROOT_HALF)))).astype(BF16)
        for k in range(2):
            pres[2 * j + k] = column(pre, k)
            own1[18 + 4 * (2 * (j % 2) + k) + j // 2, pl.ds(0, ROWS_ALL), :] = column(act, k).astype(F32)
        accs[...] += mm(act, wd[j % 2])
        return carry

    lax.fori_loop(0, FF_STEPS, ff_forward, 0)
    give(ACT)
    fetch(0)

    def turn_forward():
        for k in range(4):
            lefts[L_FF, k] = turned(gave[0, k])

        def use_ff(s, piece):
            for k in range(4):
                lefts[L_FF + s, k] = turned(piece[k])

        taken(FF_IN, use_ff)
        for k in range(4):
            lefts[L_ACT, k] = turned(own1[18 + 4 * coords[Y] + k, pl.ds(0, ROWS_ALL), :])

        def use_act(s, piece):
            for k in range(4):
                lefts[L_ACT + s, k] = turned(piece[k])

        taken(ACT, use_act)
        for i in range(4):
            part = jnp.concatenate([att[:, pl.ds(128 * i, 128)].astype(F32), jnp.zeros((64, 128), F32)], 0)
            part = part.T.reshape(16, 8, 256)
            none = jnp.zeros_like(part)
            lefts[L_ATT, i] = jnp.concatenate([part, none], 1).reshape(256, 256).astype(BF16)
            lefts[L_ATT + 1, i] = jnp.concatenate([none, part], 1).reshape(256, 256).astype(BF16)

    @pl.when(section == 0)
    def _():
        to_other(accs, xs, x_sem).start()
        turn_forward()
        to_other(accs, xs, x_sem).wait_send()
        to_other(accs, gys, g_sem).wait_recv()
        to_rows(gave.at[1], gys[...].astype(BF16).astype(F32))
        give(G_OUT)

    @pl.when(section == 1)
    def _():
        sent[...] = accs[:, pl.ds(0, 512)]
        to_other(sent, resampled, r_sem).start()
        resampled[...] = accs[:, pl.ds(512, 512)]

    ffin[...] = gys[...].astype(BF16)
    for k in range(4):
        rights[R_OUT + k, pl.ds(0, ROWS_ALL), :] = ffin[:, pl.ds(COLS * k, COLS)]
    accs[...] = jnp.zeros((ROWS_ALL, 1024), F32)

    def ff_backward(j, carry):
        fetched(j)

        @pl.when(j + 1 < FF_STEPS)
        def _():
            fetch(j + 1)

        grad_act = mm_nt(ffin[...], wd[j % 2])
        halves = []
        for k in range(2):
            pre = pres[2 * j + k]
            slope = 0.5 * (1.0 + lax.erf(pre * ROOT_HALF)) + pre * jnp.exp(-0.5 * pre * pre) * INV_ROOT_TAU
            halves.append((column(grad_act, k) * slope).astype(BF16))
            pres[2 * j + k] = halves[k].astype(F32)
        accs[...] += mm_nt(halves[0], wu[j % 2, :, pl.ds(0, 256)]) + mm_nt(halves[1], wu[j % 2, :, pl.ds(256, 256)])
        return carry

    lax.fori_loop(0, FF_STEPS, ff_backward, 0)
    give(G_PRE)

    normed, inverse = normed_rows(x1s[...])
    back, gain_sum, bias_sum = norm_back(accs[...], normed, inverse, gains[2:3, :])
    sums[pl.ds(2, 1), :] = gain_sum
    sums[pl.ds(5, 1), :] = bias_sum
    grad_x1 = gys[...] + back
    gys[...] = grad_x1
    grad_attn = grad_x1.astype(BF16)
    for k in range(4):
        rights[R_ATT + k, pl.ds(0, ROWS_ALL), :] = column(grad_attn, k)
    gatt[...] = mm_nt(grad_attn, w_out[...]).astype(BF16)

    def attend_back(v, carry):
        rows = pl.ds(pl.multiple_of(v * 64, 64), 64)
        for g in range(2):
            cols = pl.ds(COLS * g, COLS)
            q_stack = head_stack(qs[rows, cols])
            g_stack = head_stack(gatt[rows, cols])
            widths = (256, 256, 128)
            probs = [own1[(v * 2 + g) * 3 + n, :, pl.ds(0, widths[n])] for n in range(3)]
            weighted = [p * mm_nt(g_stack, values) for p, values in zip(probs, keyvals_of(v, 2 + g))]
            whole = jnp.sum(weighted[0] + weighted[1], -1, keepdims=True) + jnp.sum(weighted[2], -1, keepdims=True)
            grad_s = [(w - p * whole).astype(BF16) for w, p in zip(weighted, probs)]
            grad_q = sum(mm(s, k) for s, k in zip(grad_s, keyvals_of(v, g)))
            rights[R_QUERY + g, rows, :] = head_merge(grad_q).astype(BF16)
            for base, factors, stack in (
                (R_KV + 7 * g, grad_s, q_stack),
                (R_KV + 14 + 7 * g, [p.astype(BF16) for p in probs], g_stack),
            ):
                rights[base + 2 * v] = mm_tn(factors[0], stack).astype(BF16)
                rights[base + 2 * v + 1] = mm_tn(factors[1], stack).astype(BF16)
                rights[base + 6, rows, :] = mm_tn(factors[2], stack)[:64].astype(BF16)
        return carry

    lax.fori_loop(0, 3, attend_back, 0)

    grad_in = sum(mm_nt(rights[R_QUERY + g, pl.ds(0, ROWS_ALL), :], w_query[:, pl.ds(COLS * g, COLS)]) for g in range(2))
    grad_in = grad_in * 0.125
    for k in range(4):
        grad_in += mm_nt(rights[R_KV + 6 + 7 * k, pl.ds(0, ROWS_ALL), :], w_keyval[:, pl.ds(COLS * k, COLS)])
    normed, inverse = normed_rows(xs[...])
    back, gain_sum, bias_sum = norm_back(grad_in, normed, inverse, gains[1:2, :])
    sums[pl.ds(1, 1), :] = gain_sum
    sums[pl.ds(4, 1), :] = bias_sum
    accs[...] = gys[...] + back

    @pl.when(section == 1)
    def _():
        to_other(accs, gys, g_sem).start()
        turn_forward()

    @pl.when(section == 0)
    def _():
        sent[...] = accs[:, pl.ds(512, 512)]
        to_other(sent, latents_grad, l_sem).start()
        latents_grad[...] = accs[:, pl.ds(0, 512)]

    def use_out(s, piece):
        for k in range(4):
            rights[R_OUT + 4 * s + k, pl.ds(0, ROWS_ALL), :] = piece[k].astype(BF16)

    taken(G_OUT, use_out)

    def turn_pre():
        for k in range(4):
            rights[R_PRE + k, pl.ds(0, ROWS_ALL), :] = pres[4 * coords[X] + k].astype(BF16)

        def use_pre(s, piece):
            for k in range(4):
                rights[R_PRE + 4 * s + k, pl.ds(0, ROWS_ALL), :] = piece[k].astype(BF16)

        taken(G_PRE, use_pre)

    def media_away(i):
        return pltpu.make_async_remote_copy(
            src_ref=m_stage.at[i % 2, pl.ds(2 * other, 2)], dst_ref=m_got.at[i], send_sem=m_send.at[i], recv_sem=m_recv.at[i],
            device_id={"section": other}, device_id_type=MESH,
        )

    def media_home(i):
        return pltpu.make_async_copy(m_stage.at[i % 2, pl.ds(2 * section, 2)], m_own.at[i], m_local.at[i])

    def media_back(i):
        if i < 5:
            media_rows(i + 1).start()
        media_rows(i).wait()
        if i >= 2:
            media_away(i - 2).wait_send()
            media_home(i - 2).wait()
        normed, inverse = normed_rows(m_buf[i % 2].astype(F32))
        media_in = normed * gains[0:1, :] + biases[0:1, :]
        grad_media = mm_nt(rights[R_KV + i], w_keyval[:, pl.ds(0, COLS)])
        for k in range(1, 4):
            grad_media += mm_nt(rights[R_KV + 7 * k + i], w_keyval[:, pl.ds(COLS * k, COLS)])
        back, gain_sum, bias_sum = norm_back(grad_media, normed, inverse, gains[0:1, :])
        if i == 0:
            sums[pl.ds(0, 1), :] = gain_sum
            sums[pl.ds(3, 1), :] = bias_sum
        else:
            sums[pl.ds(0, 1), :] += gain_sum
            sums[pl.ds(3, 1), :] += bias_sum
        for k in range(4):
            m_stage[i % 2, k] = column(back, k)
        media_away(i).start()
        media_home(i).start()
        for k in range(4):
            lefts[i, k] = turned(column(media_in, k).astype(BF16).astype(F32))

    def small_left():
        total = sums[pl.ds(0, 6), :]
        high = total.astype(BF16).astype(F32)
        block = jnp.concatenate([high, total - high, jnp.zeros((244, 1024), F32)], 0)
        for k in range(4):
            lefts[L_SMALL, k] = turned(column(block, k))

    def factors(what, which):
        if what == "up":
            return [(L_FF + s, R_PRE + 4 * s + which) for s in range(4)]
        if what == "down":
            return [(L_ACT + s, R_OUT + 4 * s + which) for s in range(4)]
        if what == "out":
            return [(L_ATT + s, R_ATT + 2 * which + s) for s in range(2)]
        if what == "query":
            return [(L_LATENT, R_QUERY + which)]
        if what == "small":
            return [(L_SMALL, R_SMALL)]
        return [(k, R_KV + 7 * which + k) for k in range(7)]

    own = (own1, own2, own3)
    far = (far1, far2, far3)
    near = (near1, near2, near3)

    def spot(lane, group):
        return (lane * 3 + group % 3) * 4

    def terms(lane, group):
        what, which, _, order = PLAN[lane][group]
        base = spot(lane, group)

        def block(i, carry):
            total = sum(mm(lefts[a, i], rights[b]) for a, b in factors(what, which))
            if order == ABC:
                own1[base + i] = total
            else:
                for b in range(4):
                    for c in range(4):
                        first, second, third = [(i, b, c)[n] for n in order]
                        rows = pl.ds(pl.multiple_of((second * 4 + third) * 16, 16), 16)
                        own1[base + first, rows, :] = total[(b * 4 + c) * 16 : (b * 4 + c) * 16 + 16]
            return carry

        lax.fori_loop(0, 4, block, 0)

    def ring_copy(lane, group, stage, step, way):
        axis = PLAN[lane][group][2][stage]
        half = RING_ROWS[stage] // 2
        shift = 1 if way == 0 else 3
        turn = group % 3 if stage == 0 and step == 0 else group % 2
        sem = (((lane * 3 + stage) * 2 + step) * 2 + way) * 3 + turn
        if step == 0:
            source = own[stage].at[spot(lane, group) + at(axis, 2), pl.ds(way * half, half)]
            target = far[stage].at[lane, way, turn]
        else:
            source = own[stage].at[spot(lane, group) + at(axis, shift)]
            target = near[stage].at[lane, way, turn]
        return pltpu.make_async_remote_copy(
            src_ref=source, dst_ref=target, send_sem=t_send.at[sem], recv_sem=t_recv.at[sem],
            device_id={"dp": peer(axis, shift)}, device_id_type=MESH,
        )

    def runs(lane, group, stage):
        return 0 <= group < GROUPS and PLAN[lane][group] is not None and stage < len(PLAN[lane][group][2])

    def up_copy(shift):
        rows = pl.ds(pl.multiple_of(16 * at(X, shift), 16), 16)
        return pltpu.make_async_remote_copy(
            src_ref=up_sum.at[rows, :], dst_ref=up_got.at[shift - 1], send_sem=u_send.at[shift - 1], recv_sem=u_recv.at[shift - 1],
            device_id={"dp": peer(X, shift)}, device_id_type=MESH,
        )

    def finish(what, which, total):
        cols = pl.ds(COLS * which, COLS)
        if what == "up":
            up_sum[:, cols] = total
        elif what == "down":
            out_down[:, cols] = total
        elif what == "query":
            out_query[:, cols] = total * 0.125
        elif what == "keyval":
            out_keyval[:, cols] = total
        elif what == "out":
            out_out[:, pl.ds(512 * which, COLS)] = total[:8]
            out_out[:, pl.ds(512 * which + COLS, COLS)] = total[8:]
        else:
            out_small[...] = total

    for k in range(4):
        lefts[L_LATENT, k] = turned(lin[:, pl.ds(COLS * k, COLS)].astype(F32))
    media_rows(0).start()
    ups = 0
    for t in range(TICKS):
        for lane in range(3):
            if runs(lane, t, 0):
                terms(lane, t)
                for way in range(2):
                    ring_copy(lane, t, 0, 0, way).start()
        if t == 0:
            media_back(0)
            turn_pre()
        if t == 1:
            media_back(1)
            media_back(2)
        if t == 2:
            media_back(3)
            media_back(4)
        if t == 3:
            media_back(5)
            small_left()
        for stage in range(3):
            for lane in range(3):
                half = RING_ROWS[stage] // 2
                group = t - 1 - 2 * stage
                if runs(lane, group, stage):
                    axis = PLAN[lane][group][2][stage]
                    turn = group % 3 if stage == 0 else group % 2
                    for way in range(2):
                        ring_copy(lane, group, stage, 0, way).wait()
                        own[stage][spot(lane, group) + at(axis, 1 if way == 0 else 3), pl.ds(way * half, half), :] += far[stage][
                            lane, way, turn
                        ]
                group = t - 2 - 2 * stage
                if runs(lane, group, stage):
                    what, which, axes, _ = PLAN[lane][group]
                    for way in range(2):
                        ring_copy(lane, group, stage, 1, way).wait()
                    total = (
                        own[stage][spot(lane, group) + at(axes[stage], 0)]
                        + near[stage][lane, 0, group % 2]
                        + near[stage][lane, 1, group % 2]
                    )
                    if stage + 1 < len(axes):
                        rows = RING_ROWS[stage + 1]
                        for k in range(4):
                            own[stage + 1][spot(lane, group) + k] = total[rows * k : rows * k + rows]
                    else:
                        finish(what, which, total)
                        if what == "up":
                            ups += 1
                            if ups == 4:
                                for shift in (1, 2, 3):
                                    up_copy(shift).start()
        for stage in range(3):
            for lane in range(3):
                if stage > 0 and runs(lane, t - 2 * stage, stage):
                    for way in range(2):
                        ring_copy(lane, t - 2 * stage, stage, 0, way).start()
                if runs(lane, t - 1 - 2 * stage, stage):
                    for way in range(2):
                        ring_copy(lane, t - 1 - 2 * stage, stage, 1, way).start()

    for s in range(4):
        part = up_sum[pl.ds(pl.multiple_of(16 * coords[X], 16), 16), :] if s == 0 else None
        if s > 0:
            up_copy(s).wait()
            part = up_got[s - 1]
        cols = pl.ds(pl.multiple_of(1024 * at(X, 4 - s), 1024), 1024)
        out_up[:, cols] = part

    for i in (4, 5):
        media_away(i).wait_send()
        media_home(i).wait()
    for i in range(6):
        media_away(i).wait_recv()

    @pl.when(section == 0)
    def _():
        to_other(sent, resampled, r_sem).wait_recv()
        to_other(sent, latents_grad, l_sem).wait_send()

    @pl.when(section == 1)
    def _():
        to_other(sent, resampled, r_sem).wait_send()
        to_other(accs, gys, g_sem).wait_send()
        to_other(sent, latents_grad, l_sem).wait_recv()


def run_resampler(latents, media, mask, gains, biases, w_query, w_keyval, w_out, w_up, w_down, cotangent):
    vmem = pl.BlockSpec(memory_space=pltpu.VMEM)
    hbm = pl.BlockSpec(memory_space=pl.ANY)

    def sds(*shape):
        return jax.ShapeDtypeStruct(shape, F32)

    dma = pltpu.SemaphoreType.DMA
    return pl.pallas_call(
        resampler_kernel,
        out_shape=[
            sds(192, 512), sds(192, 512), sds(16, 256), sds(16, 512), sds(16, 1024), sds(8, 1024), sds(16, 4096), sds(64, 1024),
            sds(6, 2, 256, 256), sds(6, 2, 256, 256), sds(4, 3, 4, 192, 256),
        ],
        in_specs=[hbm, hbm] + [vmem] * 6 + [hbm, hbm, hbm],
        out_specs=[vmem] * 8 + [hbm] * 3,
        scratch_shapes=[
            pltpu.VMEM((192, 1024), F32),
            pltpu.VMEM((192, 1024), F32),
            pltpu.VMEM((192, 1024), F32),
            pltpu.VMEM((192, 1024), F32),
            pltpu.VMEM((192, 1024), BF16),
            pltpu.VMEM((192, 1024), BF16),
            pltpu.VMEM((192, 512), BF16),
            pltpu.VMEM((192, 512), BF16),
            pltpu.VMEM((192, 512), BF16),
            pltpu.VMEM((16, 192, 256), F32),
            pltpu.VMEM((8, 1024), F32),
            pltpu.VMEM((192, 512), F32),
            pltpu.VMEM((2, 4, 256, 256), F32),
            pltpu.VMEM((2, 256, 1024), BF16),
            pltpu.VMEM((2, 1024, 512), BF16),
            pltpu.VMEM((2, 512, 1024), BF16),
            pltpu.VMEM((2, 4, 192, 256), F32),
            pltpu.VMEM((18, 4, 256, 256), BF16),
            pltpu.VMEM((67, 256, 256), BF16),
        ]
        + [pltpu.VMEM((36, r, COLS), F32) for r in RING_ROWS]
        + [pltpu.VMEM((3, 2, 3 if r == 256 else 2, r // 2, COLS), F32) for r in RING_ROWS]
        + [pltpu.VMEM((3, 2, 2, r, COLS), F32) for r in RING_ROWS]
        + [
            pltpu.VMEM((64, 1024), F32),
            pltpu.VMEM((3, 16, 1024), F32),
            dma((2, 2)), dma((2,)), dma((2,)), dma((2,)), dma((2,)), dma((2,)), dma((6,)), dma((6,)), dma((6,)),
            dma((4, 3)), dma((4, 3)), dma((2,)), dma((108,)), dma((108,)), dma((3,)), dma((3,)),
        ],
        compiler_params=pltpu.CompilerParams(collective_id=1, has_side_effects=True, vmem_limit_bytes=VMEM_BYTES),
        name="resampler",
    )(latents, media, mask, gains, biases, w_query, w_keyval, w_out, w_up, w_down, cotangent)


def body(
    latents_in, media, frame_count, gains, biases, w_query, w_keyval, w_out, w_up, w_down, cotangent
):
    key = jnp.arange(KEYS)
    valid = (key[None] < 64 * frame_count) | ((key[None] >= 512) & (key[None] < 576))
    mask = valid.astype(F32)[:, None, :]
    resampled, latents_grad, small, query, keyval, out, up, down, mine, theirs, _ = run_resampler(
        latents_in.reshape(192, 1024), media.reshape(1536, 1024), mask, gains[0], biases[0],
        w_query[0], w_keyval[0], w_out[0], w_up[0], w_down[0], cotangent.reshape(192, 1024),
    )
    small = small[:, :6].T
    return (
        resampled.reshape(3, 1, 64, 512),
        latents_grad.reshape(3, 1, 64, 512),
        (mine + theirs).transpose(0, 2, 1, 3).reshape(3, 1, 512, 512),
        small[None, :3],
        small[None, 3:],
        query[None],
        keyval[None],
        out[None],
        up[None],
        down[None],
    )


def solution(mesh):
    placed = (
        P(None, "dp", None, None),
        P(None, "dp", None, None),
        P(None, "dp"),
        P("section", None, None),
        P("section", None, None),
        P("section", None, None),
        P("section", None, None),
        P("section", None, None),
        P("section", None, None),
        P("section", None, None),
        P(None, "dp", None, None),
    )
    return jax.shard_map(
        body,
        mesh=mesh,
        in_specs=placed,
        out_specs=(
            P(None, "dp", None, "section"),
            P(None, "dp", None, "section"),
            P(None, "dp", None, "section"),
            P("section", None, "dp"),
            P("section", None, "dp"),
            P("section", "dp", None),
            P("section", "dp", None),
            P("section", "dp", None),
            P("section", "dp", None),
            P("section", "dp", None),
        ),
        check_vma=False,
    )
```

```python
import jax
import jax.numpy as jnp
from jax import lax
from jax.experimental import pallas as pl
from jax.experimental.pallas import tpu as pltpu
from jax.sharding import PartitionSpec as P

VMEM_BYTES = 63 * 2**20
MESH = pl.DeviceIdType.MESH
F32 = jnp.float32
BF16 = jnp.bfloat16
NORM_EPS = 1e-05
MASK_FILL = -1e30
ROOT_HALF = 0.7071067811865476
INV_ROOT_TAU = 0.3989422804014327
ROWS_ALL = 192
KEYS = 640
FF_STEPS = 8
RING_ROWS = (256, 64, 16)
COLS = 256
A, B, C = 0, 1, 2
FF_IN, ACT, G_OUT, G_PRE = 0, 1, 2, 3
L_LATENT, L_SMALL, L_FF, L_ACT, L_ATT = 6, 7, 8, 12, 16
R_PRE, R_OUT, R_ATT, R_QUERY, R_SMALL, R_KV = 0, 16, 32, 36, 38, 39
PLAN = (
    (
        ("down", 0, (A, C)),
        ("query", 0, (A, B, C)),
        ("query", 1, (A, B, C)),
        ("keyval", 0, (A, B, C)),
        ("keyval", 2, (A, B, C)),
        ("down", 1, (A, C)),
    ),
    (
        ("out", 0, (B, C, A)),
        ("up", 0, (B, C)),
        ("up", 1, (B, C)),
        ("keyval", 1, (B, C, A)),
        ("keyval", 3, (B, C, A)),
        None,
    ),
    (
        ("out", 1, (C, B, A)),
        ("down", 2, (C, A)),
        ("up", 2, (C, B)),
        ("up", 3, (C, B)),
        ("small", 0, (C, B, A)),
        ("down", 3, (C, A)),
    ),
)
GROUPS = 6
TICKS = GROUPS + 4
WIDE = 4
DEEP = 3
WU_BASE = 35


def mm(left, right):
    return jnp.dot(left, right, preferred_element_type=F32)


def mm_nt(left, right):
    return lax.dot_general(left, right, (((1,), (1,)), ((), ())), preferred_element_type=F32)


def mm_tn(left, right):
    return lax.dot_general(left, right, (((0,), (0,)), ((), ())), preferred_element_type=F32)


def normed_rows(values):
    average = jnp.mean(values, -1, keepdims=True)
    centred = values - average
    inverse = lax.rsqrt(jnp.mean(centred * centred, -1, keepdims=True) + NORM_EPS)
    return centred * inverse, inverse


def norm_back(grad, normed, inverse, gain):
    scaled = grad * gain
    inner = jnp.mean(scaled, -1, keepdims=True)
    along = jnp.mean(scaled * normed, -1, keepdims=True)
    back = inverse * (scaled - inner - normed * along)
    return back, jnp.sum(grad * normed, 0, keepdims=True), jnp.sum(grad, 0, keepdims=True)


def turned(block):
    rows = block.shape[0]
    if rows < 256:
        block = jnp.concatenate([block, jnp.zeros((256 - rows, block.shape[1]), block.dtype)], 0)
    return block.T.astype(BF16)


def head_stack(block):
    lane = lax.broadcasted_iota(jnp.int32, (64, 256), 1) // 64
    return jnp.concatenate([jnp.where(lane == h, block, jnp.zeros_like(block)) for h in range(4)], 0)


def head_merge(block):
    lane = lax.broadcasted_iota(jnp.int32, (64, 256), 1) // 64
    return sum(jnp.where(lane == h, block[64 * h : 64 * h + 64], 0.0) for h in range(4))


def column(block, k):
    return block[:, COLS * k : COLS * k + COLS]


def resampler_kernel(
    latents, media, frame_count, gains, biases, w_query, w_keyval, w_out, w_up, w_down, cotangent,
    resampled, latents_grad, out_small, out_query, out_keyval, out_out, out_up, out_down, m_own, m_got, land,
    wq, wkv, wo, xs, x1s, gys, accs, lin, ffin, qs, att, gatt, pres, sums, sent, m_stage, m_buf, wd, gave,
    lefts, rights, own1, own2, own3, far1, far2, mine1, summed1, near2, last, up_sum, up_got,
    a_sem, w_sem, b_sem, x_sem, g_sem, r_sem, l_sem, m_send, m_recv, m_local, e_send, e_recv, c_sem, t_send, t_recv, z_send, z_recv, u_send, u_recv,
):
    section = lax.axis_index("section")
    other = 1 - section
    me = lax.axis_index("dp")
    x, y, z = me // 16, (me // 4) % 4, me % 4

    def by_section(first, second):
        return first + section * (second - first)

    coords = (by_section(x, z), by_section(y, x), by_section(z, y))
    strides = (by_section(16, 1), by_section(4, 16), by_section(1, 4))

    def at(axis, shift):
        return (coords[axis] + shift) % 4

    def peer(axis, shift):
        return me + (at(axis, shift) - coords[axis]) * strides[axis]

    held = [pltpu.make_async_copy(*pair, a_sem.at[n]) for n, pair in enumerate(((w_keyval, wkv), (w_query, wq), (w_out, wo)))]
    for c in held:
        c.start()
    barrier = pltpu.get_barrier_semaphore()
    pl.semaphore_signal(barrier, inc=1, device_id={"section": other}, device_id_type=MESH)
    greeted = [(axis, shift) for axis in (A, B, C) for shift in (1, 2, 3)]
    for axis, shift in greeted:
        pl.semaphore_signal(barrier, inc=1, device_id={"dp": peer(axis, shift)}, device_id_type=MESH)
    pl.semaphore_wait(barrier, 1 + len(greeted))

    def to_other(source, target, sem):
        return pltpu.make_async_remote_copy(
            src_ref=source, dst_ref=target, send_sem=sem.at[0], recv_sem=sem.at[1],
            device_id={"section": other}, device_id_type=MESH,
        )

    def up_block(step):
        return WU_BASE + 8 * (step % WIDE)

    def weights(step):
        copies = [pltpu.make_async_copy(w_down.at[pl.ds(pl.multiple_of(step * 512, 512), 512), :], wd.at[step % DEEP], w_sem.at[2, step % DEEP])]
        for k in range(2):
            cols = pl.ds(pl.multiple_of(step * 512 + COLS * k, COLS), COLS)
            copies.append(
                pltpu.make_async_copy(w_up.at[:, :, cols], rights.at[pl.ds(up_block(step) + 4 * k, 4)], w_sem.at[k, step % WIDE])
            )
        return copies

    def fetch(step):
        for c in weights(step):
            c.start()

    def fetch_first():
        for step in range(DEEP - 1):
            fetch(step)

    def fetch_next(step):
        @pl.when(step + DEEP - 1 < FF_STEPS)
        def _():
            fetch(step + DEEP - 1)

    def fetched(step):
        for c in weights(step):
            c.wait()

    def media_rows(i):
        return pltpu.make_async_copy(
            media.at[pl.ds(pl.multiple_of(i * 256, 256), 256), :], m_buf.at[i % 2], b_sem.at[i % 2]
        )

    def exchange(kind, shift):
        axis = A if kind in (FF_IN, G_PRE) else B
        if kind == FF_IN:
            source = gave.at[0]
        elif kind == G_OUT:
            source = gave.at[1]
        elif kind == ACT:
            source = own1.at[pl.ds(18 + 4 * at(axis, shift), 4), pl.ds(0, ROWS_ALL), :]
        else:
            source = pres.at[pl.ds(4 * at(axis, shift), 4)]
        return pltpu.make_async_remote_copy(
            src_ref=source, dst_ref=land.at[kind, shift - 1], send_sem=e_send.at[kind, shift - 1], recv_sem=e_recv.at[kind, shift - 1],
            device_id={"dp": peer(axis, shift)}, device_id_type=MESH,
        )

    def give(kind):
        for shift in (1, 3, 2):
            exchange(kind, shift).start()

    def taken(kind, use):
        def held(s):
            if kind == G_PRE:
                return own1.at[pl.ds(8 + 12 * (s % 2), 4), pl.ds(0, ROWS_ALL), :]
            return m_stage.at[s % 2, :, pl.ds(0, ROWS_ALL), :]

        def load(s):
            return pltpu.make_async_copy(land.at[kind, s], held(s), c_sem.at[s % 2])

        exchange(kind, 1).wait()
        load(0).start()
        for s in range(3):
            if s < 2:
                exchange(kind, s + 2).wait()
                load(s + 1).start()
            load(s).wait()
            use(s + 1, held(s))

    fetch_first()
    media_rows(0).start()

    def to_rows(ref, value):
        for k in range(4):
            ref[k] = column(value, k)

    @pl.when(section == 0)
    def _():
        given = pltpu.make_async_copy(latents, lin, c_sem.at[0])
        given.start()
        given.wait()
        xs[...] = lin[...].astype(F32)

    @pl.when(section == 1)
    def _():
        given = pltpu.make_async_copy(cotangent, lin, c_sem.at[0])
        given.start()
        given.wait()
        gys[...] = lin[...].astype(F32)
        to_rows(gave.at[1], lin[...].astype(F32))
        give(G_OUT)

    def media_block(i, carry):
        @pl.when(i < 5)
        def _():
            media_rows(i + 1).start()

        media_rows(i).wait()
        normed, _ = normed_rows(m_buf[i % 2].astype(F32))
        media_in = (normed * gains[0, 0:1, :] + biases[0, 0:1, :]).astype(BF16)
        keyval = mm(media_in, wkv[0]).astype(BF16)
        for j in range(4):
            lefts[i, j] = column(keyval, j)
        return carry

    held[0].wait()
    lax.fori_loop(0, 6, media_block, 0)
    held[1].wait()
    held[2].wait()
    @pl.when(section == 1)
    def _():
        to_other(accs, xs, x_sem).wait_recv()

    normed, _ = normed_rows(xs[...])
    lin[...] = (normed * gains[0, 1:2, :] + biases[0, 1:2, :]).astype(BF16)
    qs[...] = (mm(lin[...], wq[0]) * 0.125).astype(BF16)
    latent_kv = mm(lin[...], wkv[0]).astype(BF16)
    for v in range(3):
        for j in range(4):
            rows = pl.ds((v % 2) * 128, 64)
            lefts[6 + v // 2, j, rows, :] = latent_kv[64 * v : 64 * v + 64, COLS * j : COLS * j + COLS]
            lefts[6 + v // 2, j, pl.ds((v % 2) * 128 + 64, 64), :] = jnp.zeros((64, COLS), BF16)

    def keyvals_of(v, j):
        tail = pl.ds(pl.multiple_of((v % 2) * 128, 128), 128)
        return lefts[2 * v, j], lefts[2 * v + 1, j], lefts[6 + v // 2, j, tail, :]

    key = lax.broadcasted_iota(jnp.int32, (1, KEYS), 1)

    def attend(v, carry):
        rows = pl.ds(pl.multiple_of(v * 64, 64), 64)
        valid = (key < 64 * frame_count[v, 0]) | ((key >= 512) & (key < 576))
        for g in range(2):
            cols = pl.ds(COLS * g, COLS)
            stacked = head_stack(qs[rows, cols])
            scores = [mm_nt(stacked, k) for k in keyvals_of(v, g)]
            scores = [
                jnp.where(valid[:, 256 * n : 256 * n + s.shape[1]], s, MASK_FILL) for n, s in enumerate(scores)
            ]
            top = jnp.max(jnp.maximum(scores[0], scores[1]), -1, keepdims=True)
            top = jnp.maximum(top, jnp.max(scores[2], -1, keepdims=True))
            raised = [jnp.exp(s - top) for s in scores]
            whole = jnp.sum(raised[0] + raised[1], -1, keepdims=True) + jnp.sum(raised[2], -1, keepdims=True)
            scale = 1.0 / whole
            mixed = jnp.zeros((256, COLS), F32)
            for n, (e, values) in enumerate(zip(raised, keyvals_of(v, 2 + g))):
                p = e * scale
                own1[(v * 2 + g) * 3 + n, :, pl.ds(0, p.shape[1])] = p
                mixed += mm(p.astype(BF16), values)
            att[rows, cols] = head_merge(mixed).astype(BF16)
        return carry

    lax.fori_loop(0, 3, attend, 0)

    x1 = xs[...] + mm(att[...], wo[0])
    x1s[...] = x1
    accs[...] = x1
    normed, _ = normed_rows(x1)
    ffin[...] = (normed * gains[0, 2:3, :] + biases[0, 2:3, :]).astype(BF16)
    to_rows(gave.at[0], ffin[...].astype(F32))
    give(FF_IN)

    def ff_forward(j, carry):
        fetched(j)
        fetch_next(j)
        acts = []
        for k in range(2):
            base = up_block(j) + 4 * k
            pre = sum(mm(ffin[:, pl.ds(COLS * r, COLS)], rights[base + r]) for r in range(4))
            act = (pre * (0.5 * (1.0 + lax.erf(pre * ROOT_HALF)))).astype(BF16)
            pres[2 * j + k] = pre
            own1[18 + by_section(4 * (2 * (j % 2) + k) + j // 2, 2 * j + k), pl.ds(0, ROWS_ALL), :] = act.astype(F32)
            acts.append(act)
        accs[...] += mm(jnp.concatenate(acts, 1), wd[j % DEEP])
        return carry

    lax.fori_loop(0, FF_STEPS, ff_forward, 0)
    give(ACT)
    fetch_first()

    def turn_forward():
        for k in range(4):
            lefts[L_FF, k] = turned(gave[0, k])

        def use_ff(s, piece):
            for k in range(4):
                lefts[L_FF + s, k] = turned(piece[k])

        taken(FF_IN, use_ff)
        for k in range(4):
            lefts[L_ACT, k] = turned(own1[18 + 4 * coords[B] + k, pl.ds(0, ROWS_ALL), :])

        def use_act(s, piece):
            for k in range(4):
                lefts[L_ACT + s, k] = turned(piece[k])

        taken(ACT, use_act)
        for i in range(4):
            part = jnp.concatenate([att[:, pl.ds(128 * i, 128)].astype(F32), jnp.zeros((64, 128), F32)], 0)
            part = part.T.reshape(16, 8, 256)
            none = jnp.zeros_like(part)
            lefts[L_ATT, i] = jnp.concatenate([part, none], 1).reshape(256, 256).astype(BF16)
            lefts[L_ATT + 1, i] = jnp.concatenate([none, part], 1).reshape(256, 256).astype(BF16)

    @pl.when(section == 0)
    def _():
        to_other(accs, xs, x_sem).start()
        turn_forward()
        to_other(accs, xs, x_sem).wait_send()
        to_other(accs, gys, g_sem).wait_recv()
        to_rows(gave.at[1], gys[...].astype(BF16).astype(F32))
        give(G_OUT)

    @pl.when(section == 1)
    def _():
        sent[...] = accs[:, pl.ds(0, 512)]
        to_other(sent, resampled, r_sem).start()
        resampled[...] = accs[:, pl.ds(512, 512)]

    ffin[...] = gys[...].astype(BF16)
    accs[...] = jnp.zeros((ROWS_ALL, 1024), F32)

    def ff_backward(j, carry):
        fetched(j)
        fetch_next(j)
        grad_act = mm_nt(ffin[...], wd[j % DEEP])
        halves = []
        for k in range(2):
            pre = pres[2 * j + k]
            slope = 0.5 * (1.0 + lax.erf(pre * ROOT_HALF)) + pre * jnp.exp(-0.5 * pre * pre) * INV_ROOT_TAU
            halves.append((column(grad_act, k) * slope).astype(BF16))
            pres[2 * j + k] = halves[k].astype(F32)
        base = up_block(j)
        for r in range(4):
            accs[:, pl.ds(COLS * r, COLS)] += mm_nt(halves[0], rights[base + r]) + mm_nt(halves[1], rights[base + 4 + r])
        quarter = j // 2
        shift = (quarter - coords[A] + 4) % 4

        @pl.when((j % 2 == 1) & (shift != 0))
        def _():
            exchange(G_PRE, shift).start()

        return carry

    lax.fori_loop(0, FF_STEPS, ff_backward, 0)
    for k in list(range(38)) + [R_KV + 7 * j + 6 for j in range(4)]:
        rights[k, pl.ds(192, 64), :] = jnp.zeros((64, COLS), BF16)
    for k in range(4):
        rights[R_OUT + k, pl.ds(0, ROWS_ALL), :] = ffin[:, pl.ds(COLS * k, COLS)]
    row = lax.broadcasted_iota(jnp.int32, (256, COLS), 0)
    col = lax.broadcasted_iota(jnp.int32, (256, COLS), 1)
    rights[R_SMALL] = jnp.where(((row == col) & (row < 6)) | ((row == col + 6) & (row >= 6) & (row < 12)), 1.0, 0.0).astype(BF16)

    normed, inverse = normed_rows(x1s[...])
    back, gain_sum, bias_sum = norm_back(accs[...], normed, inverse, gains[0, 2:3, :])
    sums[pl.ds(2, 1), :] = gain_sum
    sums[pl.ds(5, 1), :] = bias_sum
    grad_x1 = gys[...] + back
    gys[...] = grad_x1
    grad_attn = grad_x1.astype(BF16)
    for k in range(4):
        rights[R_ATT + k, pl.ds(0, ROWS_ALL), :] = column(grad_attn, k)
    gatt[...] = mm_nt(grad_attn, wo[0]).astype(BF16)

    def attend_back(v, carry):
        rows = pl.ds(pl.multiple_of(v * 64, 64), 64)
        for g in range(2):
            cols = pl.ds(COLS * g, COLS)
            q_stack = head_stack(qs[rows, cols])
            g_stack = head_stack(gatt[rows, cols])
            widths = (256, 256, 128)
            probs = [own1[(v * 2 + g) * 3 + n, :, pl.ds(0, widths[n])] for n in range(3)]
            weighted = [p * mm_nt(g_stack, values) for p, values in zip(probs, keyvals_of(v, 2 + g))]
            whole = jnp.sum(weighted[0] + weighted[1], -1, keepdims=True) + jnp.sum(weighted[2], -1, keepdims=True)
            grad_s = [(w - p * whole).astype(BF16) for w, p in zip(weighted, probs)]
            grad_q = sum(mm(s, k) for s, k in zip(grad_s, keyvals_of(v, g)))
            rights[R_QUERY + g, rows, :] = head_merge(grad_q).astype(BF16)
            for base, factors, stack in (
                (R_KV + 7 * g, grad_s, q_stack),
                (R_KV + 14 + 7 * g, [p.astype(BF16) for p in probs], g_stack),
            ):
                rights[base + 2 * v] = mm_tn(factors[0], stack).astype(BF16)
                rights[base + 2 * v + 1] = mm_tn(factors[1], stack).astype(BF16)
                rights[base + 6, rows, :] = mm_tn(factors[2], stack)[:64].astype(BF16)
        return carry

    lax.fori_loop(0, 3, attend_back, 0)

    grad_in = sum(mm_nt(rights[R_QUERY + g, pl.ds(0, ROWS_ALL), :], wq[0, :, pl.ds(COLS * g, COLS)]) for g in range(2))
    grad_in = grad_in * 0.125
    for k in range(4):
        grad_in += mm_nt(rights[R_KV + 6 + 7 * k, pl.ds(0, ROWS_ALL), :], wkv[0, :, pl.ds(COLS * k, COLS)])
    normed, inverse = normed_rows(xs[...])
    back, gain_sum, bias_sum = norm_back(grad_in, normed, inverse, gains[0, 1:2, :])
    sums[pl.ds(1, 1), :] = gain_sum
    sums[pl.ds(4, 1), :] = bias_sum
    accs[...] = gys[...] + back

    @pl.when(section == 1)
    def _():
        to_other(accs, gys, g_sem).start()
        turn_forward()

    @pl.when(section == 0)
    def _():
        sent[...] = accs[:, pl.ds(512, 512)]
        to_other(sent, latents_grad, l_sem).start()
        latents_grad[...] = accs[:, pl.ds(0, 512)]

    def use_out(s, piece):
        for k in range(4):
            rights[R_OUT + 4 * s + k, pl.ds(0, ROWS_ALL), :] = piece[k].astype(BF16)

    taken(G_OUT, use_out)

    def turn_pre():
        for k in range(4):
            rights[R_PRE + k, pl.ds(0, ROWS_ALL), :] = pres[4 * coords[A] + k].astype(BF16)

        def use_pre(s, piece):
            for k in range(4):
                rights[R_PRE + 4 * s + k, pl.ds(0, ROWS_ALL), :] = piece[k].astype(BF16)

        taken(G_PRE, use_pre)

    def media_away(i):
        return pltpu.make_async_remote_copy(
            src_ref=m_stage.at[i % 2, pl.ds(2 * other, 2)], dst_ref=m_got.at[i], send_sem=m_send.at[i], recv_sem=m_recv.at[i],
            device_id={"section": other}, device_id_type=MESH,
        )

    def media_home(i):
        return pltpu.make_async_copy(m_stage.at[i % 2, pl.ds(2 * section, 2)], m_own.at[i], m_local.at[i])

    def media_back(i):
        if i < 5:
            media_rows(i + 1).start()
        media_rows(i).wait()
        if i >= 2:
            media_away(i - 2).wait_send()
            media_home(i - 2).wait()
        normed, inverse = normed_rows(m_buf[i % 2].astype(F32))
        media_in = normed * gains[0, 0:1, :] + biases[0, 0:1, :]
        grad_media = mm_nt(rights[R_KV + i], wkv[0, :, pl.ds(0, COLS)])
        for k in range(1, 4):
            grad_media += mm_nt(rights[R_KV + 7 * k + i], wkv[0, :, pl.ds(COLS * k, COLS)])
        back, gain_sum, bias_sum = norm_back(grad_media, normed, inverse, gains[0, 0:1, :])
        if i == 0:
            sums[pl.ds(0, 1), :] = gain_sum
            sums[pl.ds(3, 1), :] = bias_sum
        else:
            sums[pl.ds(0, 1), :] += gain_sum
            sums[pl.ds(3, 1), :] += bias_sum
        for k in range(4):
            m_stage[i % 2, k] = column(back, k)
        media_away(i).start()
        media_home(i).start()
        for k in range(4):
            lefts[i, k] = turned(column(media_in, k).astype(BF16).astype(F32))

    def small_left():
        total = sums[pl.ds(0, 6), :]
        high = total.astype(BF16).astype(F32)
        block = jnp.concatenate([high, total - high, jnp.zeros((244, 1024), F32)], 0)
        for k in range(4):
            lefts[L_SMALL, k] = turned(column(block, k))

    def factors(what, which):
        if what == "up":
            return [(L_FF + s, R_PRE + 4 * s + which) for s in range(4)]
        if what == "down":
            return [(L_ACT + s, R_OUT + 4 * s + which) for s in range(4)]
        if what == "out":
            return [(L_ATT + s, R_ATT + 2 * which + s) for s in range(2)]
        if what == "query":
            return [(L_LATENT, R_QUERY + which)]
        if what == "small":
            return [(L_SMALL, R_SMALL)]
        return [(k, R_KV + 7 * which + k) for k in range(7)]

    own = (own1, own2, own3)

    def spot(lane, group):
        return (lane * 3 + group % 3) * 4

    def pieces(what, axes, i, b, c):
        if what == "down":
            block = {A: by_section(i, b), C: by_section(b, i)}
            return block[axes[0]], block[axes[1]] * 4 + c
        block = {A: by_section(i, c), B: by_section(b, i), C: by_section(c, b)}
        second, third = {A: (B, C), B: (C, A), C: (B, A)}[axes[0]]
        return block[axes[0]], block[second] * 4 + block[third]

    def terms(lane, group):
        what, which, axes = PLAN[lane][group]
        base = spot(lane, group)

        def block(i, carry):
            total = sum(mm(lefts[a, i], rights[b]) for a, b in factors(what, which))
            for b in range(4):
                for c in range(4):
                    first, rest = pieces(what, axes, i, b, c)
                    rows = pl.ds(pl.multiple_of(rest * 16, 16), 16)
                    own1[base + first, rows, :] = total[(b * 4 + c) * 16 : (b * 4 + c) * 16 + 16]
            return carry

        lax.fori_loop(0, 4, block, 0)

    def ring_copy(lane, group, stage, step, way):
        axis = PLAN[lane][group][2][stage]
        half = RING_ROWS[stage] // 2
        shift = 1 if way == 0 else 3
        place = own[stage].at[spot(lane, group) + at(axis, 2 if step == 0 else shift)]
        if stage == 0:
            turn = group % 2 if step == 2 else group % 3
            source = place.at[pl.ds((1 - way if step == 1 else way) * half, half)]
            target = (far1, mine1, summed1)[step].at[lane, way, turn]
        else:
            turn = group % 2
            source = place.at[pl.ds(way * half, half)] if step == 0 else place
            target = (far2, near2)[step].at[lane, way, turn]
        sem = (((lane * 2 + stage) * 3 + step) * 2 + way) * 3 + turn
        return pltpu.make_async_remote_copy(
            src_ref=source, dst_ref=target, send_sem=t_send.at[sem], recv_sem=t_recv.at[sem],
            device_id={"dp": peer(axis, shift)}, device_id_type=MESH,
        )

    def last_turn(lane, group):
        return sum(1 for g in range(group) if runs(lane, g, 2)) % 3

    def last_copy(lane, group, shift):
        axis = PLAN[lane][group][2][2]
        sem = (lane * 3 + last_turn(lane, group)) * 3 + shift - 1
        return pltpu.make_async_remote_copy(
            src_ref=own3.at[spot(lane, group) + at(axis, shift)], dst_ref=last.at[lane, last_turn(lane, group), shift - 1],
            send_sem=z_send.at[sem], recv_sem=z_recv.at[sem],
            device_id={"dp": peer(axis, shift)}, device_id_type=MESH,
        )

    def runs(lane, group, stage):
        return 0 <= group < GROUPS and PLAN[lane][group] is not None and stage < len(PLAN[lane][group][2])

    def up_copy(shift):
        rows = pl.ds(pl.multiple_of(16 * at(A, shift), 16), 16)
        return pltpu.make_async_remote_copy(
            src_ref=up_sum.at[rows, :], dst_ref=up_got.at[shift - 1], send_sem=u_send.at[shift - 1], recv_sem=u_recv.at[shift - 1],
            device_id={"dp": peer(A, shift)}, device_id_type=MESH,
        )

    def finish(what, which, total):
        cols = pl.ds(COLS * which, COLS)
        if what == "up":
            up_sum[:, cols] = total
        elif what == "down":
            out_down[:, cols] = total
        elif what == "query":
            out_query[:, cols] = total * 0.125
        elif what == "keyval":
            out_keyval[:, cols] = total
        elif what == "out":
            out_out[:, pl.ds(512 * which, COLS)] = total[:8]
            out_out[:, pl.ds(512 * which + COLS, COLS)] = total[8:]
        else:
            out_small[...] = total

    for k in range(4):
        lefts[L_LATENT, k] = turned(lin[:, pl.ds(COLS * k, COLS)].astype(F32))
    media_rows(0).start()
    ups = 0
    for t in range(TICKS):
        for lane in range(3):
            if runs(lane, t, 0):
                terms(lane, t)
                for way in range(2):
                    ring_copy(lane, t, 0, 0, way).start()
        if t == 0:
            media_back(0)
            turn_pre()
            media_back(1)
        if t == 1:
            media_back(2)
            media_back(3)
        if t == 2:
            media_back(4)
            media_back(5)
            small_left()
        for lane in range(3):
            for stage in range(2):
                half = RING_ROWS[stage] // 2
                group = t - 1 - 2 * stage
                if runs(lane, group, stage):
                    axis = PLAN[lane][group][2][stage]
                    for way in range(2):
                        ring_copy(lane, group, stage, 0, way).wait()
                        arrived = far1[lane, way, group % 3] if stage == 0 else far2[lane, way, group % 2]
                        own[stage][spot(lane, group) + at(axis, 1 if way == 0 else 3), pl.ds(way * half, half), :] += arrived
                group = t - 2 - 2 * stage
                if runs(lane, group, stage):
                    what, which, axes = PLAN[lane][group]
                    for way in range(2):
                        ring_copy(lane, group, stage, 1, way).wait()
                        if stage == 0:
                            ring_copy(lane, group, stage, 2, way).wait()
                    mine = spot(lane, group) + at(axes[stage], 0)
                    rows = RING_ROWS[stage + 1]
                    if stage == 0:
                        three, two = group % 3, group % 2
                        total = [
                            own1[mine, pl.ds(0, 128), :] + summed1[lane, 0, two] + mine1[lane, 1, three],
                            own1[mine, pl.ds(128, 128), :] + mine1[lane, 0, three] + summed1[lane, 1, two],
                        ]
                        for k in range(4):
                            own2[spot(lane, group) + k] = total[k // 2][rows * (k % 2) : rows * (k % 2) + rows]
                    else:
                        total = own2[mine] + near2[lane, 0, group % 2] + near2[lane, 1, group % 2]
                        if len(axes) == 3:
                            for k in range(4):
                                own3[spot(lane, group) + k] = total[rows * k : rows * k + rows]
                        else:
                            finish(what, which, total)
                            if what == "up":
                                ups += 1
            group = t - 5
            if runs(lane, group, 2):
                what, which, axes = PLAN[lane][group]
                total = own3[spot(lane, group) + at(axes[2], 0)]
                for shift in (1, 2, 3):
                    last_copy(lane, group, shift).wait()
                    total += last[lane, last_turn(lane, group), shift - 1]
                finish(what, which, total)
        for lane in range(3):
            for way in range(2):
                if runs(lane, t - 1, 0):
                    ring_copy(lane, t - 1, 0, 2, way).start()
                if runs(lane, t - 2, 1):
                    ring_copy(lane, t - 2, 1, 0, way).start()
                if runs(lane, t - 3, 1):
                    ring_copy(lane, t - 3, 1, 1, way).start()
            if runs(lane, t - 4, 2):
                for shift in (1, 2, 3):
                    last_copy(lane, t - 4, shift).start()
            for way in range(2):
                if runs(lane, t, 0):
                    ring_copy(lane, t, 0, 1, way).start()
        if ups == 4:
            ups = 0
            for shift in (1, 2, 3):
                up_copy(shift).start()

    for s in range(4):
        part = up_sum[pl.ds(pl.multiple_of(16 * coords[A], 16), 16), :] if s == 0 else None
        if s > 0:
            up_copy(s).wait()
            part = up_got[s - 1]
        cols = pl.ds(pl.multiple_of(1024 * at(A, 4 - s), 1024), 1024)
        out_up[:, cols] = part

    for i in (4, 5):
        media_away(i).wait_send()
        media_home(i).wait()
    for i in range(6):
        media_away(i).wait_recv()

    @pl.when(section == 0)
    def _():
        to_other(sent, resampled, r_sem).wait_recv()
        to_other(sent, latents_grad, l_sem).wait_send()

    @pl.when(section == 1)
    def _():
        to_other(sent, resampled, r_sem).wait_send()
        to_other(accs, gys, g_sem).wait_send()
        to_other(sent, latents_grad, l_sem).wait_recv()


def run_resampler(latents, media, frame_count, gains, biases, w_query, w_keyval, w_out, w_up, w_down, cotangent):
    vmem = pl.BlockSpec(memory_space=pltpu.VMEM)
    hbm = pl.BlockSpec(memory_space=pl.ANY)

    def sds(*shape):
        return jax.ShapeDtypeStruct(shape, F32)

    dma = pltpu.SemaphoreType.DMA
    return pl.pallas_call(
        resampler_kernel,
        out_shape=[
            sds(192, 512), sds(192, 512), sds(16, 256), sds(16, 512), sds(16, 1024), sds(8, 1024), sds(16, 4096), sds(64, 1024),
            sds(6, 2, 256, 256), sds(6, 2, 256, 256), sds(4, 3, 4, 192, 256),
        ],
        in_specs=[hbm, hbm, pl.BlockSpec(memory_space=pltpu.SMEM)] + [vmem] * 2 + [hbm] * 6,
        out_specs=[vmem] * 8 + [hbm] * 3,
        scratch_shapes=[
            pltpu.VMEM((1, 1024, 512), BF16),
            pltpu.VMEM((1, 1024, 1024), BF16),
            pltpu.VMEM((1, 512, 1024), BF16),
            pltpu.VMEM((192, 1024), F32),
            pltpu.VMEM((192, 1024), F32),
            pltpu.VMEM((192, 1024), F32),
            pltpu.VMEM((192, 1024), F32),
            pltpu.VMEM((192, 1024), BF16),
            pltpu.VMEM((192, 1024), BF16),
            pltpu.VMEM((192, 512), BF16),
            pltpu.VMEM((192, 512), BF16),
            pltpu.VMEM((192, 512), BF16),
            pltpu.VMEM((16, 192, 256), F32),
            pltpu.VMEM((8, 1024), F32),
            pltpu.VMEM((192, 512), F32),
            pltpu.VMEM((2, 4, 256, 256), F32),
            pltpu.VMEM((2, 256, 1024), BF16),
            pltpu.VMEM((DEEP, 512, 1024), BF16),
            pltpu.VMEM((2, 4, 192, 256), F32),
            pltpu.VMEM((18, 4, 256, 256), BF16),
            pltpu.VMEM((67, 256, 256), BF16),
        ]
        + [pltpu.VMEM((36, r, COLS), F32) for r in RING_ROWS]
        + [
            pltpu.VMEM((3, 2, 3, 128, COLS), F32),
            pltpu.VMEM((3, 2, 2, 32, COLS), F32),
            pltpu.VMEM((3, 2, 3, 128, COLS), F32),
            pltpu.VMEM((3, 2, 2, 128, COLS), F32),
            pltpu.VMEM((3, 2, 2, 64, COLS), F32),
            pltpu.VMEM((3, 3, 3, 16, COLS), F32),
            pltpu.VMEM((64, 1024), F32),
            pltpu.VMEM((3, 16, 1024), F32),
            dma((3,)), dma((3, 4)), dma((2,)), dma((2,)), dma((2,)), dma((2,)), dma((2,)), dma((6,)), dma((6,)), dma((6,)),
            dma((4, 3)), dma((4, 3)), dma((2,)), dma((108,)), dma((108,)), dma((27,)), dma((27,)), dma((3,)), dma((3,)),
        ],
        compiler_params=pltpu.CompilerParams(collective_id=1, has_side_effects=True, vmem_limit_bytes=VMEM_BYTES),
        name="resampler",
    )(latents, media, frame_count, gains, biases, w_query, w_keyval, w_out, w_up, w_down, cotangent)


def results_kernel(mine, theirs, *refs):
    given, made = refs[:8], refs[8:]
    total = mine[0] + theirs[0]
    made[0][:, pl.ds(0, COLS)] = total[0]
    made[0][:, pl.ds(COLS, COLS)] = total[1]

    @pl.when(pl.program_id(0) == 0)
    def _():
        for source, target in zip(given[1:], made[3:]):
            target[...] = source[...]
        columns = given[0][...].T
        made[1][0] = columns[:3]
        made[2][0] = columns[3:6]


def results(mine, theirs, small, resampled, latents_grad, query, keyval, out, up, down):
    rest = [resampled, latents_grad, query, keyval, out, up, down]
    whole = [pl.BlockSpec(a.shape, lambda i: (0, 0)) for a in rest]

    def sds(*shape):
        return jax.ShapeDtypeStruct(shape, F32)

    part = pl.BlockSpec((1, 2, COLS, COLS), lambda i: (i, 0, 0, 0))
    norms = pl.BlockSpec((1, 3, 16), lambda i: (0, 0, 0))
    return pl.pallas_call(
        results_kernel,
        grid=(6,),
        out_shape=[sds(1536, 512), sds(1, 3, 16), sds(1, 3, 16)] + [sds(*a.shape) for a in rest],
        in_specs=[part, part, pl.BlockSpec((16, COLS), lambda i: (0, 0))] + whole,
        out_specs=[pl.BlockSpec((COLS, 512), lambda i: (i, 0)), norms, norms] + whole,
        compiler_params=pltpu.CompilerParams(vmem_limit_bytes=32 * 2**20),
        name="results",
    )(mine, theirs, small, *rest)


def body(
    latents_in, media, frame_count, gains, biases, w_query, w_keyval, w_out, w_up, w_down, cotangent
):
    resampled, latents_grad, small, query, keyval, out, up, down, mine, theirs, _ = run_resampler(
        latents_in.reshape(192, 1024), media.reshape(1536, 1024), frame_count, gains, biases,
        w_query, w_keyval, w_out, w_up.reshape(4, 256, 4096), w_down.reshape(4096, 1024), cotangent.reshape(192, 1024),
    )
    media_grad, gains_grad, biases_grad, resampled, latents_grad, query, keyval, out, up, down = results(
        mine, theirs, small, resampled, latents_grad, query, keyval, out, up, down
    )
    return (
        resampled.reshape(3, 1, 64, 512),
        latents_grad.reshape(3, 1, 64, 512),
        media_grad.reshape(3, 1, 512, 512),
        gains_grad,
        biases_grad,
        query[None],
        keyval[None],
        out[None],
        up[None],
        down[None],
    )


def solution(mesh):
    placed = (
        P(None, "dp", None, None),
        P(None, "dp", None, None),
        P(None, "dp"),
        P("section", None, None),
        P("section", None, None),
        P("section", None, None),
        P("section", None, None),
        P("section", None, None),
        P("section", None, None),
        P("section", None, None),
        P(None, "dp", None, None),
    )
    return jax.shard_map(
        body,
        mesh=mesh,
        in_specs=placed,
        out_specs=(
            P(None, "dp", None, "section"),
            P(None, "dp", None, "section"),
            P(None, "dp", None, "section"),
            P("section", None, "dp"),
            P("section", None, "dp"),
            P("section", "dp", None),
            P("section", "dp", None),
            P("section", "dp", None),
            P("section", "dp", None),
            P("section", "dp", None),
        ),
        check_vma=False,
    )
```

```python
import jax
import jax.numpy as jnp
from jax import lax
from jax.experimental import pallas as pl
from jax.experimental.pallas import tpu as pltpu
from jax.sharding import PartitionSpec as P

VMEM_BYTES = 63 * 2**20
MESH = pl.DeviceIdType.MESH
F32 = jnp.float32
BF16 = jnp.bfloat16
NORM_EPS = 1e-05
MASK_FILL = -1e30
ROOT_HALF = 0.7071067811865476
INV_ROOT_TAU = 0.3989422804014327
ROWS_ALL = 192
KEYS = 640
FF_STEPS = 8
RING_ROWS = (256, 64, 16)
COLS = 256
A, B, C = 0, 1, 2
FF_IN, ACT, G_OUT, G_PRE = 0, 1, 2, 3
L_LATENT, L_FF, L_ACT, L_ATT = 6, 8, 12, 16
R_PRE, R_OUT, R_ATT, R_QUERY, R_KV = 0, 16, 32, 36, 38
PLAN = (
    (
        ("down", 0, (A, C)),
        ("query", 0, (A, B, C)),
        ("query", 1, (A, B, C)),
        ("keyval", 0, (A, B, C)),
        ("keyval", 2, (A, B, C)),
        ("down", 1, (A, C)),
    ),
    (
        ("out", 0, (B, C, A)),
        ("out", 1, (B, C, A)),
        ("up", 0, (B, C)),
        ("keyval", 1, (B, C, A)),
        ("up", 1, (B, C)),
        None,
    ),
    (
        ("down", 2, (C, A)),
        ("down", 3, (C, A)),
        ("up", 2, (C, B)),
        ("up", 3, (C, B)),
        ("keyval", 3, (C, B, A)),
        None,
    ),
)
GROUPS = 6
TICKS = GROUPS + 4
WIDE = 4
DEEP = 3
WU_BASE = 34


def mm(left, right):
    return jnp.dot(left, right, preferred_element_type=F32)


def mm_nt(left, right):
    return lax.dot_general(left, right, (((1,), (1,)), ((), ())), preferred_element_type=F32)


def mm_tn(left, right):
    return lax.dot_general(left, right, (((0,), (0,)), ((), ())), preferred_element_type=F32)


def normed_rows(values):
    average = jnp.mean(values, -1, keepdims=True)
    centred = values - average
    inverse = lax.rsqrt(jnp.mean(centred * centred, -1, keepdims=True) + NORM_EPS)
    return centred * inverse, inverse


def norm_back(grad, normed, inverse, gain):
    scaled = grad * gain
    inner = jnp.mean(scaled, -1, keepdims=True)
    along = jnp.mean(scaled * normed, -1, keepdims=True)
    back = inverse * (scaled - inner - normed * along)
    return back, jnp.sum(grad * normed, 0, keepdims=True), jnp.sum(grad, 0, keepdims=True)


def turned(block):
    rows = block.shape[0]
    if rows < 256:
        block = jnp.concatenate([block, jnp.zeros((256 - rows, block.shape[1]), block.dtype)], 0)
    return block.T.astype(BF16)


def head_stack(block):
    lane = lax.broadcasted_iota(jnp.int32, (64, 256), 1) // 64
    return jnp.concatenate([jnp.where(lane == h, block, jnp.zeros_like(block)) for h in range(4)], 0)


def head_merge(block):
    lane = lax.broadcasted_iota(jnp.int32, (64, 256), 1) // 64
    return sum(jnp.where(lane == h, block[64 * h : 64 * h + 64], 0.0) for h in range(4))


def column(block, k):
    return block[:, COLS * k : COLS * k + COLS]


def resampler_kernel(
    latents, media, norms, w_query, w_keyval, w_out, w_up, w_down, cotangent,
    resampled, latents_grad, out_small, out_query, out_keyval, out_out, out_up, out_down, m_own, m_got, land,
    wq, wkv, wo, xs, x1s, gys, accs, lin, ffin, qs, att, gatt, pres, sums, sent, m_stage, m_buf, wd, gave,
    lefts, rights, own1, own2, own3, far1, far2, mine1, summed1, near2, last, up_sum, up_got, small_sum, small_got, columns,
    a_sem, w_sem, b_sem, x_sem, g_sem, r_sem, l_sem, m_send, m_recv, m_local, e_send, e_recv, c_sem, t_send, t_recv, z_send, z_recv, u_send, u_recv, s_send, s_recv,
):
    section = lax.axis_index("section")
    other = 1 - section
    me = lax.axis_index("dp")
    x, y, z = me // 16, (me // 4) % 4, me % 4

    def by_section(first, second):
        return first + section * (second - first)

    coords = (by_section(x, z), by_section(y, x), by_section(z, y))
    strides = (by_section(16, 1), by_section(4, 16), by_section(1, 4))

    def at(axis, shift):
        return (coords[axis] + shift) % 4

    def peer(axis, shift):
        return me + (at(axis, shift) - coords[axis]) * strides[axis]

    held = [pltpu.make_async_copy(*pair, a_sem.at[n]) for n, pair in enumerate(((w_keyval, wkv), (w_query, wq), (w_out, wo)))]
    for c in held:
        c.start()
    barrier = pltpu.get_barrier_semaphore()
    pl.semaphore_signal(barrier, inc=1, device_id={"section": other}, device_id_type=MESH)
    greeted = [(axis, shift) for axis in (A, B, C) for shift in (1, 2, 3)]
    for axis, shift in greeted:
        pl.semaphore_signal(barrier, inc=1, device_id={"dp": peer(axis, shift)}, device_id_type=MESH)
    pl.semaphore_wait(barrier, 1 + len(greeted))

    def to_other(source, target, sem):
        return pltpu.make_async_remote_copy(
            src_ref=source, dst_ref=target, send_sem=sem.at[0], recv_sem=sem.at[1],
            device_id={"section": other}, device_id_type=MESH,
        )

    def up_block(step):
        return WU_BASE + 8 * (step % WIDE)

    def weights(step):
        copies = [pltpu.make_async_copy(w_down.at[pl.ds(pl.multiple_of(step * 512, 512), 512), :], wd.at[step % DEEP], w_sem.at[2, step % DEEP])]
        for k in range(2):
            cols = pl.ds(pl.multiple_of(step * 512 + COLS * k, COLS), COLS)
            copies.append(
                pltpu.make_async_copy(w_up.at[:, :, cols], rights.at[pl.ds(up_block(step) + 4 * k, 4)], w_sem.at[k, step % WIDE])
            )
        return copies

    def fetch(step):
        for c in weights(step):
            c.start()

    def fetch_first():
        for step in range(DEEP - 1):
            fetch(step)

    def fetch_next(step):
        @pl.when(step + DEEP - 1 < FF_STEPS)
        def _():
            fetch(step + DEEP - 1)

    def fetched(step):
        for c in weights(step):
            c.wait()

    def media_rows(i):
        return pltpu.make_async_copy(
            media.at[pl.ds(pl.multiple_of(i * 256, 256), 256), :], m_buf.at[i % 2], b_sem.at[i % 2]
        )

    def exchange(kind, shift):
        axis = A if kind in (FF_IN, G_PRE) else B
        if kind == FF_IN:
            source = gave.at[0]
        elif kind == G_OUT:
            source = gave.at[1]
        elif kind == ACT:
            source = own1.at[pl.ds(18 + 4 * at(axis, shift), 4), pl.ds(0, ROWS_ALL), :]
        else:
            source = pres.at[pl.ds(4 * at(axis, shift), 4)]
        return pltpu.make_async_remote_copy(
            src_ref=source, dst_ref=land.at[kind, shift - 1], send_sem=e_send.at[kind, shift - 1], recv_sem=e_recv.at[kind, shift - 1],
            device_id={"dp": peer(axis, shift)}, device_id_type=MESH,
        )

    def give(kind):
        for shift in (1, 3, 2):
            exchange(kind, shift).start()

    def taken(kind, use, late=False):
        def held(s):
            if late:
                return own1.at[pl.ds(8 + 12 * (s % 2), 4), pl.ds(0, ROWS_ALL), :]
            return m_stage.at[s % 2, :, pl.ds(0, ROWS_ALL), :]

        def load(s):
            return pltpu.make_async_copy(land.at[kind, s], held(s), c_sem.at[s % 2])

        exchange(kind, 1).wait()
        load(0).start()
        for s in range(3):
            if s < 2:
                exchange(kind, s + 2).wait()
                load(s + 1).start()
            load(s).wait()
            use(s + 1, held(s))

    fetch_first()
    media_rows(0).start()

    def to_rows(ref, value):
        for k in range(4):
            ref[k] = column(value, k)

    @pl.when(section == 0)
    def _():
        given = pltpu.make_async_copy(latents, lin, c_sem.at[0])
        given.start()
        given.wait()
        xs[...] = lin[...].astype(F32)

    @pl.when(section == 1)
    def _():
        given = pltpu.make_async_copy(cotangent, lin, c_sem.at[0])
        given.start()
        given.wait()
        gys[...] = lin[...].astype(F32)
        to_rows(gave.at[1], lin[...].astype(F32))
        give(G_OUT)

    def media_block(i, carry):
        @pl.when(i < 5)
        def _():
            media_rows(i + 1).start()

        media_rows(i).wait()
        normed, _ = normed_rows(m_buf[i % 2].astype(F32))
        media_in = (normed * norms[0:1, :] + norms[3:4, :]).astype(BF16)
        keyval = mm(media_in, wkv[0]).astype(BF16)
        for j in range(4):
            lefts[i, j] = column(keyval, j)
        return carry

    held[0].wait()
    lax.fori_loop(0, 6, media_block, 0)
    held[1].wait()
    held[2].wait()
    @pl.when(section == 1)
    def _():
        to_other(accs, xs, x_sem).wait_recv()

    normed, _ = normed_rows(xs[...])
    lin[...] = (normed * norms[1:2, :] + norms[4:5, :]).astype(BF16)
    qs[...] = (mm(lin[...], wq[0]) * 0.125).astype(BF16)
    latent_kv = mm(lin[...], wkv[0]).astype(BF16)
    for v in range(3):
        for j in range(4):
            rows = pl.ds((v % 2) * 128, 64)
            lefts[6 + v // 2, j, rows, :] = latent_kv[64 * v : 64 * v + 64, COLS * j : COLS * j + COLS]
            lefts[6 + v // 2, j, pl.ds((v % 2) * 128 + 64, 64), :] = jnp.zeros((64, COLS), BF16)

    def keyvals_of(v, j):
        tail = pl.ds((v % 2) * 128, 128)
        return lefts[2 * v, j], lefts[2 * v + 1, j], lefts[6 + v // 2, j, tail, :]

    key = lax.broadcasted_iota(jnp.int32, (1, KEYS), 1).astype(F32)

    def attend(v):
        rows = pl.ds(v * 64, 64)
        valid = (key < norms[6:7, 256 * v : 256 * v + 1]) | ((key >= 512.0) & (key < 576.0))
        for g in range(2):
            cols = pl.ds(COLS * g, COLS)
            stacked = head_stack(qs[rows, cols])
            scores = [mm_nt(stacked, k) for k in keyvals_of(v, g)]
            scores = [
                jnp.where(valid[:, 256 * n : 256 * n + s.shape[1]], s, MASK_FILL) for n, s in enumerate(scores)
            ]
            top = jnp.max(jnp.maximum(scores[0], scores[1]), -1, keepdims=True)
            top = jnp.maximum(top, jnp.max(scores[2], -1, keepdims=True))
            raised = [jnp.exp(s - top) for s in scores]
            whole = jnp.sum(raised[0] + raised[1], -1, keepdims=True) + jnp.sum(raised[2], -1, keepdims=True)
            scale = 1.0 / whole
            mixed = jnp.zeros((256, COLS), F32)
            for n, (e, values) in enumerate(zip(raised, keyvals_of(v, 2 + g))):
                p = e * scale
                own1[(v * 2 + g) * 3 + n, :, pl.ds(0, p.shape[1])] = p
                mixed += mm(p.astype(BF16), values)
            att[rows, cols] = head_merge(mixed).astype(BF16)

    for v in range(3):
        attend(v)

    x1 = xs[...] + mm(att[...], wo[0])
    x1s[...] = x1
    accs[...] = x1
    normed, _ = normed_rows(x1)
    ffin[...] = (normed * norms[2:3, :] + norms[5:6, :]).astype(BF16)
    to_rows(gave.at[0], ffin[...].astype(F32))
    give(FF_IN)

    def ff_forward(j, carry):
        fetched(j)
        fetch_next(j)
        acts = []
        for k in range(2):
            base = up_block(j) + 4 * k
            pre = sum(mm(ffin[:, pl.ds(COLS * r, COLS)], rights[base + r]) for r in range(4))
            act = (pre * (0.5 * (1.0 + lax.erf(pre * ROOT_HALF)))).astype(BF16)
            pres[2 * j + k] = pre
            own1[18 + by_section(4 * (2 * (j % 2) + k) + j // 2, 2 * j + k), pl.ds(0, ROWS_ALL), :] = act.astype(F32)
            acts.append(act)
        accs[...] += mm(jnp.concatenate(acts, 1), wd[j % DEEP])
        return carry

    lax.fori_loop(0, FF_STEPS, ff_forward, 0)
    give(ACT)
    fetch_first()

    def turn_ff(late):
        for k in range(4):
            lefts[L_FF, k] = turned(gave[0, k])

        def use_ff(s, piece):
            for k in range(4):
                lefts[L_FF + s, k] = turned(piece[k])

        taken(FF_IN, use_ff, late)

    def turn_act():
        for k in range(4):
            lefts[L_ACT, k] = turned(own1[18 + 4 * coords[B] + k, pl.ds(0, ROWS_ALL), :])
        for i in range(4):
            part = jnp.concatenate([att[:, pl.ds(128 * i, 128)].astype(F32), jnp.zeros((64, 128), F32)], 0)
            part = part.T.reshape(16, 8, 256)
            none = jnp.zeros_like(part)
            lefts[L_ATT, i] = jnp.concatenate([part, none], 1).reshape(256, 256).astype(BF16)
            lefts[L_ATT + 1, i] = jnp.concatenate([none, part], 1).reshape(256, 256).astype(BF16)

        def use_act(s, piece):
            for k in range(4):
                lefts[L_ACT + s, k] = turned(piece[k])

        taken(ACT, use_act)

    @pl.when(section == 0)
    def _():
        to_other(accs, xs, x_sem).start()
        turn_ff(False)
        turn_act()
        to_other(accs, xs, x_sem).wait_send()
        to_other(accs, gys, g_sem).wait_recv()
        to_rows(gave.at[1], gys[...].astype(BF16).astype(F32))
        give(G_OUT)

    @pl.when(section == 1)
    def _():
        sent[...] = accs[:, pl.ds(0, 512)]
        to_other(sent, resampled, r_sem).start()
        resampled[...] = accs[:, pl.ds(512, 512)]

    ffin[...] = gys[...].astype(BF16)
    accs[...] = jnp.zeros((ROWS_ALL, 1024), F32)

    def ff_backward(j, carry):
        fetched(j)
        fetch_next(j)
        grad_act = mm_nt(ffin[...], wd[j % DEEP])
        halves = []
        for k in range(2):
            pre = pres[2 * j + k]
            slope = 0.5 * (1.0 + lax.erf(pre * ROOT_HALF)) + pre * jnp.exp(-0.5 * pre * pre) * INV_ROOT_TAU
            halves.append((column(grad_act, k) * slope).astype(BF16))
            pres[2 * j + k] = halves[k].astype(F32)
        base = up_block(j)
        for r in range(4):
            accs[:, pl.ds(COLS * r, COLS)] += mm_nt(halves[0], rights[base + r]) + mm_nt(halves[1], rights[base + 4 + r])
        quarter = j // 2
        shift = (quarter - coords[A] + 4) % 4

        @pl.when((j % 2 == 1) & (shift != 0))
        def _():
            exchange(G_PRE, shift).start()

        return carry

    lax.fori_loop(0, FF_STEPS, ff_backward, 0)
    for k in list(range(R_KV)) + [R_KV + 7 * j + 6 for j in range(4)]:
        rights[k, pl.ds(192, 64), :] = jnp.zeros((64, COLS), BF16)
    for k in range(4):
        rights[R_OUT + k, pl.ds(0, ROWS_ALL), :] = ffin[:, pl.ds(COLS * k, COLS)]
    normed, inverse = normed_rows(x1s[...])
    back, gain_sum, bias_sum = norm_back(accs[...], normed, inverse, norms[2:3, :])
    sums[pl.ds(6, 2), :] = jnp.zeros((2, 1024), F32)
    sums[pl.ds(2, 1), :] = gain_sum
    sums[pl.ds(5, 1), :] = bias_sum
    grad_x1 = gys[...] + back
    gys[...] = grad_x1
    grad_attn = grad_x1.astype(BF16)
    for k in range(4):
        rights[R_ATT + k, pl.ds(0, ROWS_ALL), :] = column(grad_attn, k)
    gatt[...] = mm_nt(grad_attn, wo[0]).astype(BF16)

    def attend_back(v):
        rows = pl.ds(v * 64, 64)
        for g in range(2):
            cols = pl.ds(COLS * g, COLS)
            q_stack = head_stack(qs[rows, cols])
            g_stack = head_stack(gatt[rows, cols])
            widths = (256, 256, 128)
            probs = [own1[(v * 2 + g) * 3 + n, :, pl.ds(0, widths[n])] for n in range(3)]
            weighted = [p * mm_nt(g_stack, values) for p, values in zip(probs, keyvals_of(v, 2 + g))]
            whole = jnp.sum(weighted[0] + weighted[1], -1, keepdims=True) + jnp.sum(weighted[2], -1, keepdims=True)
            grad_s = [(w - p * whole).astype(BF16) for w, p in zip(weighted, probs)]
            grad_q = sum(mm(s, k) for s, k in zip(grad_s, keyvals_of(v, g)))
            rights[R_QUERY + g, rows, :] = head_merge(grad_q).astype(BF16)
            for base, factors, stack in (
                (R_KV + 7 * g, grad_s, q_stack),
                (R_KV + 14 + 7 * g, [p.astype(BF16) for p in probs], g_stack),
            ):
                rights[base + 2 * v] = mm_tn(factors[0], stack).astype(BF16)
                rights[base + 2 * v + 1] = mm_tn(factors[1], stack).astype(BF16)
                rights[base + 6, rows, :] = mm_tn(factors[2], stack)[:64].astype(BF16)

    for v in range(3):
        attend_back(v)

    grad_in = sum(mm_nt(rights[R_QUERY + g, pl.ds(0, ROWS_ALL), :], wq[0, :, pl.ds(COLS * g, COLS)]) for g in range(2))
    grad_in = grad_in * 0.125
    for k in range(4):
        grad_in += mm_nt(rights[R_KV + 6 + 7 * k, pl.ds(0, ROWS_ALL), :], wkv[0, :, pl.ds(COLS * k, COLS)])
    normed, inverse = normed_rows(xs[...])
    back, gain_sum, bias_sum = norm_back(grad_in, normed, inverse, norms[1:2, :])
    sums[pl.ds(1, 1), :] = gain_sum
    sums[pl.ds(4, 1), :] = bias_sum
    accs[...] = gys[...] + back

    @pl.when(section == 1)
    def _():
        to_other(accs, gys, g_sem).start()
        turn_act()

    @pl.when(section == 0)
    def _():
        sent[...] = accs[:, pl.ds(512, 512)]
        to_other(sent, latents_grad, l_sem).start()
        latents_grad[...] = accs[:, pl.ds(0, 512)]

    def use_out(s, piece):
        for k in range(4):
            rights[R_OUT + 4 * s + k, pl.ds(0, ROWS_ALL), :] = piece[k].astype(BF16)

    taken(G_OUT, use_out)

    def turn_pre():
        for k in range(4):
            rights[R_PRE + k, pl.ds(0, ROWS_ALL), :] = pres[4 * coords[A] + k].astype(BF16)

        def use_pre(s, piece):
            for k in range(4):
                rights[R_PRE + 4 * s + k, pl.ds(0, ROWS_ALL), :] = piece[k].astype(BF16)

        taken(G_PRE, use_pre, True)

    def media_away(i):
        return pltpu.make_async_remote_copy(
            src_ref=m_stage.at[i % 2, pl.ds(2 * other, 2)], dst_ref=m_got.at[i], send_sem=m_send.at[i], recv_sem=m_recv.at[i],
            device_id={"section": other}, device_id_type=MESH,
        )

    def media_home(i):
        return pltpu.make_async_copy(m_stage.at[i % 2, pl.ds(2 * section, 2)], m_own.at[i], m_local.at[i])

    def media_back(i):
        if i < 5:
            media_rows(i + 1).start()
        media_rows(i).wait()
        if i >= 2:
            media_away(i - 2).wait_send()
            media_home(i - 2).wait()
        normed, inverse = normed_rows(m_buf[i % 2].astype(F32))
        media_in = normed * norms[0:1, :] + norms[3:4, :]
        grad_media = mm_nt(rights[R_KV + i], wkv[0, :, pl.ds(0, COLS)])
        for k in range(1, 4):
            grad_media += mm_nt(rights[R_KV + 7 * k + i], wkv[0, :, pl.ds(COLS * k, COLS)])
        back, gain_sum, bias_sum = norm_back(grad_media, normed, inverse, norms[0:1, :])
        if i == 0:
            sums[pl.ds(0, 1), :] = gain_sum
            sums[pl.ds(3, 1), :] = bias_sum
        else:
            sums[pl.ds(0, 1), :] += gain_sum
            sums[pl.ds(3, 1), :] += bias_sum
        for k in range(4):
            m_stage[i % 2, k] = column(back, k)
        media_away(i).start()
        media_home(i).start()
        for k in range(4):
            lefts[i, k] = turned(column(media_in, k).astype(BF16).astype(F32))

    places, steps = (x, y, z), (16, 4, 1)

    def small_copy(axis, shift):
        place = (places[axis] + shift) % 4
        source = sums.at[:, pl.ds(pl.multiple_of(COLS * place, COLS), COLS)] if axis == 0 else small_sum.at[axis - 1]
        return pltpu.make_async_remote_copy(
            src_ref=source, dst_ref=small_got.at[axis, shift - 1], send_sem=s_send.at[axis, shift - 1], recv_sem=s_recv.at[axis, shift - 1],
            device_id={"dp": me + (place - places[axis]) * steps[axis]}, device_id_type=MESH,
        )

    def small_give(axis):
        for shift in (1, 2, 3):
            small_copy(axis, shift).start()

    def small_take(axis):
        total = sums[:, pl.ds(pl.multiple_of(COLS * x, COLS), COLS)] if axis == 0 else small_sum[axis - 1]
        for shift in (1, 2, 3):
            small_copy(axis, shift).wait()
            total += small_got[axis, shift - 1]
        if axis < 2:
            small_sum[axis] = total
        else:
            columns[...] = jnp.concatenate([total, jnp.zeros((120, COLS), F32)], 0).T
            out_small[...] = columns[pl.ds(pl.multiple_of(16 * (4 * y + z), 16), 16), :]

    def factors(what, which):
        if what == "up":
            return [(L_FF + s, R_PRE + 4 * s + which) for s in range(4)]
        if what == "down":
            return [(L_ACT + s, R_OUT + 4 * s + which) for s in range(4)]
        if what == "out":
            return [(L_ATT + s, R_ATT + 2 * which + s) for s in range(2)]
        if what == "query":
            return [(L_LATENT, R_QUERY + which)]
        return [(k, R_KV + 7 * which + k) for k in range(7)]

    own = (own1, own2, own3)

    def spot(lane, group):
        return (lane * 3 + group % 3) * 4

    def pieces(what, axes, i, b, c):
        if what == "down":
            block = {A: by_section(i, b), C: by_section(b, i)}
            return block[axes[0]], block[axes[1]] * 4 + c
        block = {A: by_section(i, c), B: by_section(b, i), C: by_section(c, b)}
        second, third = {A: (B, C), B: (C, A), C: (B, A)}[axes[0]]
        return block[axes[0]], block[second] * 4 + block[third]

    def terms(lane, group):
        what, which, axes = PLAN[lane][group]
        base = spot(lane, group)

        def block(i, carry):
            total = sum(mm(lefts[a, i], rights[b]) for a, b in factors(what, which))
            for b in range(4):
                for c in range(4):
                    first, rest = pieces(what, axes, i, b, c)
                    rows = pl.ds(pl.multiple_of(rest * 16, 16), 16)
                    own1[base + first, rows, :] = total[(b * 4 + c) * 16 : (b * 4 + c) * 16 + 16]
            return carry

        lax.fori_loop(0, 4, block, 0)

    def ring_copy(lane, group, stage, step, way):
        axis = PLAN[lane][group][2][stage]
        half = RING_ROWS[stage] // 2
        shift = 1 if way == 0 else 3
        place = own[stage].at[spot(lane, group) + at(axis, 2 if step == 0 else shift)]
        if stage == 0:
            turn = group % 2 if step == 2 else group % 3
            source = place.at[pl.ds((1 - way if step == 1 else way) * half, half)]
            target = (far1, mine1, summed1)[step].at[lane, way, turn]
        else:
            turn = group % 2
            source = place.at[pl.ds(way * half, half)] if step == 0 else place
            target = (far2, near2)[step].at[lane, way, turn]
        sem = (((lane * 2 + stage) * 3 + step) * 2 + way) * 3 + turn
        return pltpu.make_async_remote_copy(
            src_ref=source, dst_ref=target, send_sem=t_send.at[sem], recv_sem=t_recv.at[sem],
            device_id={"dp": peer(axis, shift)}, device_id_type=MESH,
        )

    def last_turn(lane, group):
        return sum(1 for g in range(group) if runs(lane, g, 2)) % 3

    def last_copy(lane, group, shift):
        axis = PLAN[lane][group][2][2]
        sem = (lane * 3 + last_turn(lane, group)) * 3 + shift - 1
        return pltpu.make_async_remote_copy(
            src_ref=own3.at[spot(lane, group) + at(axis, shift)], dst_ref=last.at[lane, last_turn(lane, group), shift - 1],
            send_sem=z_send.at[sem], recv_sem=z_recv.at[sem],
            device_id={"dp": peer(axis, shift)}, device_id_type=MESH,
        )

    def runs(lane, group, stage):
        return 0 <= group < GROUPS and PLAN[lane][group] is not None and stage < len(PLAN[lane][group][2])

    def up_copy(shift):
        rows = pl.ds(pl.multiple_of(16 * at(A, shift), 16), 16)
        return pltpu.make_async_remote_copy(
            src_ref=up_sum.at[rows, :], dst_ref=up_got.at[shift - 1], send_sem=u_send.at[shift - 1], recv_sem=u_recv.at[shift - 1],
            device_id={"dp": peer(A, shift)}, device_id_type=MESH,
        )

    def finish(what, which, total):
        cols = pl.ds(COLS * which, COLS)
        if what == "up":
            up_sum[:, cols] = total
        elif what == "down":
            out_down[:, cols] = total
        elif what == "query":
            out_query[:, cols] = total * 0.125
        elif what == "keyval":
            out_keyval[:, cols] = total
        else:
            out_out[:, pl.ds(512 * which, COLS)] = total[:8]
            out_out[:, pl.ds(512 * which + COLS, COLS)] = total[8:]

    for k in range(4):
        lefts[L_LATENT, k] = turned(lin[:, pl.ds(COLS * k, COLS)].astype(F32))
    media_rows(0).start()
    ups = 0
    for t in range(TICKS):
        for lane in range(3):
            if runs(lane, t, 0):
                terms(lane, t)
                for way in range(2):
                    ring_copy(lane, t, 0, 0, way).start()
        if t == 0:
            media_back(0)
            media_back(1)
        if t == 1:
            media_back(2)
            media_back(3)

            @pl.when(section == 1)
            def _():
                turn_ff(True)

            turn_pre()
        if t == 2:
            media_back(4)
            media_back(5)
            small_give(0)
        if t in (3, 4, 5):
            small_take(t - 3)
            if t < 5:
                small_give(t - 2)
        for lane in range(3):
            for stage in range(2):
                half = RING_ROWS[stage] // 2
                group = t - 1 - 2 * stage
                if runs(lane, group, stage):
                    axis = PLAN[lane][group][2][stage]
                    for way in range(2):
                        ring_copy(lane, group, stage, 0, way).wait()
                        arrived = far1[lane, way, group % 3] if stage == 0 else far2[lane, way, group % 2]
                        own[stage][spot(lane, group) + at(axis, 1 if way == 0 else 3), pl.ds(way * half, half), :] += arrived
                group = t - 2 - 2 * stage
                if runs(lane, group, stage):
                    what, which, axes = PLAN[lane][group]
                    for way in range(2):
                        ring_copy(lane, group, stage, 1, way).wait()
                        if stage == 0:
                            ring_copy(lane, group, stage, 2, way).wait()
                    mine = spot(lane, group) + at(axes[stage], 0)
                    rows = RING_ROWS[stage + 1]
                    if stage == 0:
                        three, two = group % 3, group % 2
                        total = [
                            own1[mine, pl.ds(0, 128), :] + summed1[lane, 0, two] + mine1[lane, 1, three],
                            own1[mine, pl.ds(128, 128), :] + mine1[lane, 0, three] + summed1[lane, 1, two],
                        ]
                        for k in range(4):
                            own2[spot(lane, group) + k] = total[k // 2][rows * (k % 2) : rows * (k % 2) + rows]
                    else:
                        total = own2[mine] + near2[lane, 0, group % 2] + near2[lane, 1, group % 2]
                        if len(axes) == 3:
                            for k in range(4):
                                own3[spot(lane, group) + k] = total[rows * k : rows * k + rows]
                        else:
                            finish(what, which, total)
                            if what == "up":
                                ups += 1
            group = t - 5
            if runs(lane, group, 2):
                what, which, axes = PLAN[lane][group]
                total = own3[spot(lane, group) + at(axes[2], 0)]
                for shift in (1, 2, 3):
                    last_copy(lane, group, shift).wait()
                    total += last[lane, last_turn(lane, group), shift - 1]
                finish(what, which, total)
        for lane in range(3):
            for way in range(2):
                if runs(lane, t - 1, 0):
                    ring_copy(lane, t - 1, 0, 2, way).start()
                if runs(lane, t - 2, 1):
                    ring_copy(lane, t - 2, 1, 0, way).start()
                if runs(lane, t - 3, 1):
                    ring_copy(lane, t - 3, 1, 1, way).start()
            if runs(lane, t - 4, 2):
                for shift in (1, 2, 3):
                    last_copy(lane, t - 4, shift).start()
            for way in range(2):
                if runs(lane, t, 0):
                    ring_copy(lane, t, 0, 1, way).start()
        if ups == 4:
            ups = 0
            for shift in (1, 2, 3):
                up_copy(shift).start()

    for s in range(4):
        part = up_sum[pl.ds(pl.multiple_of(16 * coords[A], 16), 16), :] if s == 0 else None
        if s > 0:
            up_copy(s).wait()
            part = up_got[s - 1]
        cols = pl.ds(pl.multiple_of(1024 * at(A, 4 - s), 1024), 1024)
        out_up[:, cols] = part

    for i in (4, 5):
        media_away(i).wait_send()
        media_home(i).wait()
    for i in range(6):
        media_away(i).wait_recv()

    @pl.when(section == 0)
    def _():
        to_other(sent, resampled, r_sem).wait_recv()
        to_other(sent, latents_grad, l_sem).wait_send()

    @pl.when(section == 1)
    def _():
        to_other(sent, resampled, r_sem).wait_send()
        to_other(accs, gys, g_sem).wait_send()
        to_other(sent, latents_grad, l_sem).wait_recv()


def run_resampler(latents, media, norms, w_query, w_keyval, w_out, w_up, w_down, cotangent):
    vmem = pl.BlockSpec(memory_space=pltpu.VMEM)
    hbm = pl.BlockSpec(memory_space=pl.ANY)

    def sds(*shape):
        return jax.ShapeDtypeStruct(shape, F32)

    dma = pltpu.SemaphoreType.DMA
    return pl.pallas_call(
        resampler_kernel,
        out_shape=[
            sds(192, 512), sds(192, 512), sds(16, 128), sds(16, 512), sds(16, 1024), sds(8, 1024), sds(16, 4096), sds(64, 1024),
            sds(6, 2, 256, 256), sds(6, 2, 256, 256), sds(4, 3, 4, 192, 256),
        ],
        in_specs=[hbm, hbm, vmem] + [hbm] * 6,
        out_specs=[vmem] * 8 + [hbm] * 3,
        scratch_shapes=[
            pltpu.VMEM((1, 1024, 512), BF16),
            pltpu.VMEM((1, 1024, 1024), BF16),
            pltpu.VMEM((1, 512, 1024), BF16),
            pltpu.VMEM((192, 1024), F32),
            pltpu.VMEM((192, 1024), F32),
            pltpu.VMEM((192, 1024), F32),
            pltpu.VMEM((192, 1024), F32),
            pltpu.VMEM((192, 1024), BF16),
            pltpu.VMEM((192, 1024), BF16),
            pltpu.VMEM((192, 512), BF16),
            pltpu.VMEM((192, 512), BF16),
            pltpu.VMEM((192, 512), BF16),
            pltpu.VMEM((16, 192, 256), F32),
            pltpu.VMEM((8, 1024), F32),
            pltpu.VMEM((192, 512), F32),
            pltpu.VMEM((2, 4, 256, 256), F32),
            pltpu.VMEM((2, 256, 1024), BF16),
            pltpu.VMEM((DEEP, 512, 1024), BF16),
            pltpu.VMEM((2, 4, 192, 256), F32),
            pltpu.VMEM((18, 4, 256, 256), BF16),
            pltpu.VMEM((66, 256, 256), BF16),
        ]
        + [pltpu.VMEM((36, r, COLS), F32) for r in RING_ROWS]
        + [
            pltpu.VMEM((3, 2, 3, 128, COLS), F32),
            pltpu.VMEM((3, 2, 2, 32, COLS), F32),
            pltpu.VMEM((3, 2, 3, 128, COLS), F32),
            pltpu.VMEM((3, 2, 2, 128, COLS), F32),
            pltpu.VMEM((3, 2, 2, 64, COLS), F32),
            pltpu.VMEM((3, 3, 3, 16, COLS), F32),
            pltpu.VMEM((64, 1024), F32),
            pltpu.VMEM((3, 16, 1024), F32),
            pltpu.VMEM((2, 8, COLS), F32),
            pltpu.VMEM((3, 3, 8, COLS), F32),
            pltpu.VMEM((COLS, 128), F32),
            dma((3,)), dma((3, 4)), dma((2,)), dma((2,)), dma((2,)), dma((2,)), dma((2,)), dma((6,)), dma((6,)), dma((6,)),
            dma((4, 3)), dma((4, 3)), dma((2,)), dma((108,)), dma((108,)), dma((27,)), dma((27,)), dma((3,)), dma((3,)), dma((3, 3)), dma((3, 3)),
        ],
        compiler_params=pltpu.CompilerParams(collective_id=1, has_side_effects=True, vmem_limit_bytes=VMEM_BYTES),
        name="resampler",
    )(latents, media, norms, w_query, w_keyval, w_out, w_up, w_down, cotangent)


def results_kernel(mine, theirs, *refs):
    given, made = refs[:8], refs[8:]
    total = mine[0] + theirs[0]
    made[0][:, pl.ds(0, COLS)] = total[0]
    made[0][:, pl.ds(COLS, COLS)] = total[1]

    @pl.when(pl.program_id(0) == 0)
    def _():
        for source, target in zip(given[1:], made[3:]):
            target[...] = source[...]
        columns = given[0][...].T
        made[1][0] = columns[:3]
        made[2][0] = columns[3:6]


def results(mine, theirs, small, resampled, latents_grad, query, keyval, out, up, down):
    rest = [resampled, latents_grad, query, keyval, out, up, down]
    whole = [pl.BlockSpec(a.shape, lambda i: (0, 0)) for a in rest]

    def sds(*shape):
        return jax.ShapeDtypeStruct(shape, F32)

    part = pl.BlockSpec((1, 2, COLS, COLS), lambda i: (i, 0, 0, 0))
    norms = pl.BlockSpec((1, 3, 16), lambda i: (0, 0, 0))
    return pl.pallas_call(
        results_kernel,
        grid=(6,),
        out_shape=[sds(1536, 512), sds(1, 3, 16), sds(1, 3, 16)] + [sds(*a.shape) for a in rest],
        in_specs=[part, part, pl.BlockSpec((16, 128), lambda i: (0, 0))] + whole,
        out_specs=[pl.BlockSpec((COLS, 512), lambda i: (i, 0)), norms, norms] + whole,
        compiler_params=pltpu.CompilerParams(vmem_limit_bytes=VMEM_BYTES),
        name="results",
    )(mine, theirs, small, *rest)


def body(
    latents_in, media, frame_count, gains, biases, w_query, w_keyval, w_out, w_up, w_down, cotangent
):
    frames = jnp.broadcast_to(64.0 * frame_count.astype(F32)[:, :1], (3, COLS)).reshape(1, 768)
    norms = jnp.concatenate([gains[0], biases[0], jnp.pad(frames, ((0, 1), (0, 256)))], 0)
    resampled, latents_grad, small, query, keyval, out, up, down, mine, theirs, _ = run_resampler(
        latents_in.reshape(192, 1024), media.reshape(1536, 1024), norms,
        w_query, w_keyval, w_out, w_up.reshape(4, 256, 4096), w_down.reshape(4096, 1024), cotangent.reshape(192, 1024),
    )
    media_grad, gains_grad, biases_grad, resampled, latents_grad, query, keyval, out, up, down = results(
        mine, theirs, small, resampled, latents_grad, query, keyval, out, up, down
    )
    return (
        resampled.reshape(3, 1, 64, 512),
        latents_grad.reshape(3, 1, 64, 512),
        media_grad.reshape(3, 1, 512, 512),
        gains_grad,
        biases_grad,
        query[None],
        keyval[None],
        out[None],
        up[None],
        down[None],
    )


def solution(mesh):
    placed = (
        P(None, "dp", None, None),
        P(None, "dp", None, None),
        P(None, "dp"),
        P("section", None, None),
        P("section", None, None),
        P("section", None, None),
        P("section", None, None),
        P("section", None, None),
        P("section", None, None),
        P("section", None, None),
        P(None, "dp", None, None),
    )
    return jax.shard_map(
        body,
        mesh=mesh,
        in_specs=placed,
        out_specs=(
            P(None, "dp", None, "section"),
            P(None, "dp", None, "section"),
            P(None, "dp", None, "section"),
            P("section", None, "dp"),
            P("section", None, "dp"),
            P("section", "dp", None),
            P("section", "dp", None),
            P("section", "dp", None),
            P("section", "dp", None),
            P("section", "dp", None),
        ),
        check_vma=False,
    )
```

```python
import jax
import jax.numpy as jnp
from jax import lax
from jax.experimental import pallas as pl
from jax.experimental.pallas import tpu as pltpu
from jax.sharding import PartitionSpec as P

VMEM_BYTES = 63 * 2**20
MESH = pl.DeviceIdType.MESH
F32 = jnp.float32
BF16 = jnp.bfloat16
NORM_EPS = 1e-05
MASK_FILL = -1e30
ROOT_HALF = 0.7071067811865476
INV_ROOT_TAU = 0.3989422804014327
ROWS_ALL = 192
KEYS = 640
FF_STEPS = 8
RING_ROWS = (256, 64, 16)
COLS = 256
A, B, C = 0, 1, 2
FF_IN, ACT, G_OUT, G_PRE = 0, 1, 2, 3
L_LATENT, L_FF, L_ACT, L_ATT = 6, 8, 12, 16
R_PRE, R_OUT, R_ATT, R_QUERY, R_KV = 0, 16, 32, 36, 38
PLAN = (
    (
        ("query", 0, (A, B, C)),
        ("query", 1, (A, B, C)),
        ("down", 0, (A, C)),
        ("keyval", 0, (A, B, C)),
        ("keyval", 2, (A, B, C)),
        ("down", 1, (A, C)),
    ),
    (
        ("out", 0, (B, C, A)),
        None,
        ("up", 0, (B, C)),
        ("up", 1, (B, C)),
        ("keyval", 1, (B, C, A)),
        None,
    ),
    (
        ("out", 1, (C, B, A)),
        ("down", 2, (C, A)),
        ("up", 2, (C, B)),
        ("up", 3, (C, B)),
        ("keyval", 3, (C, B, A)),
        ("down", 3, (C, A)),
    ),
)
GROUPS = 6
TICKS = GROUPS + 3
STRAIGHT = 4
WIDE = 4
DEEP = 3
WU_BASE = 34


def mm(left, right):
    return jnp.dot(left, right, preferred_element_type=F32)


def mm_nt(left, right):
    return lax.dot_general(left, right, (((1,), (1,)), ((), ())), preferred_element_type=F32)


def mm_tn(left, right):
    return lax.dot_general(left, right, (((0,), (0,)), ((), ())), preferred_element_type=F32)


def normed_rows(values):
    average = jnp.mean(values, -1, keepdims=True)
    centred = values - average
    inverse = lax.rsqrt(jnp.mean(centred * centred, -1, keepdims=True) + NORM_EPS)
    return centred * inverse, inverse


def norm_back(grad, normed, inverse, gain):
    scaled = grad * gain
    inner = jnp.mean(scaled, -1, keepdims=True)
    along = jnp.mean(scaled * normed, -1, keepdims=True)
    back = inverse * (scaled - inner - normed * along)
    return back, jnp.sum(grad * normed, 0, keepdims=True), jnp.sum(grad, 0, keepdims=True)


def turned(block):
    rows = block.shape[0]
    if rows < 256:
        block = jnp.concatenate([block, jnp.zeros((256 - rows, block.shape[1]), block.dtype)], 0)
    return block.T.astype(BF16)


def head_stack(block):
    lane = lax.broadcasted_iota(jnp.int32, (64, 256), 1) // 64
    return jnp.concatenate([jnp.where(lane == h, block, jnp.zeros_like(block)) for h in range(4)], 0)


def head_merge(block):
    lane = lax.broadcasted_iota(jnp.int32, (64, 256), 1) // 64
    return sum(jnp.where(lane == h, block[64 * h : 64 * h + 64], 0.0) for h in range(4))


def column(block, k):
    return block[:, COLS * k : COLS * k + COLS]


def resampler_kernel(
    latents, media, norms, w_query, w_keyval, w_out, w_up, w_down, cotangent,
    resampled, latents_grad, out_small, out_query, out_keyval, out_out, out_up, out_down, m_sum, m_own, m_got, land,
    wq, wkv, wo, xs, x1s, gys, accs, lin, ffin, qs, att, gatt, pres, sums, sent, m_stage, m_buf, wd, gave,
    lefts, rights, own1, own2, own3, far1, far2, mine1, summed1, near2, last, straight, up_sum, up_got, small_sum, small_got, columns,
    a_sem, w_sem, b_sem, x_sem, g_sem, r_sem, l_sem, m_send, m_recv, m_local, e_send, e_recv, c_sem, t_send, t_recv, z_send, z_recv, d_send, d_recv, u_send, u_recv, s_send, s_recv,
):
    section = lax.axis_index("section")
    other = 1 - section
    me = lax.axis_index("dp")
    x, y, z = me // 16, (me // 4) % 4, me % 4

    def by_section(first, second):
        return first + section * (second - first)

    coords = (by_section(x, z), by_section(y, x), by_section(z, y))
    strides = (by_section(16, 1), by_section(4, 16), by_section(1, 4))

    def at(axis, shift):
        return (coords[axis] + shift) % 4

    def peer(axis, shift):
        return me + (at(axis, shift) - coords[axis]) * strides[axis]

    held = [pltpu.make_async_copy(*pair, a_sem.at[n]) for n, pair in enumerate(((w_keyval, wkv), (w_query, wq), (w_out, wo)))]
    for c in held:
        c.start()
    barrier = pltpu.get_barrier_semaphore()
    pl.semaphore_signal(barrier, inc=1, device_id={"section": other}, device_id_type=MESH)
    greeted = [(axis, shift) for axis in (A, B, C) for shift in (1, 2, 3)]
    for axis, shift in greeted:
        pl.semaphore_signal(barrier, inc=1, device_id={"dp": peer(axis, shift)}, device_id_type=MESH)

    pl.semaphore_wait(barrier, 1 + len(greeted))

    def to_other(source, target, sem):
        return pltpu.make_async_remote_copy(
            src_ref=source, dst_ref=target, send_sem=sem.at[0], recv_sem=sem.at[1],
            device_id={"section": other}, device_id_type=MESH,
        )

    def up_block(step):
        return WU_BASE + 8 * (step % WIDE)

    def down_rows(step):
        rows = pl.ds(pl.multiple_of(step * 512, 512), 512)
        return [pltpu.make_async_copy(w_down.at[rows, :], wd.at[step % DEEP], w_sem.at[2, step % DEEP])]

    def up_columns(step):
        copies = []
        for k in range(2):
            cols = pl.ds(pl.multiple_of(step * 512 + COLS * k, COLS), COLS)
            copies.append(
                pltpu.make_async_copy(w_up.at[:, :, cols], rights.at[pl.ds(up_block(step) + 4 * k, 4)], w_sem.at[k, step % WIDE])
            )
        return copies

    def fetch_first():
        for step in range(DEEP - 1):
            for c in down_rows(step) + up_columns(step):
                c.start()

    def fetch_next(step):
        @pl.when(step + DEEP - 1 < FF_STEPS)
        def _():
            for c in down_rows(step + DEEP - 1) + up_columns(step + DEEP - 1):
                c.start()

    def fetched(step):
        for c in down_rows(step) + up_columns(step):
            c.wait()

    def media_rows(i):
        return pltpu.make_async_copy(
            media.at[pl.ds(pl.multiple_of(i * 256, 256), 256), :], m_buf.at[i % 2], b_sem.at[i % 2]
        )

    def exchange(kind, shift):
        axis = A if kind in (FF_IN, G_PRE) else B
        if kind == FF_IN:
            source = gave.at[0]
        elif kind == G_OUT:
            source = gave.at[1]
        elif kind == ACT:
            source = own1.at[pl.ds(18 + 4 * at(axis, shift), 4), pl.ds(0, ROWS_ALL), :]
        else:
            source = pres.at[pl.ds(4 * at(axis, shift), 4)]
        return pltpu.make_async_remote_copy(
            src_ref=source, dst_ref=land.at[kind, shift - 1], send_sem=e_send.at[kind, shift - 1], recv_sem=e_recv.at[kind, shift - 1],
            device_id={"dp": peer(axis, shift)}, device_id_type=MESH,
        )

    def give(kind):
        for shift in (1, 3, 2):
            exchange(kind, shift).start()

    def taken(kind, use, late=False):
        def held(s):
            if late:
                return own1.at[pl.ds(24 + 4 * (s % 2), 4), pl.ds(0, ROWS_ALL), :]
            return m_stage.at[s % 2, :, pl.ds(0, ROWS_ALL), :]

        def load(s):
            return pltpu.make_async_copy(land.at[kind, s], held(s), c_sem.at[s % 2])

        exchange(kind, 1).wait()
        load(0).start()
        for s in range(3):
            if s < 2:
                exchange(kind, s + 2).wait()
                load(s + 1).start()
            load(s).wait()
            use(s + 1, held(s))

    fetch_first()
    media_rows(0).start()

    def to_rows(ref, value):
        for k in range(4):
            ref[k] = column(value, k)

    @pl.when(section == 0)
    def _():
        given = pltpu.make_async_copy(latents, lin, c_sem.at[0])
        given.start()
        given.wait()
        xs[...] = lin[...].astype(F32)

    @pl.when(section == 1)
    def _():
        given = pltpu.make_async_copy(cotangent, lin, c_sem.at[0])
        given.start()
        given.wait()
        gys[...] = lin[...].astype(F32)
        to_rows(gave.at[1], lin[...].astype(F32))
        give(G_OUT)

    def media_block(i, carry):
        @pl.when(i < 5)
        def _():
            media_rows(i + 1).start()

        media_rows(i).wait()
        normed, _ = normed_rows(m_buf[i % 2].astype(F32))
        media_in = (normed * norms[0:1, :] + norms[3:4, :]).astype(BF16)
        keyval = mm(media_in, wkv[0]).astype(BF16)
        for j in range(4):
            lefts[i, j] = column(keyval, j)
        return carry

    held[0].wait()
    lax.fori_loop(0, 6, media_block, 0)
    held[1].wait()
    held[2].wait()
    @pl.when(section == 1)
    def _():
        to_other(accs, xs, x_sem).wait_recv()

    normed, _ = normed_rows(xs[...])
    lin[...] = (normed * norms[1:2, :] + norms[4:5, :]).astype(BF16)
    qs[...] = (mm(lin[...], wq[0]) * 0.125).astype(BF16)
    latent_kv = mm(lin[...], wkv[0]).astype(BF16)
    for v in range(3):
        for j in range(4):
            rows = pl.ds((v % 2) * 128, 64)
            lefts[6 + v // 2, j, rows, :] = latent_kv[64 * v : 64 * v + 64, COLS * j : COLS * j + COLS]
            lefts[6 + v // 2, j, pl.ds((v % 2) * 128 + 64, 64), :] = jnp.zeros((64, COLS), BF16)

    def keyvals_of(v, j):
        tail = pl.ds((v % 2) * 128, 128)
        return lefts[2 * v, j], lefts[2 * v + 1, j], lefts[6 + v // 2, j, tail, :]

    key = lax.broadcasted_iota(jnp.int32, (1, KEYS), 1).astype(F32)

    def attend(v):
        rows = pl.ds(v * 64, 64)
        valid = (key < norms[6:7, 256 * v : 256 * v + 1]) | ((key >= 512.0) & (key < 576.0))
        for g in range(2):
            cols = pl.ds(COLS * g, COLS)
            stacked = head_stack(qs[rows, cols])
            scores = [mm_nt(stacked, k) for k in keyvals_of(v, g)]
            scores = [
                jnp.where(valid[:, 256 * n : 256 * n + s.shape[1]], s, MASK_FILL) for n, s in enumerate(scores)
            ]
            top = jnp.max(jnp.maximum(scores[0], scores[1]), -1, keepdims=True)
            top = jnp.maximum(top, jnp.max(scores[2], -1, keepdims=True))
            raised = [jnp.exp(s - top) for s in scores]
            whole = jnp.sum(raised[0] + raised[1], -1, keepdims=True) + jnp.sum(raised[2], -1, keepdims=True)
            scale = 1.0 / whole
            mixed = jnp.zeros((256, COLS), F32)
            for n, (e, values) in enumerate(zip(raised, keyvals_of(v, 2 + g))):
                p = e * scale
                own1[(v * 2 + g) * 3 + n, :, pl.ds(0, p.shape[1])] = p
                mixed += mm(p.astype(BF16), values)
            att[rows, cols] = head_merge(mixed).astype(BF16)

    for v in range(3):
        attend(v)

    x1 = xs[...] + mm(att[...], wo[0])
    x1s[...] = x1
    accs[...] = x1
    normed, _ = normed_rows(x1)
    ffin[...] = (normed * norms[2:3, :] + norms[5:6, :]).astype(BF16)
    to_rows(gave.at[0], ffin[...].astype(F32))
    give(FF_IN)

    def ff_forward(j, carry):
        fetched(j)
        fetch_next(j)
        acts = []
        for k in range(2):
            base = up_block(j) + 4 * k
            pre = sum(mm(ffin[:, pl.ds(COLS * r, COLS)], rights[base + r]) for r in range(4))
            act = (pre * (0.5 * (1.0 + lax.erf(pre * ROOT_HALF)))).astype(BF16)
            pres[2 * j + k] = pre
            own1[18 + by_section(4 * (2 * (j % 2) + k) + j // 2, 2 * j + k), pl.ds(0, ROWS_ALL), :] = act.astype(F32)
            acts.append(act)
        accs[...] += mm(jnp.concatenate(acts, 1), wd[j % DEEP])
        return carry

    lax.fori_loop(0, FF_STEPS, ff_forward, 0)
    give(ACT)
    fetch_first()

    def turn_ff(late):
        for k in range(4):
            lefts[L_FF, k] = turned(gave[0, k])

        def use_ff(s, piece):
            for k in range(4):
                lefts[L_FF + s, k] = turned(piece[k])

        taken(FF_IN, use_ff, late)

    def turn_att():
        for i in range(4):
            part = jnp.concatenate([att[:, pl.ds(128 * i, 128)].astype(F32), jnp.zeros((64, 128), F32)], 0)
            part = part.T.reshape(16, 8, 256)
            none = jnp.zeros_like(part)
            lefts[L_ATT, i] = jnp.concatenate([part, none], 1).reshape(256, 256).astype(BF16)
            lefts[L_ATT + 1, i] = jnp.concatenate([none, part], 1).reshape(256, 256).astype(BF16)

    def turn_act():
        for k in range(4):
            lefts[L_ACT, k] = turned(own1[18 + 4 * coords[B] + k, pl.ds(0, ROWS_ALL), :])
        def use_act(s, piece):
            for k in range(4):
                lefts[L_ACT + s, k] = turned(piece[k])

        taken(ACT, use_act)

    @pl.when(section == 0)
    def _():
        to_other(accs, xs, x_sem).start()
        turn_ff(False)
        turn_act()
        turn_att()
        to_other(accs, xs, x_sem).wait_send()
        to_other(accs, gys, g_sem).wait_recv()
        to_rows(gave.at[1], gys[...].astype(BF16).astype(F32))
        give(G_OUT)

    @pl.when(section == 1)
    def _():
        sent[...] = accs[:, pl.ds(0, 512)]
        to_other(sent, resampled, r_sem).start()
        resampled[...] = accs[:, pl.ds(512, 512)]

    ffin[...] = gys[...].astype(BF16)
    accs[...] = jnp.zeros((ROWS_ALL, 1024), F32)

    def ff_backward(j, carry):
        fetched(j)
        fetch_next(j)
        grad_act = mm_nt(ffin[...], wd[j % DEEP])
        halves = []
        for k in range(2):
            pre = pres[2 * j + k]
            slope = 0.5 * (1.0 + lax.erf(pre * ROOT_HALF)) + pre * jnp.exp(-0.5 * pre * pre) * INV_ROOT_TAU
            halves.append((column(grad_act, k) * slope).astype(BF16))
            pres[2 * j + k] = halves[k].astype(F32)
        base = up_block(j)
        for r in range(4):
            accs[:, pl.ds(COLS * r, COLS)] += mm_nt(halves[0], rights[base + r]) + mm_nt(halves[1], rights[base + 4 + r])
        quarter = j // 2
        shift = (quarter - coords[A] + 4) % 4

        @pl.when((j % 2 == 1) & (shift != 0))
        def _():
            exchange(G_PRE, shift).start()

        return carry

    lax.fori_loop(0, FF_STEPS, ff_backward, 0)
    for k in list(range(R_KV)) + [R_KV + 7 * j + 6 for j in range(4)]:
        rights[k, pl.ds(192, 64), :] = jnp.zeros((64, COLS), BF16)
    for k in range(4):
        rights[R_OUT + k, pl.ds(0, ROWS_ALL), :] = ffin[:, pl.ds(COLS * k, COLS)]
    normed, inverse = normed_rows(x1s[...])
    back, gain_sum, bias_sum = norm_back(accs[...], normed, inverse, norms[2:3, :])
    sums[pl.ds(6, 2), :] = jnp.zeros((2, 1024), F32)
    sums[pl.ds(2, 1), :] = gain_sum
    sums[pl.ds(5, 1), :] = bias_sum
    grad_x1 = gys[...] + back
    gys[...] = grad_x1
    grad_attn = grad_x1.astype(BF16)
    for k in range(4):
        rights[R_ATT + k, pl.ds(0, ROWS_ALL), :] = column(grad_attn, k)
    gatt[...] = mm_nt(grad_attn, wo[0]).astype(BF16)

    def attend_back(v):
        rows = pl.ds(v * 64, 64)
        for g in range(2):
            cols = pl.ds(COLS * g, COLS)
            q_stack = head_stack(qs[rows, cols])
            g_stack = head_stack(gatt[rows, cols])
            widths = (256, 256, 128)
            probs = [own1[(v * 2 + g) * 3 + n, :, pl.ds(0, widths[n])] for n in range(3)]
            weighted = [p * mm_nt(g_stack, values) for p, values in zip(probs, keyvals_of(v, 2 + g))]
            whole = jnp.sum(weighted[0] + weighted[1], -1, keepdims=True) + jnp.sum(weighted[2], -1, keepdims=True)
            grad_s = [(w - p * whole).astype(BF16) for w, p in zip(weighted, probs)]
            grad_q = sum(mm(s, k) for s, k in zip(grad_s, keyvals_of(v, g)))
            rights[R_QUERY + g, rows, :] = head_merge(grad_q).astype(BF16)
            for base, factors, stack in (
                (R_KV + 7 * g, grad_s, q_stack),
                (R_KV + 14 + 7 * g, [p.astype(BF16) for p in probs], g_stack),
            ):
                rights[base + 2 * v] = mm_tn(factors[0], stack).astype(BF16)
                rights[base + 2 * v + 1] = mm_tn(factors[1], stack).astype(BF16)
                rights[base + 6, rows, :] = mm_tn(factors[2], stack)[:64].astype(BF16)

    for v in range(3):
        attend_back(v)

    grad_in = sum(mm_nt(rights[R_QUERY + g, pl.ds(0, ROWS_ALL), :], wq[0, :, pl.ds(COLS * g, COLS)]) for g in range(2))
    grad_in = grad_in * 0.125
    for k in range(4):
        grad_in += mm_nt(rights[R_KV + 6 + 7 * k, pl.ds(0, ROWS_ALL), :], wkv[0, :, pl.ds(COLS * k, COLS)])
    normed, inverse = normed_rows(xs[...])
    back, gain_sum, bias_sum = norm_back(grad_in, normed, inverse, norms[1:2, :])
    sums[pl.ds(1, 1), :] = gain_sum
    sums[pl.ds(4, 1), :] = bias_sum
    accs[...] = gys[...] + back

    @pl.when(section == 1)
    def _():
        to_other(accs, gys, g_sem).start()

    @pl.when(section == 0)
    def _():
        sent[...] = accs[:, pl.ds(512, 512)]
        to_other(sent, latents_grad, l_sem).start()
        latents_grad[...] = accs[:, pl.ds(0, 512)]

    def use_out(s, piece):
        for k in range(4):
            rights[R_OUT + 4 * s + k, pl.ds(0, ROWS_ALL), :] = piece[k].astype(BF16)


    def turn_pre():
        for k in range(4):
            rights[R_PRE + k, pl.ds(0, ROWS_ALL), :] = pres[4 * coords[A] + k].astype(BF16)

        def use_pre(s, piece):
            for k in range(4):
                rights[R_PRE + 4 * s + k, pl.ds(0, ROWS_ALL), :] = piece[k].astype(BF16)

        taken(G_PRE, use_pre, True)

    def media_away(i):
        return pltpu.make_async_remote_copy(
            src_ref=m_stage.at[i % 2, pl.ds(2 * other, 2)], dst_ref=m_got.at[i], send_sem=m_send.at[i], recv_sem=m_recv.at[i],
            device_id={"section": other}, device_id_type=MESH,
        )

    def media_home(i):
        return pltpu.make_async_copy(m_stage.at[i % 2, pl.ds(2 * section, 2)], m_own.at[i], m_local.at[i])

    def media_back(i):
        if i < 5:
            media_rows(i + 1).start()
        media_rows(i).wait()
        if i >= 2:
            media_away(i - 2).wait_send()
            media_home(i - 2).wait()
        normed, inverse = normed_rows(m_buf[i % 2].astype(F32))
        media_in = normed * norms[0:1, :] + norms[3:4, :]
        grad_media = mm_nt(rights[R_KV + i], wkv[0, :, pl.ds(0, COLS)])
        for k in range(1, 4):
            grad_media += mm_nt(rights[R_KV + 7 * k + i], wkv[0, :, pl.ds(COLS * k, COLS)])
        back, gain_sum, bias_sum = norm_back(grad_media, normed, inverse, norms[0:1, :])
        if i == 0:
            sums[pl.ds(0, 1), :] = gain_sum
            sums[pl.ds(3, 1), :] = bias_sum
        else:
            sums[pl.ds(0, 1), :] += gain_sum
            sums[pl.ds(3, 1), :] += bias_sum
        for k in range(4):
            m_stage[i % 2, k] = column(back, k)
        media_away(i).start()
        media_home(i).start()
        for k in range(4):
            lefts[i, k] = turned(column(media_in, k).astype(BF16).astype(F32))

    def media_parts(i):
        return (
            pltpu.make_async_copy(m_own.at[i], m_stage.at[i % 2, pl.ds(0, 2)], m_local.at[i]),
            pltpu.make_async_copy(m_got.at[i], m_stage.at[i % 2, pl.ds(2, 2)], m_send.at[i]),
        )

    def media_done(i):
        return pltpu.make_async_copy(m_stage.at[i % 2, pl.ds(0, 2)], m_sum.at[i], m_local.at[i])

    def media_sum(first):
        for i in (first, first + 1):
            if i >= 2:
                media_done(i - 2).wait()
            media_away(i).wait_recv()
            for c in media_parts(i):
                c.start()
        for i in (first, first + 1):
            for c in media_parts(i):
                c.wait()
            for k in range(2):
                m_stage[i % 2, k] += m_stage[i % 2, 2 + k]
            media_done(i).start()

    places, steps = (x, y, z), (16, 4, 1)

    def small_copy(axis, shift):
        place = (places[axis] + shift) % 4
        source = sums.at[:, pl.ds(pl.multiple_of(COLS * place, COLS), COLS)] if axis == 0 else small_sum.at[axis - 1]
        return pltpu.make_async_remote_copy(
            src_ref=source, dst_ref=small_got.at[axis, shift - 1], send_sem=s_send.at[axis, shift - 1], recv_sem=s_recv.at[axis, shift - 1],
            device_id={"dp": me + (place - places[axis]) * steps[axis]}, device_id_type=MESH,
        )

    def small_give(axis):
        for shift in (1, 2, 3):
            small_copy(axis, shift).start()

    def small_take(axis):
        total = sums[:, pl.ds(pl.multiple_of(COLS * x, COLS), COLS)] if axis == 0 else small_sum[axis - 1]
        for shift in (1, 2, 3):
            small_copy(axis, shift).wait()
            total += small_got[axis, shift - 1]
        if axis < 2:
            small_sum[axis] = total
        else:
            columns[...] = jnp.concatenate([total, jnp.zeros((120, COLS), F32)], 0).T
            out_small[...] = columns[pl.ds(pl.multiple_of(16 * (4 * y + z), 16), 16), :]

    def factors(what, which):
        if what == "up":
            return [(L_FF + s, R_PRE + 4 * s + which) for s in range(4)]
        if what == "down":
            return [(L_ACT + s, R_OUT + 4 * s + which) for s in range(4)]
        if what == "out":
            return [(L_ATT + s, R_ATT + 2 * which + s) for s in range(2)]
        if what == "query":
            return [(L_LATENT, R_QUERY + which)]
        return [(k, R_KV + 7 * which + k) for k in range(7)]

    own = (own1, own2, own3)

    def spot(lane, group):
        return (group % 3 * 3 + lane) * 4

    def pieces(what, axes, i, b, c):
        if what == "down":
            block = {A: by_section(i, b), C: by_section(b, i)}
            return block[axes[0]], block[axes[1]] * 4 + c
        block = {A: by_section(i, c), B: by_section(b, i), C: by_section(c, b)}
        first, second, third = axes if len(axes) == 3 else axes + (A,)
        return block[first], block[second] * 4 + block[third]

    def terms(lane, group):
        what, which, axes = PLAN[lane][group]
        base = spot(lane, group)

        def block(i, carry):
            total = sum(mm(lefts[a, i], rights[b]) for a, b in factors(what, which))
            for b in range(4):
                for c in range(4):
                    first, rest = pieces(what, axes, i, b, c)
                    rows = pl.ds(pl.multiple_of(rest * 16, 16), 16)
                    own1[base + first, rows, :] = total[(b * 4 + c) * 16 : (b * 4 + c) * 16 + 16]
            return carry

        lax.fori_loop(0, 4, block, 0)

    def ring_copy(lane, group, stage, step, way):
        axis = PLAN[lane][group][2][stage]
        half = RING_ROWS[stage] // 2
        shift = 1 if way == 0 else 3
        place = own[stage].at[spot(lane, group) + at(axis, 2 if step == 0 else shift)]
        if stage == 0:
            turn = group % 2 if step == 2 else group % 3
            source = place.at[pl.ds((1 - way if step == 1 else way) * half, half)]
            target = (far1, mine1, summed1)[step].at[lane, way, turn]
        else:
            turn = group % 2
            source = place.at[pl.ds(way * half, half)] if step == 0 else place
            target = (far2, near2)[step].at[lane, way, turn]
        sem = (((lane * 2 + stage) * 3 + step) * 2 + way) * 3 + turn
        return pltpu.make_async_remote_copy(
            src_ref=source, dst_ref=target, send_sem=t_send.at[sem], recv_sem=t_recv.at[sem],
            device_id={"dp": peer(axis, shift)}, device_id_type=MESH,
        )

    def straight_copy(lane, group, shift):
        axis = PLAN[lane][group][2][1]
        sem = (lane * 2 + group - STRAIGHT) * 3 + shift - 1
        return pltpu.make_async_remote_copy(
            src_ref=own2.at[spot(lane, group) + at(axis, shift)], dst_ref=straight.at[lane, group - STRAIGHT, shift - 1],
            send_sem=d_send.at[sem], recv_sem=d_recv.at[sem],
            device_id={"dp": peer(axis, shift)}, device_id_type=MESH,
        )

    def last_turn(lane, group):
        return sum(1 for g in range(group) if runs(lane, g, 2)) % 3

    def last_copy(lane, group, shift):
        axis = PLAN[lane][group][2][2]
        sem = (lane * 3 + last_turn(lane, group)) * 3 + shift - 1
        return pltpu.make_async_remote_copy(
            src_ref=own3.at[spot(lane, group) + at(axis, shift)], dst_ref=last.at[lane, last_turn(lane, group), shift - 1],
            send_sem=z_send.at[sem], recv_sem=z_recv.at[sem],
            device_id={"dp": peer(axis, shift)}, device_id_type=MESH,
        )

    def runs(lane, group, stage):
        return 0 <= group < GROUPS and PLAN[lane][group] is not None and stage < len(PLAN[lane][group][2])

    def up_copy(shift):
        rows = pl.ds(pl.multiple_of(16 * at(A, shift), 16), 16)
        return pltpu.make_async_remote_copy(
            src_ref=up_sum.at[rows, :], dst_ref=up_got.at[shift - 1], send_sem=u_send.at[shift - 1], recv_sem=u_recv.at[shift - 1],
            device_id={"dp": peer(A, shift)}, device_id_type=MESH,
        )

    def finish(what, which, total):
        cols = pl.ds(COLS * which, COLS)
        if what == "up":
            up_sum[:, cols] = total
        elif what == "down":
            out_down[:, cols] = total
        elif what == "query":
            out_query[:, cols] = total * 0.125
        elif what == "keyval":
            out_keyval[:, cols] = total
        else:
            out_out[:, pl.ds(512 * which, COLS)] = total[:8]
            out_out[:, pl.ds(512 * which + COLS, COLS)] = total[8:]

    for k in range(4):
        lefts[L_LATENT, k] = turned(lin[:, pl.ds(COLS * k, COLS)].astype(F32))

    @pl.when(section == 1)
    def _():
        turn_att()

    media_rows(0).start()
    ups = 0
    for t in range(TICKS):
        for lane in range(3):
            if runs(lane, t, 0):
                terms(lane, t)
                for way in range(2):
                    ring_copy(lane, t, 0, 0, way).start()
        if t == 0:

            @pl.when(section == 1)
            def _():
                turn_act()

            taken(G_OUT, use_out)
            media_back(0)
        if t == 1:

            @pl.when(section == 1)
            def _():
                turn_ff(True)

            turn_pre()
            media_back(1)
            media_back(2)
        if t == 2:
            media_back(3)
            media_back(4)
            media_back(5)
            small_give(0)
        if t in (4, 5, 6):
            if t == 4:
                for i in (4, 5):
                    media_away(i).wait_send()
                    media_home(i).wait()
            media_sum(2 * t - 8)
        if t in (3, 4, 5):
            small_take(t - 3)
            if t < 5:
                small_give(t - 2)
        for lane in range(3):
            group = t - 1
            if runs(lane, group, 0):
                axis = PLAN[lane][group][2][0]
                for way in range(2):
                    ring_copy(lane, group, 0, 0, way).wait()
                    own1[spot(lane, group) + at(axis, 1 if way == 0 else 3), pl.ds(way * 128, 128), :] += far1[lane, way, group % 3]
            group = t - 2
            if runs(lane, group, 0):
                for way in range(2):
                    ring_copy(lane, group, 0, 1, way).wait()
                    ring_copy(lane, group, 0, 2, way).wait()
                mine = spot(lane, group) + at(PLAN[lane][group][2][0], 0)
                three, two = group % 3, group % 2
                total = [
                    own1[mine, pl.ds(0, 128), :] + summed1[lane, 0, two] + mine1[lane, 1, three],
                    own1[mine, pl.ds(128, 128), :] + mine1[lane, 0, three] + summed1[lane, 1, two],
                ]
                for k in range(4):
                    own2[spot(lane, group) + k] = total[k // 2][64 * (k % 2) : 64 * (k % 2) + 64]
            group = t - 3
            if runs(lane, group, 1) and group < STRAIGHT:
                axis = PLAN[lane][group][2][1]
                for way in range(2):
                    ring_copy(lane, group, 1, 0, way).wait()
                    own2[spot(lane, group) + at(axis, 1 if way == 0 else 3), pl.ds(way * 32, 32), :] += far2[lane, way, group % 2]
            for group in (t - 3, t - 4):
                if runs(lane, group, 1) and (group >= STRAIGHT) == (group == t - 3):
                    what, which, axes = PLAN[lane][group]
                    total = own2[spot(lane, group) + at(axes[1], 0)]
                    if group < STRAIGHT:
                        for way in range(2):
                            ring_copy(lane, group, 1, 1, way).wait()
                            total += near2[lane, way, group % 2]
                    else:
                        for shift in (1, 2, 3):
                            straight_copy(lane, group, shift).wait()
                            total += straight[lane, group - STRAIGHT, shift - 1]
                    if len(axes) == 3:
                        for k in range(4):
                            own3[spot(lane, group) + k] = total[16 * k : 16 * k + 16]
                    else:
                        finish(what, which, total)
                        if what == "up":
                            ups += 1
            for group in (t - 4, t - 5):
                if runs(lane, group, 2) and (group >= STRAIGHT) == (group == t - 4):
                    what, which, axes = PLAN[lane][group]
                    total = own3[spot(lane, group) + at(axes[2], 0)]
                    for shift in (1, 2, 3):
                        last_copy(lane, group, shift).wait()
                        total += last[lane, last_turn(lane, group), shift - 1]
                    finish(what, which, total)
        for lane in range(3):
            for way in range(2):
                if runs(lane, t - 1, 0):
                    ring_copy(lane, t - 1, 0, 2, way).start()
                if runs(lane, t - 2, 1) and t - 2 < STRAIGHT:
                    ring_copy(lane, t - 2, 1, 0, way).start()
                if runs(lane, t - 3, 1) and t - 3 < STRAIGHT:
                    ring_copy(lane, t - 3, 1, 1, way).start()
            for shift in (1, 2, 3):
                if runs(lane, t - 2, 1) and t - 2 >= STRAIGHT:
                    straight_copy(lane, t - 2, shift).start()
                if runs(lane, t - 3, 2) and t - 3 >= STRAIGHT:
                    last_copy(lane, t - 3, shift).start()
                if runs(lane, t - 4, 2) and t - 4 < STRAIGHT:
                    last_copy(lane, t - 4, shift).start()
            for way in range(2):
                if runs(lane, t, 0):
                    ring_copy(lane, t, 0, 1, way).start()
        if ups == 4:
            ups = 0
            for shift in (1, 2, 3):
                up_copy(shift).start()

    for s in range(4):
        part = up_sum[pl.ds(pl.multiple_of(16 * coords[A], 16), 16), :] if s == 0 else None
        if s > 0:
            up_copy(s).wait()
            part = up_got[s - 1]
        cols = pl.ds(pl.multiple_of(1024 * at(A, 4 - s), 1024), 1024)
        out_up[:, cols] = part

    for i in (4, 5):
        media_done(i).wait()

    @pl.when(section == 0)
    def _():
        to_other(sent, resampled, r_sem).wait_recv()
        to_other(sent, latents_grad, l_sem).wait_send()

    @pl.when(section == 1)
    def _():
        to_other(sent, resampled, r_sem).wait_send()
        to_other(accs, gys, g_sem).wait_send()
        to_other(sent, latents_grad, l_sem).wait_recv()


def run_resampler(latents, media, norms, w_query, w_keyval, w_out, w_up, w_down, cotangent):
    vmem = pl.BlockSpec(memory_space=pltpu.VMEM)
    hbm = pl.BlockSpec(memory_space=pl.ANY)

    def sds(*shape):
        return jax.ShapeDtypeStruct(shape, F32)

    dma = pltpu.SemaphoreType.DMA
    return pl.pallas_call(
        resampler_kernel,
        out_shape=[
            sds(192, 512), sds(192, 512), sds(16, 128), sds(16, 512), sds(16, 1024), sds(8, 1024), sds(16, 4096), sds(64, 1024),
            sds(6, 2, 256, 256), sds(6, 2, 256, 256), sds(6, 2, 256, 256), sds(4, 3, 4, 192, 256),
        ],
        in_specs=[hbm, hbm, vmem] + [hbm] * 6,
        out_specs=[vmem] * 8 + [hbm] * 4,
        scratch_shapes=[
            pltpu.VMEM((1, 1024, 512), BF16),
            pltpu.VMEM((1, 1024, 1024), BF16),
            pltpu.VMEM((1, 512, 1024), BF16),
            pltpu.VMEM((192, 1024), F32),
            pltpu.VMEM((192, 1024), F32),
            pltpu.VMEM((192, 1024), F32),
            pltpu.VMEM((192, 1024), F32),
            pltpu.VMEM((192, 1024), BF16),
            pltpu.VMEM((192, 1024), BF16),
            pltpu.VMEM((192, 512), BF16),
            pltpu.VMEM((192, 512), BF16),
            pltpu.VMEM((192, 512), BF16),
            pltpu.VMEM((16, 192, 256), F32),
            pltpu.VMEM((8, 1024), F32),
            pltpu.VMEM((192, 512), F32),
            pltpu.VMEM((2, 4, 256, 256), F32),
            pltpu.VMEM((2, 256, 1024), BF16),
            pltpu.VMEM((DEEP, 512, 1024), BF16),
            pltpu.VMEM((2, 4, 192, 256), F32),
            pltpu.VMEM((18, 4, 256, 256), BF16),
            pltpu.VMEM((66, 256, 256), BF16),
        ]
        + [pltpu.VMEM((36, r, COLS), F32) for r in RING_ROWS]
        + [
            pltpu.VMEM((3, 2, 3, 128, COLS), F32),
            pltpu.VMEM((3, 2, 2, 32, COLS), F32),
            pltpu.VMEM((3, 2, 3, 128, COLS), F32),
            pltpu.VMEM((3, 2, 2, 128, COLS), F32),
            pltpu.VMEM((3, 2, 2, 64, COLS), F32),
            pltpu.VMEM((3, 3, 3, 16, COLS), F32),
            pltpu.VMEM((3, 2, 3, 64, COLS), F32),
            pltpu.VMEM((64, 1024), F32),
            pltpu.VMEM((3, 16, 1024), F32),
            pltpu.VMEM((2, 8, COLS), F32),
            pltpu.VMEM((3, 3, 8, COLS), F32),
            pltpu.VMEM((COLS, 128), F32),
            dma((3,)), dma((3, 4)), dma((2,)), dma((2,)), dma((2,)), dma((2,)), dma((2,)), dma((6,)), dma((6,)), dma((6,)),
            dma((4, 3)), dma((4, 3)), dma((2,)), dma((108,)), dma((108,)), dma((27,)), dma((27,)), dma((18,)), dma((18,)), dma((3,)), dma((3,)), dma((3, 3)), dma((3, 3)),
        ],
        compiler_params=pltpu.CompilerParams(collective_id=1, has_side_effects=True, vmem_limit_bytes=VMEM_BYTES),
        name="resampler",
    )(latents, media, norms, w_query, w_keyval, w_out, w_up, w_down, cotangent)


def results_kernel(small, media, *refs):
    given, (media_grad, gains_grad, biases_grad), made, held, sem = refs[:7], refs[7:10], refs[10:17], refs[17:25], refs[25]
    moves = []
    for i in range(6):
        for k in range(2):
            moves.append((media.at[i, k], held[7].at[i, k], media_grad.at[pl.ds(COLS * i, COLS), pl.ds(COLS * k, COLS)]))
    moves += list(zip(given, held, made))
    loads = [pltpu.make_async_copy(a, b, sem.at[0, n]) for n, (a, b, _) in enumerate(moves)]
    stores = [pltpu.make_async_copy(b, c, sem.at[1, n]) for n, (_, b, c) in enumerate(moves)]
    for c in loads:
        c.start()
    columns = jnp.concatenate([small[...], jnp.zeros((112, 128), F32)], 0).T
    gains_grad[0] = columns[:3, :16]
    biases_grad[0] = columns[3:6, :16]
    for a, b in zip(loads, stores):
        a.wait()
        b.start()
    for c in stores:
        c.wait()


def results(media, small, *rest):
    vmem = pl.BlockSpec(memory_space=pltpu.VMEM)
    hbm = pl.BlockSpec(memory_space=pl.ANY)

    def sds(*shape):
        return jax.ShapeDtypeStruct(shape, F32)

    return pl.pallas_call(
        results_kernel,
        out_shape=[sds(1536, 512), sds(1, 3, 16), sds(1, 3, 16)] + [sds(*a.shape) for a in rest],
        in_specs=[vmem] + [hbm] * 8,
        out_specs=[hbm, vmem, vmem] + [hbm] * 7,
        scratch_shapes=[pltpu.VMEM(a.shape, F32) for a in rest + (media,)] + [pltpu.SemaphoreType.DMA((2, 19))],
        compiler_params=pltpu.CompilerParams(vmem_limit_bytes=VMEM_BYTES),
        name="results",
    )(small, media, *rest)


def body(
    latents_in, media, frame_count, gains, biases, w_query, w_keyval, w_out, w_up, w_down, cotangent
):
    frames = jnp.broadcast_to(64.0 * frame_count.astype(F32)[:, :1], (3, COLS)).reshape(1, 768)
    norms = jnp.concatenate([gains[0], biases[0], jnp.pad(frames, ((0, 1), (0, 256)))], 0)
    resampled, latents_grad, small, query, keyval, out, up, down, media_sum, _, _, _ = run_resampler(
        latents_in.reshape(192, 1024), media.reshape(1536, 1024), norms,
        w_query, w_keyval, w_out, w_up.reshape(4, 256, 4096), w_down.reshape(4096, 1024), cotangent.reshape(192, 1024),
    )
    media_grad, gains_grad, biases_grad, resampled, latents_grad, query, keyval, out, up, down = results(
        media_sum, small, resampled, latents_grad, query, keyval, out, up, down
    )
    return (
        resampled.reshape(3, 1, 64, 512),
        latents_grad.reshape(3, 1, 64, 512),
        media_grad.reshape(3, 1, 512, 512),
        gains_grad,
        biases_grad,
        query[None],
        keyval[None],
        out[None],
        up[None],
        down[None],
    )


def solution(mesh):
    placed = (
        P(None, "dp", None, None),
        P(None, "dp", None, None),
        P(None, "dp"),
        P("section", None, None),
        P("section", None, None),
        P("section", None, None),
        P("section", None, None),
        P("section", None, None),
        P("section", None, None),
        P("section", None, None),
        P(None, "dp", None, None),
    )
    return jax.shard_map(
        body,
        mesh=mesh,
        in_specs=placed,
        out_specs=(
            P(None, "dp", None, "section"),
            P(None, "dp", None, "section"),
            P(None, "dp", None, "section"),
            P("section", None, "dp"),
            P("section", None, "dp"),
            P("section", "dp", None),
            P("section", "dp", None),
            P("section", "dp", None),
            P("section", "dp", None),
            P("section", "dp", None),
        ),
        check_vma=False,
    )
```

```python
import jax
import jax.numpy as jnp
from jax import lax
from jax.experimental import pallas as pl
from jax.experimental.pallas import tpu as pltpu
from jax.sharding import PartitionSpec as P

VMEM_BYTES = 63 * 2**20
MESH = pl.DeviceIdType.MESH
F32 = jnp.float32
BF16 = jnp.bfloat16
NORM_EPS = 1e-05
MASK_FILL = -1e30
ROOT_HALF = 0.7071067811865476
INV_ROOT_TAU = 0.3989422804014327
ROWS_ALL = 192
KEYS = 640
FF_STEPS = 8
RING_ROWS = (256, 64, 16)
COLS = 256
A, B, C = 0, 1, 2
FF_IN, ACT, G_OUT, G_PRE = 0, 1, 2, 3
L_LATENT, L_FF, L_ACT, L_ATT = 6, 8, 12, 16
R_PRE, R_OUT, R_ATT, R_QUERY, R_KV = 0, 16, 32, 36, 38
PLAN = (
    (
        ("query", 0, (A, B, C)),
        ("query", 1, (A, B, C)),
        ("down", 0, (A, C)),
        ("keyval", 0, (A, B, C)),
        ("keyval", 2, (A, B, C)),
        ("down", 1, (A, C)),
    ),
    (
        ("out", 0, (B, C, A)),
        None,
        ("up", 0, (B, C)),
        ("up", 1, (B, C)),
        ("keyval", 1, (B, C, A)),
        None,
    ),
    (
        ("out", 1, (C, B, A)),
        ("down", 2, (C, A)),
        ("up", 2, (C, B)),
        ("up", 3, (C, B)),
        ("keyval", 3, (C, B, A)),
        ("down", 3, (C, A)),
    ),
)
GROUPS = 6
TICKS = GROUPS + 3
STRAIGHT = 4
WIDE = 4
DEEP = 3
WU_BASE = 34


def mm(left, right):
    return jnp.dot(left, right, preferred_element_type=F32)


def mm_nt(left, right):
    return lax.dot_general(left, right, (((1,), (1,)), ((), ())), preferred_element_type=F32)


def mm_tn(left, right):
    return lax.dot_general(left, right, (((0,), (0,)), ((), ())), preferred_element_type=F32)


def normed_rows(values):
    average = jnp.mean(values, -1, keepdims=True)
    centred = values - average
    inverse = lax.rsqrt(jnp.mean(centred * centred, -1, keepdims=True) + NORM_EPS)
    return centred * inverse, inverse


def norm_back(grad, normed, inverse, gain):
    scaled = grad * gain
    inner = jnp.mean(scaled, -1, keepdims=True)
    along = jnp.mean(scaled * normed, -1, keepdims=True)
    back = inverse * (scaled - inner - normed * along)
    return back, jnp.sum(grad * normed, 0, keepdims=True), jnp.sum(grad, 0, keepdims=True)


def turned(block):
    rows = block.shape[0]
    if rows < 256:
        block = jnp.concatenate([block, jnp.zeros((256 - rows, block.shape[1]), block.dtype)], 0)
    return block.T.astype(BF16)


def head_stack(block):
    lane = lax.broadcasted_iota(jnp.int32, (64, 256), 1) // 64
    return jnp.concatenate([jnp.where(lane == h, block, jnp.zeros_like(block)) for h in range(4)], 0)


def head_merge(block):
    lane = lax.broadcasted_iota(jnp.int32, (64, 256), 1) // 64
    return sum(jnp.where(lane == h, block[64 * h : 64 * h + 64], 0.0) for h in range(4))


def column(block, k):
    return block[:, COLS * k : COLS * k + COLS]


def resampler_kernel(
    latents, media, norms, w_query, w_keyval, w_out, w_up, w_down, cotangent,
    resampled, latents_grad, out_small, out_query, out_keyval, out_out, out_up, out_down, m_sum, m_own, m_got, land,
    wq, wkv, wo, xs, x1s, gys, accs, lin, ffin, qs, att, gatt, pres, sums, sent, m_stage, m_buf, wd, gave,
    lefts, rights, own1, own2, own3, far1, far2, mine1, summed1, near2, last, straight, up_sum, up_got, small_sum, small_got, columns,
    a_sem, w_sem, b_sem, x_sem, g_sem, r_sem, l_sem, m_send, m_recv, m_local, e_send, e_recv, c_sem, t_send, t_recv, z_send, z_recv, d_send, d_recv, u_send, u_recv, s_send, s_recv,
):
    section = lax.axis_index("section")
    other = 1 - section
    me = lax.axis_index("dp")
    x, y, z = me // 16, (me // 4) % 4, me % 4

    def by_section(first, second):
        return first + section * (second - first)

    coords = (by_section(x, z), by_section(y, x), by_section(z, y))
    strides = (by_section(16, 1), by_section(4, 16), by_section(1, 4))

    def at(axis, shift):
        return (coords[axis] + shift) % 4

    def peer(axis, shift):
        return me + (at(axis, shift) - coords[axis]) * strides[axis]

    held = [pltpu.make_async_copy(*pair, a_sem.at[n]) for n, pair in enumerate(((w_keyval, wkv), (w_query, wq), (w_out, wo)))]
    for c in held:
        c.start()
    barrier = pltpu.get_barrier_semaphore()
    pl.semaphore_signal(barrier, inc=1, device_id={"section": other}, device_id_type=MESH)
    greeted = [(axis, shift) for axis in (A, B, C) for shift in (1, 2, 3)]
    for axis, shift in greeted:
        pl.semaphore_signal(barrier, inc=1, device_id={"dp": peer(axis, shift)}, device_id_type=MESH)

    pl.semaphore_wait(barrier, 1 + len(greeted))

    def to_other(source, target, sem):
        return pltpu.make_async_remote_copy(
            src_ref=source, dst_ref=target, send_sem=sem.at[0], recv_sem=sem.at[1],
            device_id={"section": other}, device_id_type=MESH,
        )

    def up_block(step):
        return WU_BASE + 8 * (step % WIDE)

    def down_rows(step):
        rows = pl.ds(pl.multiple_of(step * 512, 512), 512)
        return [pltpu.make_async_copy(w_down.at[rows, :], wd.at[step % DEEP], w_sem.at[2, step % DEEP])]

    def up_columns(step):
        copies = []
        for k in range(2):
            cols = pl.ds(pl.multiple_of(step * 512 + COLS * k, COLS), COLS)
            copies.append(
                pltpu.make_async_copy(w_up.at[:, :, cols], rights.at[pl.ds(up_block(step) + 4 * k, 4)], w_sem.at[k, step % WIDE])
            )
        return copies

    def fetch_first():
        for step in range(DEEP - 1):
            for c in down_rows(step) + up_columns(step):
                c.start()

    def fetch_next(step):
        @pl.when(step + DEEP - 1 < FF_STEPS)
        def _():
            for c in down_rows(step + DEEP - 1) + up_columns(step + DEEP - 1):
                c.start()

    def fetched(step):
        for c in down_rows(step) + up_columns(step):
            c.wait()

    def media_rows(i):
        return pltpu.make_async_copy(
            media.at[pl.ds(pl.multiple_of(i * 256, 256), 256), :], m_buf.at[i % 2], b_sem.at[i % 2]
        )

    def exchange(kind, shift):
        axis = A if kind in (FF_IN, G_PRE) else B
        if kind == FF_IN:
            source = gave.at[0]
        elif kind == G_OUT:
            source = gave.at[1]
        elif kind == ACT:
            source = own1.at[pl.ds(18 + 4 * at(axis, shift), 4), pl.ds(0, ROWS_ALL), :]
        else:
            source = pres.at[pl.ds(4 * at(axis, shift), 4)]
        return pltpu.make_async_remote_copy(
            src_ref=source, dst_ref=land.at[kind, shift - 1], send_sem=e_send.at[kind, shift - 1], recv_sem=e_recv.at[kind, shift - 1],
            device_id={"dp": peer(axis, shift)}, device_id_type=MESH,
        )

    def give(kind):
        for shift in (1, 3, 2):
            exchange(kind, shift).start()

    def taken(kind, use, late=False):
        def held(s):
            if late:
                return own1.at[pl.ds(24 + 4 * (s % 2), 4), pl.ds(0, ROWS_ALL), :]
            return m_stage.at[s % 2, :, pl.ds(0, ROWS_ALL), :]

        def load(s):
            return pltpu.make_async_copy(land.at[kind, s], held(s), c_sem.at[s % 2])

        exchange(kind, 1).wait()
        load(0).start()
        for s in range(3):
            if s < 2:
                exchange(kind, s + 2).wait()
                load(s + 1).start()
            load(s).wait()
            use(s + 1, held(s))

    fetch_first()
    media_rows(0).start()

    def to_rows(ref, value):
        for k in range(4):
            ref[k] = column(value, k)

    @pl.when(section == 0)
    def _():
        given = pltpu.make_async_copy(latents, lin, c_sem.at[0])
        given.start()
        given.wait()
        xs[...] = lin[...].astype(F32)

    @pl.when(section == 1)
    def _():
        given = pltpu.make_async_copy(cotangent, lin, c_sem.at[0])
        given.start()
        given.wait()
        gys[...] = lin[...].astype(F32)
        to_rows(gave.at[1], lin[...].astype(F32))
        give(G_OUT)

    def media_block(i, carry):
        @pl.when(i < 5)
        def _():
            media_rows(i + 1).start()

        media_rows(i).wait()
        normed, _ = normed_rows(m_buf[i % 2].astype(F32))
        media_in = (normed * norms[0:1, :] + norms[3:4, :]).astype(BF16)
        keyval = mm(media_in, wkv[0]).astype(BF16)
        for j in range(4):
            lefts[i, j] = column(keyval, j)
        return carry

    held[0].wait()
    lax.fori_loop(0, 6, media_block, 0)
    held[1].wait()
    held[2].wait()
    @pl.when(section == 1)
    def _():
        to_other(accs, xs, x_sem).wait_recv()

    normed, _ = normed_rows(xs[...])
    lin[...] = (normed * norms[1:2, :] + norms[4:5, :]).astype(BF16)
    qs[...] = (mm(lin[...], wq[0]) * 0.125).astype(BF16)
    latent_kv = mm(lin[...], wkv[0]).astype(BF16)
    for v in range(3):
        for j in range(4):
            rows = pl.ds((v % 2) * 128, 64)
            lefts[6 + v // 2, j, rows, :] = latent_kv[64 * v : 64 * v + 64, COLS * j : COLS * j + COLS]
            lefts[6 + v // 2, j, pl.ds((v % 2) * 128 + 64, 64), :] = jnp.zeros((64, COLS), BF16)

    def keyvals_of(v, j):
        tail = pl.ds((v % 2) * 128, 128)
        return lefts[2 * v, j], lefts[2 * v + 1, j], lefts[6 + v // 2, j, tail, :]

    key = lax.broadcasted_iota(jnp.int32, (1, KEYS), 1).astype(F32)

    def attend(v):
        rows = pl.ds(v * 64, 64)
        valid = (key < norms[6:7, 256 * v : 256 * v + 1]) | ((key >= 512.0) & (key < 576.0))
        for g in range(2):
            cols = pl.ds(COLS * g, COLS)
            stacked = head_stack(qs[rows, cols])
            scores = [mm_nt(stacked, k) for k in keyvals_of(v, g)]
            scores = [
                jnp.where(valid[:, 256 * n : 256 * n + s.shape[1]], s, MASK_FILL) for n, s in enumerate(scores)
            ]
            top = jnp.max(jnp.maximum(scores[0], scores[1]), -1, keepdims=True)
            top = jnp.maximum(top, jnp.max(scores[2], -1, keepdims=True))
            raised = [jnp.exp(s - top) for s in scores]
            whole = jnp.sum(raised[0] + raised[1], -1, keepdims=True) + jnp.sum(raised[2], -1, keepdims=True)
            scale = 1.0 / whole
            mixed = jnp.zeros((256, COLS), F32)
            for n, (e, values) in enumerate(zip(raised, keyvals_of(v, 2 + g))):
                p = e * scale
                own1[(v * 2 + g) * 3 + n, :, pl.ds(0, p.shape[1])] = p
                mixed += mm(p.astype(BF16), values)
            att[rows, cols] = head_merge(mixed).astype(BF16)

    for v in range(3):
        attend(v)

    x1 = xs[...] + mm(att[...], wo[0])
    x1s[...] = x1
    accs[...] = x1
    normed, _ = normed_rows(x1)
    ffin[...] = (normed * norms[2:3, :] + norms[5:6, :]).astype(BF16)
    to_rows(gave.at[0], ffin[...].astype(F32))
    give(FF_IN)

    def ff_forward(j, carry):
        fetched(j)
        fetch_next(j)
        acts = []
        for k in range(2):
            base = up_block(j) + 4 * k
            pre = sum(mm(ffin[:, pl.ds(COLS * r, COLS)], rights[base + r]) for r in range(4))
            act = (pre * (0.5 * (1.0 + lax.erf(pre * ROOT_HALF)))).astype(BF16)
            pres[2 * j + k] = pre
            own1[18 + by_section(4 * (2 * (j % 2) + k) + j // 2, 2 * j + k), pl.ds(0, ROWS_ALL), :] = act.astype(F32)
            acts.append(act)
        accs[...] += mm(jnp.concatenate(acts, 1), wd[j % DEEP])
        return carry

    lax.fori_loop(0, FF_STEPS, ff_forward, 0)
    give(ACT)
    fetch_first()

    def turn_ff(late):
        for k in range(4):
            lefts[L_FF, k] = turned(gave[0, k])

        def use_ff(s, piece):
            for k in range(4):
                lefts[L_FF + s, k] = turned(piece[k])

        taken(FF_IN, use_ff, late)

    def turn_att():
        for i in range(4):
            part = jnp.concatenate([att[:, pl.ds(128 * i, 128)].astype(F32), jnp.zeros((64, 128), F32)], 0)
            part = part.T.reshape(16, 8, 256)
            none = jnp.zeros_like(part)
            lefts[L_ATT, i] = jnp.concatenate([part, none], 1).reshape(256, 256).astype(BF16)
            lefts[L_ATT + 1, i] = jnp.concatenate([none, part], 1).reshape(256, 256).astype(BF16)

    def turn_act():
        for k in range(4):
            lefts[L_ACT, k] = turned(own1[18 + 4 * coords[B] + k, pl.ds(0, ROWS_ALL), :])
        def use_act(s, piece):
            for k in range(4):
                lefts[L_ACT + s, k] = turned(piece[k])

        taken(ACT, use_act)

    @pl.when(section == 0)
    def _():
        to_other(accs, xs, x_sem).start()
        turn_ff(False)
        turn_act()
        turn_att()
        to_other(accs, xs, x_sem).wait_send()
        to_other(accs, gys, g_sem).wait_recv()
        to_rows(gave.at[1], gys[...].astype(BF16).astype(F32))
        give(G_OUT)

    @pl.when(section == 1)
    def _():
        sent[...] = accs[:, pl.ds(0, 512)]
        to_other(sent, resampled, r_sem).start()
        resampled[...] = accs[:, pl.ds(512, 512)]

    ffin[...] = gys[...].astype(BF16)
    accs[...] = jnp.zeros((ROWS_ALL, 1024), F32)

    def ff_backward(j, carry):
        fetched(j)
        fetch_next(j)
        grad_act = mm_nt(ffin[...], wd[j % DEEP])
        halves = []
        for k in range(2):
            pre = pres[2 * j + k]
            slope = 0.5 * (1.0 + lax.erf(pre * ROOT_HALF)) + pre * jnp.exp(-0.5 * pre * pre) * INV_ROOT_TAU
            halves.append((column(grad_act, k) * slope).astype(BF16))
            pres[2 * j + k] = halves[k].astype(F32)
        base = up_block(j)
        for r in range(4):
            accs[:, pl.ds(COLS * r, COLS)] += mm_nt(halves[0], rights[base + r]) + mm_nt(halves[1], rights[base + 4 + r])
        quarter = j // 2
        shift = (quarter - coords[A] + 4) % 4

        @pl.when((j % 2 == 1) & (shift != 0))
        def _():
            exchange(G_PRE, shift).start()

        return carry

    lax.fori_loop(0, FF_STEPS, ff_backward, 0)
    for k in list(range(R_KV)) + [R_KV + 7 * j + 6 for j in range(4)]:
        rights[k, pl.ds(192, 64), :] = jnp.zeros((64, COLS), BF16)
    for k in range(4):
        rights[R_OUT + k, pl.ds(0, ROWS_ALL), :] = ffin[:, pl.ds(COLS * k, COLS)]
    normed, inverse = normed_rows(x1s[...])
    back, gain_sum, bias_sum = norm_back(accs[...], normed, inverse, norms[2:3, :])
    sums[pl.ds(6, 2), :] = jnp.zeros((2, 1024), F32)
    sums[pl.ds(2, 1), :] = gain_sum
    sums[pl.ds(5, 1), :] = bias_sum
    grad_x1 = gys[...] + back
    gys[...] = grad_x1
    grad_attn = grad_x1.astype(BF16)
    for k in range(4):
        rights[R_ATT + k, pl.ds(0, ROWS_ALL), :] = column(grad_attn, k)
    gatt[...] = mm_nt(grad_attn, wo[0]).astype(BF16)

    def attend_back(v):
        rows = pl.ds(v * 64, 64)
        for g in range(2):
            cols = pl.ds(COLS * g, COLS)
            q_stack = head_stack(qs[rows, cols])
            g_stack = head_stack(gatt[rows, cols])
            widths = (256, 256, 128)
            probs = [own1[(v * 2 + g) * 3 + n, :, pl.ds(0, widths[n])] for n in range(3)]
            weighted = [p * mm_nt(g_stack, values) for p, values in zip(probs, keyvals_of(v, 2 + g))]
            whole = jnp.sum(weighted[0] + weighted[1], -1, keepdims=True) + jnp.sum(weighted[2], -1, keepdims=True)
            grad_s = [(w - p * whole).astype(BF16) for w, p in zip(weighted, probs)]
            grad_q = sum(mm(s, k) for s, k in zip(grad_s, keyvals_of(v, g)))
            rights[R_QUERY + g, rows, :] = head_merge(grad_q).astype(BF16)
            for base, factors, stack in (
                (R_KV + 7 * g, grad_s, q_stack),
                (R_KV + 14 + 7 * g, [p.astype(BF16) for p in probs], g_stack),
            ):
                rights[base + 2 * v] = mm_tn(factors[0], stack).astype(BF16)
                rights[base + 2 * v + 1] = mm_tn(factors[1], stack).astype(BF16)
                rights[base + 6, rows, :] = mm_tn(factors[2], stack)[:64].astype(BF16)

    for v in range(3):
        attend_back(v)

    grad_in = sum(mm_nt(rights[R_QUERY + g, pl.ds(0, ROWS_ALL), :], wq[0, :, pl.ds(COLS * g, COLS)]) for g in range(2))
    grad_in = grad_in * 0.125
    for k in range(4):
        grad_in += mm_nt(rights[R_KV + 6 + 7 * k, pl.ds(0, ROWS_ALL), :], wkv[0, :, pl.ds(COLS * k, COLS)])
    normed, inverse = normed_rows(xs[...])
    back, gain_sum, bias_sum = norm_back(grad_in, normed, inverse, norms[1:2, :])
    sums[pl.ds(1, 1), :] = gain_sum
    sums[pl.ds(4, 1), :] = bias_sum
    accs[...] = gys[...] + back

    @pl.when(section == 1)
    def _():
        to_other(accs, gys, g_sem).start()

    @pl.when(section == 0)
    def _():
        sent[...] = accs[:, pl.ds(512, 512)]
        to_other(sent, latents_grad, l_sem).start()
        latents_grad[...] = accs[:, pl.ds(0, 512)]

    def use_out(s, piece):
        for k in range(4):
            rights[R_OUT + 4 * s + k, pl.ds(0, ROWS_ALL), :] = piece[k].astype(BF16)


    def turn_pre():
        for k in range(4):
            rights[R_PRE + k, pl.ds(0, ROWS_ALL), :] = pres[4 * coords[A] + k].astype(BF16)

        def use_pre(s, piece):
            for k in range(4):
                rights[R_PRE + 4 * s + k, pl.ds(0, ROWS_ALL), :] = piece[k].astype(BF16)

        taken(G_PRE, use_pre, True)

    def media_away(i):
        return pltpu.make_async_remote_copy(
            src_ref=m_stage.at[i % 2, pl.ds(2 * other, 2)], dst_ref=m_got.at[i], send_sem=m_send.at[i], recv_sem=m_recv.at[i],
            device_id={"section": other}, device_id_type=MESH,
        )

    def media_home(i):
        return pltpu.make_async_copy(m_stage.at[i % 2, pl.ds(2 * section, 2)], m_own.at[i], m_local.at[i])

    def media_back(i):
        if i < 5:
            media_rows(i + 1).start()
        media_rows(i).wait()
        if i >= 2:
            media_away(i - 2).wait_send()
            media_home(i - 2).wait()
        normed, inverse = normed_rows(m_buf[i % 2].astype(F32))
        media_in = normed * norms[0:1, :] + norms[3:4, :]
        grad_media = mm_nt(rights[R_KV + i], wkv[0, :, pl.ds(0, COLS)])
        for k in range(1, 4):
            grad_media += mm_nt(rights[R_KV + 7 * k + i], wkv[0, :, pl.ds(COLS * k, COLS)])
        back, gain_sum, bias_sum = norm_back(grad_media, normed, inverse, norms[0:1, :])
        if i == 0:
            sums[pl.ds(0, 1), :] = gain_sum
            sums[pl.ds(3, 1), :] = bias_sum
        else:
            sums[pl.ds(0, 1), :] += gain_sum
            sums[pl.ds(3, 1), :] += bias_sum
        for k in range(4):
            m_stage[i % 2, k] = column(back, k)
        media_away(i).start()
        media_home(i).start()
        for k in range(4):
            lefts[i, k] = turned(column(media_in, k).astype(BF16).astype(F32))

    def media_parts(i):
        return (
            pltpu.make_async_copy(m_own.at[i], m_stage.at[i % 2, pl.ds(0, 2)], m_local.at[i]),
            pltpu.make_async_copy(m_got.at[i], m_stage.at[i % 2, pl.ds(2, 2)], m_send.at[i]),
        )

    def media_done(i):
        return pltpu.make_async_copy(m_stage.at[i % 2, pl.ds(0, 2)], m_sum.at[i], m_local.at[i])

    def media_sum(first):
        for i in (first, first + 1):
            if i >= 2:
                media_done(i - 2).wait()
            media_away(i).wait_recv()
            for c in media_parts(i):
                c.start()
        for i in (first, first + 1):
            for c in media_parts(i):
                c.wait()
            for k in range(2):
                m_stage[i % 2, k] += m_stage[i % 2, 2 + k]
            media_done(i).start()

    places, steps = (x, y, z), (16, 4, 1)

    def small_copy(axis, shift):
        place = (places[axis] + shift) % 4
        source = sums.at[:, pl.ds(pl.multiple_of(COLS * place, COLS), COLS)] if axis == 0 else small_sum.at[axis - 1]
        return pltpu.make_async_remote_copy(
            src_ref=source, dst_ref=small_got.at[axis, shift - 1], send_sem=s_send.at[axis, shift - 1], recv_sem=s_recv.at[axis, shift - 1],
            device_id={"dp": me + (place - places[axis]) * steps[axis]}, device_id_type=MESH,
        )

    def small_give(axis):
        for shift in (1, 2, 3):
            small_copy(axis, shift).start()

    def small_take(axis):
        total = sums[:, pl.ds(pl.multiple_of(COLS * x, COLS), COLS)] if axis == 0 else small_sum[axis - 1]
        for shift in (1, 2, 3):
            small_copy(axis, shift).wait()
            total += small_got[axis, shift - 1]
        if axis < 2:
            small_sum[axis] = total
        else:
            columns[...] = jnp.concatenate([total, jnp.zeros((120, COLS), F32)], 0).T
            out_small[...] = columns[pl.ds(pl.multiple_of(16 * (4 * y + z), 16), 16), :]

    def factors(what, which):
        if what == "up":
            return [(L_FF + s, R_PRE + 4 * s + which) for s in range(4)]
        if what == "down":
            return [(L_ACT + s, R_OUT + 4 * s + which) for s in range(4)]
        if what == "out":
            return [(L_ATT + s, R_ATT + 2 * which + s) for s in range(2)]
        if what == "query":
            return [(L_LATENT, R_QUERY + which)]
        return [(k, R_KV + 7 * which + k) for k in range(7)]

    own = (own1, own2, own3)

    def spot(lane, group):
        return (group % 3 * 3 + lane) * 4

    def pieces(what, axes, i, b, c):
        if what == "down":
            block = {A: by_section(i, b), C: by_section(b, i)}
            return block[axes[0]], block[axes[1]] * 4 + c
        block = {A: by_section(i, c), B: by_section(b, i), C: by_section(c, b)}
        first, second, third = axes if len(axes) == 3 else axes + (A,)
        return block[first], block[second] * 4 + block[third]

    def terms(lane, group):
        what, which, axes = PLAN[lane][group]
        base = spot(lane, group)

        def block(i, carry):
            total = sum(mm(lefts[a, i], rights[b]) for a, b in factors(what, which))
            for b in range(4):
                for c in range(4):
                    first, rest = pieces(what, axes, i, b, c)
                    rows = pl.ds(pl.multiple_of(rest * 16, 16), 16)
                    own1[base + first, rows, :] = total[(b * 4 + c) * 16 : (b * 4 + c) * 16 + 16]
            return carry

        lax.fori_loop(0, 4, block, 0)

    def ring_copy(lane, group, stage, step, way):
        axis = PLAN[lane][group][2][stage]
        half = RING_ROWS[stage] // 2
        shift = 1 if way == 0 else 3
        place = own[stage].at[spot(lane, group) + at(axis, 2 if step == 0 else shift)]
        if stage == 0:
            turn = group % 2 if step == 2 else group % 3
            source = place.at[pl.ds((1 - way if step == 1 else way) * half, half)]
            target = (far1, mine1, summed1)[step].at[lane, way, turn]
        else:
            turn = group % 2
            source = place.at[pl.ds(way * half, half)] if step == 0 else place
            target = (far2, near2)[step].at[lane, way, turn]
        sem = (((lane * 2 + stage) * 3 + step) * 2 + way) * 3 + turn
        return pltpu.make_async_remote_copy(
            src_ref=source, dst_ref=target, send_sem=t_send.at[sem], recv_sem=t_recv.at[sem],
            device_id={"dp": peer(axis, shift)}, device_id_type=MESH,
        )

    def straight_copy(lane, group, shift):
        axis = PLAN[lane][group][2][1]
        sem = (lane * 2 + group - STRAIGHT) * 3 + shift - 1
        return pltpu.make_async_remote_copy(
            src_ref=own2.at[spot(lane, group) + at(axis, shift)], dst_ref=straight.at[lane, group - STRAIGHT, shift - 1],
            send_sem=d_send.at[sem], recv_sem=d_recv.at[sem],
            device_id={"dp": peer(axis, shift)}, device_id_type=MESH,
        )

    def last_turn(lane, group):
        return sum(1 for g in range(group) if runs(lane, g, 2)) % 3

    def last_copy(lane, group, shift):
        axis = PLAN[lane][group][2][2]
        sem = (lane * 3 + last_turn(lane, group)) * 3 + shift - 1
        return pltpu.make_async_remote_copy(
            src_ref=own3.at[spot(lane, group) + at(axis, shift)], dst_ref=last.at[lane, last_turn(lane, group), shift - 1],
            send_sem=z_send.at[sem], recv_sem=z_recv.at[sem],
            device_id={"dp": peer(axis, shift)}, device_id_type=MESH,
        )

    def runs(lane, group, stage):
        return 0 <= group < GROUPS and PLAN[lane][group] is not None and stage < len(PLAN[lane][group][2])

    def up_copy(shift):
        rows = pl.ds(pl.multiple_of(16 * at(A, shift), 16), 16)
        return pltpu.make_async_remote_copy(
            src_ref=up_sum.at[rows, :], dst_ref=up_got.at[shift - 1], send_sem=u_send.at[shift - 1], recv_sem=u_recv.at[shift - 1],
            device_id={"dp": peer(A, shift)}, device_id_type=MESH,
        )

    def finish(what, which, total):
        cols = pl.ds(COLS * which, COLS)
        if what == "up":
            up_sum[:, cols] = total
        elif what == "down":
            out_down[:, cols] = total
        elif what == "query":
            out_query[:, cols] = total * 0.125
        elif what == "keyval":
            out_keyval[:, cols] = total
        else:
            out_out[:, pl.ds(512 * which, COLS)] = total[:8]
            out_out[:, pl.ds(512 * which + COLS, COLS)] = total[8:]

    for k in range(4):
        lefts[L_LATENT, k] = turned(lin[:, pl.ds(COLS * k, COLS)].astype(F32))

    @pl.when(section == 1)
    def _():
        turn_att()

    media_rows(0).start()
    ups = 0
    for t in range(TICKS):
        for lane in range(3):
            if runs(lane, t, 0):
                terms(lane, t)
                for way in range(2):
                    ring_copy(lane, t, 0, 0, way).start()
        if t == 0:

            @pl.when(section == 1)
            def _():
                turn_act()

            taken(G_OUT, use_out)
            media_back(0)
        if t == 1:

            @pl.when(section == 1)
            def _():
                turn_ff(True)

            turn_pre()
            media_back(1)
            media_back(2)
        if t == 2:
            media_back(3)
            media_back(4)
            media_back(5)
            small_give(0)
        if t in (4, 5, 6):
            if t == 4:
                for i in (4, 5):
                    media_away(i).wait_send()
                    media_home(i).wait()
            media_sum(2 * t - 8)
        if t in (3, 4, 5):
            small_take(t - 3)
            if t < 5:
                small_give(t - 2)
        for lane in range(3):
            group = t - 1
            if runs(lane, group, 0):
                axis = PLAN[lane][group][2][0]
                for way in range(2):
                    ring_copy(lane, group, 0, 0, way).wait()
                    own1[spot(lane, group) + at(axis, 1 if way == 0 else 3), pl.ds(way * 128, 128), :] += far1[lane, way, group % 3]
            group = t - 2
            if runs(lane, group, 0):
                for way in range(2):
                    ring_copy(lane, group, 0, 1, way).wait()
                    ring_copy(lane, group, 0, 2, way).wait()
                mine = spot(lane, group) + at(PLAN[lane][group][2][0], 0)
                three, two = group % 3, group % 2
                total = [
                    own1[mine, pl.ds(0, 128), :] + summed1[lane, 0, two] + mine1[lane, 1, three],
                    own1[mine, pl.ds(128, 128), :] + mine1[lane, 0, three] + summed1[lane, 1, two],
                ]
                for k in range(4):
                    own2[spot(lane, group) + k] = total[k // 2][64 * (k % 2) : 64 * (k % 2) + 64]
            group = t - 3
            if runs(lane, group, 1) and group < STRAIGHT:
                axis = PLAN[lane][group][2][1]
                for way in range(2):
                    ring_copy(lane, group, 1, 0, way).wait()
                    own2[spot(lane, group) + at(axis, 1 if way == 0 else 3), pl.ds(way * 32, 32), :] += far2[lane, way, group % 2]
            for group in (t - 3, t - 4):
                if runs(lane, group, 1) and (group >= STRAIGHT) == (group == t - 3):
                    what, which, axes = PLAN[lane][group]
                    total = own2[spot(lane, group) + at(axes[1], 0)]
                    if group < STRAIGHT:
                        for way in range(2):
                            ring_copy(lane, group, 1, 1, way).wait()
                            total += near2[lane, way, group % 2]
                    else:
                        for shift in (1, 2, 3):
                            straight_copy(lane, group, shift).wait()
                            total += straight[lane, group - STRAIGHT, shift - 1]
                    if len(axes) == 3:
                        for k in range(4):
                            own3[spot(lane, group) + k] = total[16 * k : 16 * k + 16]
                    else:
                        finish(what, which, total)
                        if what == "up":
                            ups += 1
            for group in (t - 4, t - 5):
                if runs(lane, group, 2) and (group >= STRAIGHT) == (group == t - 4):
                    what, which, axes = PLAN[lane][group]
                    total = own3[spot(lane, group) + at(axes[2], 0)]
                    for shift in (1, 2, 3):
                        last_copy(lane, group, shift).wait()
                        total += last[lane, last_turn(lane, group), shift - 1]
                    finish(what, which, total)
        for lane in range(3):
            for way in range(2):
                if runs(lane, t - 1, 0):
                    ring_copy(lane, t - 1, 0, 2, way).start()
                if runs(lane, t - 2, 1) and t - 2 < STRAIGHT:
                    ring_copy(lane, t - 2, 1, 0, way).start()
                if runs(lane, t - 3, 1) and t - 3 < STRAIGHT:
                    ring_copy(lane, t - 3, 1, 1, way).start()
            for shift in (1, 2, 3):
                if runs(lane, t - 2, 1) and t - 2 >= STRAIGHT:
                    straight_copy(lane, t - 2, shift).start()
                if runs(lane, t - 3, 2) and t - 3 >= STRAIGHT:
                    last_copy(lane, t - 3, shift).start()
                if runs(lane, t - 4, 2) and t - 4 < STRAIGHT:
                    last_copy(lane, t - 4, shift).start()
        for lane in range(3):
            for way in range(2):
                if runs(lane, t, 0):
                    ring_copy(lane, t, 0, 1, way).start()
        if ups == 4:
            ups = 0
            for shift in (1, 2, 3):
                up_copy(shift).start()

    for s in range(4):
        part = up_sum[pl.ds(pl.multiple_of(16 * coords[A], 16), 16), :] if s == 0 else None
        if s > 0:
            up_copy(s).wait()
            part = up_got[s - 1]
        cols = pl.ds(pl.multiple_of(1024 * at(A, 4 - s), 1024), 1024)
        out_up[:, cols] = part

    for i in (4, 5):
        media_done(i).wait()

    @pl.when(section == 0)
    def _():
        to_other(sent, resampled, r_sem).wait_recv()
        to_other(sent, latents_grad, l_sem).wait_send()

    @pl.when(section == 1)
    def _():
        to_other(sent, resampled, r_sem).wait_send()
        to_other(accs, gys, g_sem).wait_send()
        to_other(sent, latents_grad, l_sem).wait_recv()


def run_resampler(latents, media, norms, w_query, w_keyval, w_out, w_up, w_down, cotangent):
    vmem = pl.BlockSpec(memory_space=pltpu.VMEM)
    hbm = pl.BlockSpec(memory_space=pl.ANY)

    def sds(*shape):
        return jax.ShapeDtypeStruct(shape, F32)

    dma = pltpu.SemaphoreType.DMA
    return pl.pallas_call(
        resampler_kernel,
        out_shape=[
            sds(192, 512), sds(192, 512), sds(16, 128), sds(16, 512), sds(16, 1024), sds(8, 1024), sds(16, 4096), sds(64, 1024),
            sds(6, 2, 256, 256), sds(6, 2, 256, 256), sds(6, 2, 256, 256), sds(4, 3, 4, 192, 256),
        ],
        in_specs=[hbm, hbm, vmem] + [hbm] * 6,
        out_specs=[vmem] * 8 + [hbm] * 4,
        scratch_shapes=[
            pltpu.VMEM((1, 1024, 512), BF16),
            pltpu.VMEM((1, 1024, 1024), BF16),
            pltpu.VMEM((1, 512, 1024), BF16),
            pltpu.VMEM((192, 1024), F32),
            pltpu.VMEM((192, 1024), F32),
            pltpu.VMEM((192, 1024), F32),
            pltpu.VMEM((192, 1024), F32),
            pltpu.VMEM((192, 1024), BF16),
            pltpu.VMEM((192, 1024), BF16),
            pltpu.VMEM((192, 512), BF16),
            pltpu.VMEM((192, 512), BF16),
            pltpu.VMEM((192, 512), BF16),
            pltpu.VMEM((16, 192, 256), F32),
            pltpu.VMEM((8, 1024), F32),
            pltpu.VMEM((192, 512), F32),
            pltpu.VMEM((2, 4, 256, 256), F32),
            pltpu.VMEM((2, 256, 1024), BF16),
            pltpu.VMEM((DEEP, 512, 1024), BF16),
            pltpu.VMEM((2, 4, 192, 256), F32),
            pltpu.VMEM((18, 4, 256, 256), BF16),
            pltpu.VMEM((66, 256, 256), BF16),
        ]
        + [pltpu.VMEM((36, r, COLS), F32) for r in RING_ROWS]
        + [
            pltpu.VMEM((3, 2, 3, 128, COLS), F32),
            pltpu.VMEM((3, 2, 2, 32, COLS), F32),
            pltpu.VMEM((3, 2, 3, 128, COLS), F32),
            pltpu.VMEM((3, 2, 2, 128, COLS), F32),
            pltpu.VMEM((3, 2, 2, 64, COLS), F32),
            pltpu.VMEM((3, 3, 3, 16, COLS), F32),
            pltpu.VMEM((3, 2, 3, 64, COLS), F32),
            pltpu.VMEM((64, 1024), F32),
            pltpu.VMEM((3, 16, 1024), F32),
            pltpu.VMEM((2, 8, COLS), F32),
            pltpu.VMEM((3, 3, 8, COLS), F32),
            pltpu.VMEM((COLS, 128), F32),
            dma((3,)), dma((3, 4)), dma((2,)), dma((2,)), dma((2,)), dma((2,)), dma((2,)), dma((6,)), dma((6,)), dma((6,)),
            dma((4, 3)), dma((4, 3)), dma((2,)), dma((108,)), dma((108,)), dma((27,)), dma((27,)), dma((18,)), dma((18,)), dma((3,)), dma((3,)), dma((3, 3)), dma((3, 3)),
        ],
        compiler_params=pltpu.CompilerParams(collective_id=1, has_side_effects=True, vmem_limit_bytes=VMEM_BYTES),
        name="resampler",
    )(latents, media, norms, w_query, w_keyval, w_out, w_up, w_down, cotangent)


def results_kernel(small, media, *refs):
    given, (media_grad, gains_grad, biases_grad), made, held, sem = refs[:7], refs[7:10], refs[10:17], refs[17:25], refs[25]
    moves = []
    for i in range(6):
        for k in range(2):
            moves.append((media.at[i, k], held[7].at[i, k], media_grad.at[pl.ds(COLS * i, COLS), pl.ds(COLS * k, COLS)]))
    moves += list(zip(given, held, made))
    loads = [pltpu.make_async_copy(a, b, sem.at[0, n]) for n, (a, b, _) in enumerate(moves)]
    stores = [pltpu.make_async_copy(b, c, sem.at[1, n]) for n, (_, b, c) in enumerate(moves)]
    for c in loads:
        c.start()
    columns = jnp.concatenate([small[...], jnp.zeros((112, 128), F32)], 0).T
    gains_grad[0] = columns[:3, :16]
    biases_grad[0] = columns[3:6, :16]
    for a, b in zip(loads, stores):
        a.wait()
        b.start()
    for c in stores:
        c.wait()


def results(media, small, *rest):
    vmem = pl.BlockSpec(memory_space=pltpu.VMEM)
    hbm = pl.BlockSpec(memory_space=pl.ANY)

    def sds(*shape):
        return jax.ShapeDtypeStruct(shape, F32)

    return pl.pallas_call(
        results_kernel,
        out_shape=[sds(1536, 512), sds(1, 3, 16), sds(1, 3, 16)] + [sds(*a.shape) for a in rest],
        in_specs=[vmem] + [hbm] * 8,
        out_specs=[hbm, vmem, vmem] + [hbm] * 7,
        scratch_shapes=[pltpu.VMEM(a.shape, F32) for a in rest + (media,)] + [pltpu.SemaphoreType.DMA((2, 19))],
        compiler_params=pltpu.CompilerParams(vmem_limit_bytes=VMEM_BYTES),
        name="results",
    )(small, media, *rest)


def body(
    latents_in, media, frame_count, gains, biases, w_query, w_keyval, w_out, w_up, w_down, cotangent
):
    frames = jnp.broadcast_to(64.0 * frame_count.astype(F32)[:, :1], (3, COLS)).reshape(1, 768)
    norms = jnp.concatenate([gains[0], biases[0], jnp.pad(frames, ((0, 1), (0, 256)))], 0)
    resampled, latents_grad, small, query, keyval, out, up, down, media_sum, _, _, _ = run_resampler(
        latents_in.reshape(192, 1024), media.reshape(1536, 1024), norms,
        w_query, w_keyval, w_out, w_up.reshape(4, 256, 4096), w_down.reshape(4096, 1024), cotangent.reshape(192, 1024),
    )
    media_grad, gains_grad, biases_grad, resampled, latents_grad, query, keyval, out, up, down = results(
        media_sum, small, resampled, latents_grad, query, keyval, out, up, down
    )
    return (
        resampled.reshape(3, 1, 64, 512),
        latents_grad.reshape(3, 1, 64, 512),
        media_grad.reshape(3, 1, 512, 512),
        gains_grad,
        biases_grad,
        query[None],
        keyval[None],
        out[None],
        up[None],
        down[None],
    )


def solution(mesh):
    placed = (
        P(None, "dp", None, None),
        P(None, "dp", None, None),
        P(None, "dp"),
        P("section", None, None),
        P("section", None, None),
        P("section", None, None),
        P("section", None, None),
        P("section", None, None),
        P("section", None, None),
        P("section", None, None),
        P(None, "dp", None, None),
    )
    return jax.shard_map(
        body,
        mesh=mesh,
        in_specs=placed,
        out_specs=(
            P(None, "dp", None, "section"),
            P(None, "dp", None, "section"),
            P(None, "dp", None, "section"),
            P("section", None, "dp"),
            P("section", None, "dp"),
            P("section", "dp", None),
            P("section", "dp", None),
            P("section", "dp", None),
            P("section", "dp", None),
            P("section", "dp", None),
        ),
        check_vma=False,
    )
```
